512 devices in a mesh: vocab: 64 (over z, x), pass: 8 (over y, core).
Axes of the slice: x: 4, y: 4, z: 16, core: 2. Of those that a mesh axis runs over, the one named last changes fastest.
Arguments:
- hidden: bfloat16 [768, 1024], P('pass'), as said below
- weight: bfloat16 [1024, 196608], P(None, ('vocab', 'pass')), may hold values from -0.1875 to 0.1875
- bias: float32 [196608], P(('vocab', 'pass')), may hold values from -6 to 6
- token_ids: int32 [24, 32], replicated, may hold values from 1 to 250001, as said below
- passages: bfloat16 [1024, 196608], P('pass', 'vocab'), as said below
- positive: int32 [24], replicated, may hold values from 0 to 1023
- selected: int32 [24, 196608], P(None, ('vocab', 'pass')), may hold values from 0 to 31, as said below
Outputs:
- mean_loss: float32 [], replicated
- grad_hidden: bfloat16 [768, 1024], P('vocab', 'pass')
- grad_weight: float32 [1024, 196608], P(None, ('vocab', 'pass'))
- grad_bias: float32 [196608], P(('vocab', 'pass'))
The draws below stay inside these ranges and needn't reach their ends.
Inputs may be any that keep to these rules, and one draw needn't show every extreme that they name: `token_ids`: each query has 8 to 32 real tokens, first, then padding id 1; other ids are at least 5. selected[q, v] names a real, not padding, position of query q. `passages`: entries lie within -0.03 to 0.03. `hidden`: entries lie within -6 to 6.
All inputs are finite; a program needn't handle non-finite values.
Results may differ from the reference program's by a relative error of at most 0.013.
Values may be sent and summed in bfloat16 or wider, within the bound.
A program may use at most 64 MiB of HBM per device.

```python
import jax
import jax.numpy as jnp
from jax import lax

D = 1024
VOC_DEV = 384
QUERIES = 24
QLEN = 32
TOKENS = 768
VOCAB = 196608
PASSAGES = 1024
N_VOCAB = 64
N_PASS = 8


def query_lengths(key):
    key = jax.random.fold_in(key, 101)
    lengths = jax.random.randint(key, (QUERIES,), QLEN // 4, QLEN + 1)
    lengths = lengths.at[0].set(QLEN)
    return lengths.at[QUERIES - 1].set(QLEN // 4)


def draw_token_ids(key, part):
    lengths = query_lengths(key)
    key = jax.random.fold_in(key, 3)
    word_ids = jax.random.randint(key, (QUERIES, QLEN), 5, 250002)
    word_ids = word_ids.at[0, 0].set(250001)
    places = jnp.arange(QLEN)[None, :]
    return jnp.where(places < lengths[:, None], word_ids, 1).astype(jnp.int32)


def draw_selected(key, part):
    lengths = query_lengths(key)
    key = jax.random.fold_in(key, 5)
    picked = jax.random.randint(key, (QUERIES, VOCAB), 0, lengths[:, None])
    picked = picked.at[0, 0].set(QLEN - 1).at[0, 1].set(0)
    return picked.astype(jnp.int32)


def draw_hidden(key, part):
    key = jax.random.fold_in(key, 7)
    values = jnp.clip(jax.random.normal(key, (TOKENS, D), jnp.float32), -6.0, 6.0)
    values = values.at[0, 0].set(6.0).at[TOKENS - 1, D - 1].set(-6.0)
    return values.astype(jnp.bfloat16)


def draw_passages(key, part):
    key = jax.random.fold_in(key, 11)
    values = jnp.clip(jax.random.normal(key, (PASSAGES, VOCAB), jnp.float32) * 0.005, -0.03, 0.03)
    values = values.at[PASSAGES - 1, 0].set(0.03).at[PASSAGES - 1, VOCAB - 1].set(-0.03)
    return values.astype(jnp.bfloat16)


def set_ends(drawn, stream_key, smallest, high):
    longest = drawn.shape.index(max(drawn.shape))
    spots = []
    for shift in (0, 1):
        where = [jax.random.randint(jax.random.fold_in(stream_key, axis), (), 0, length) for axis, length in enumerate(drawn.shape)]
        where[longest] = (where[longest] + shift) % drawn.shape[longest]
        spots.append(tuple(where))
    return drawn.at[spots[0]].set(smallest).at[spots[1]].set(high)


def block_levels(own_key, extent, cuts, low, high):
    def one(axis_at, shards_of):
        steps = jax.random.uniform(jax.random.fold_in(jax.random.fold_in(own_key, 6), axis_at), (shards_of,), jnp.float32, low / len(cuts), high / len(cuts))
        return jnp.repeat(jnp.exp(steps), extent[axis_at] // shards_of).reshape((-1,) + (1,) * (len(extent) - axis_at - 1))

    factor_of = one(*cuts[0])
    for cut in cuts[1:]:
        factor_of = factor_of * one(*cut)
    return factor_of


def scatter_about(stream_key, extent, deviation, bound, cuts=(), held_as=jnp.bfloat16):
    entries = jax.random.normal(stream_key, extent, jnp.float32) * deviation
    if len(cuts) > 0:
        entries = block_levels(stream_key, extent, cuts, -0.22, 0.18) * entries
    return jnp.clip(entries, min=-bound, max=bound).astype(held_as)


def setup_inputs(seed: int = 0) -> dict:
    arg_keys = jax.random.split(jax.random.key(seed), 8)
    hidden = draw_hidden(jax.random.fold_in(arg_keys[7], 71), 0)
    weight = scatter_about(arg_keys[1], (D, VOCAB), D ** -0.5, 0.1875, ((1, 512),))
    bias = scatter_about(arg_keys[2], (VOCAB,), 1.0, 6.0, ((0, 512),), jnp.float32)
    token_ids = draw_token_ids(jax.random.fold_in(arg_keys[7], 71), 0)
    passages = draw_passages(jax.random.fold_in(arg_keys[7], 71), 0)
    positive = set_ends(jax.random.randint(arg_keys[5], (QUERIES,), 0, PASSAGES), jax.random.fold_in(arg_keys[5], 1), 0, PASSAGES - 1).astype(jnp.int32)
    selected = draw_selected(jax.random.fold_in(arg_keys[7], 71), 0)
    return dict(hidden=hidden, weight=weight, bias=bias, token_ids=token_ids, passages=passages, positive=positive, selected=selected)


loss_scale = 4096.0


def reference(hidden, weight, bias, token_ids, passages, positive, selected):
    blocks = N_VOCAB
    width = VOC_DEV * N_PASS
    valid_mask = (token_ids != 1).astype(jnp.float32)
    weight_blocks = weight.reshape(D, blocks, width).transpose(1, 0, 2)
    bias_blocks = bias.reshape(blocks, width)

    def pool_block(block_pair):
        weight_block, bias_block = block_pair
        logits = jnp.dot(hidden, weight_block, preferred_element_type=jnp.float32) + bias_block[None, :]
        activation = jnp.log1p(jax.nn.softplus(logits)).reshape(QUERIES, QLEN, width) * valid_mask[:, :, None]
        return jnp.max(activation, axis=1).astype(jnp.bfloat16)

    pooled = lax.map(pool_block, (weight_blocks, bias_blocks))
    pooled = pooled.transpose(1, 0, 2).reshape(QUERIES, blocks * width)
    scores = lax.dot_general(pooled, passages, (((1,), (1,)), ((), ())), preferred_element_type=jnp.float32)
    peak_score = jnp.max(scores, axis=1)
    log_total = peak_score + jnp.log(jnp.sum(jnp.exp(scores - peak_score[:, None]), axis=1))
    onehot = (jnp.arange(PASSAGES, dtype=jnp.int32)[None, :] == positive[:, None]).astype(jnp.float32)
    pos_score = jnp.sum(scores * onehot, axis=1)
    mean_loss = jnp.mean(log_total - pos_score)
    softmax_probs = jnp.exp(scores - log_total[:, None])
    score_grad = ((softmax_probs - onehot) * (loss_scale / QUERIES)).astype(jnp.bfloat16)
    term_grad = jnp.dot(score_grad, passages, preferred_element_type=jnp.float32)
    term_blocks = term_grad.reshape(QUERIES, blocks, width).transpose(1, 0, 2)
    chosen_blocks = selected.reshape(QUERIES, blocks, width).transpose(1, 0, 2)
    positions = jnp.arange(QLEN, dtype=jnp.int32)

    def grad_block(carry, items):
        weight_block, bias_block, term_block, chosen_block = items
        logits = jnp.dot(hidden, weight_block, preferred_element_type=jnp.float32) + bias_block[None, :]
        slopes = (jax.nn.sigmoid(logits) / (1.0 + jax.nn.softplus(logits))).reshape(QUERIES, QLEN, width)
        chosen = positions[None, :, None] == chosen_block[:, None, :]
        logit_grad = jnp.where(chosen, slopes * term_block[:, None, :], jnp.zeros_like(slopes)).reshape(TOKENS, width)
        bias_grad = jnp.sum(logit_grad, axis=0)
        logit_half = logit_grad.astype(jnp.bfloat16)
        weight_grad = lax.dot_general(hidden, logit_half, (((0,), (0,)), ((), ())), preferred_element_type=jnp.float32)
        carry = carry + lax.dot_general(logit_half, weight_block, (((1,), (1,)), ((), ())), preferred_element_type=jnp.float32)
        return carry, (weight_grad, bias_grad)

    start_grad = jnp.zeros((TOKENS, D), jnp.float32)
    hidden_grad, (weight_grads, bias_grads) = lax.scan(grad_block, start_grad, (weight_blocks, bias_blocks, term_blocks, chosen_blocks))
    grad_weight = weight_grads.transpose(1, 0, 2).reshape(D, VOCAB)
    grad_bias = bias_grads.reshape(VOCAB)
    return mean_loss, hidden_grad.astype(jnp.bfloat16), grad_weight, grad_bias
```

```python
import functools

import jax
import jax.numpy as jnp
from jax import lax
from jax.experimental import pallas as pl
from jax.experimental.pallas import tpu as pltpu
from jax.sharding import PartitionSpec as P

loss_scale = 4096.0
NX = 4
NC = 2
PAD = 8
MESH = pl.DeviceIdType.MESH
f32 = jnp.float32
bf16 = jnp.bfloat16


def dot(a, b):
    return jnp.dot(a, b, preferred_element_type=f32)


def dot_nt(a, b):
    return lax.dot_general(a, b, (((1,), (1,)), ((), ())), preferred_element_type=f32)


def iota(shape, axis):
    return lax.broadcasted_iota(jnp.int32, shape, axis)


def kernel(nz, ny, n_queries, hidden, weight, bias, tokens, passages, positive, selected,
           loss_o, gh_o, gw_o, gb_o,
           gath, gath_t, w_v, ws_t, wo_t, pas, perm, maxl, sell, selp, lenp,
           pool, pos_s, pos_r, sc_s, sc_x, zs, zr, fin, st_s, st, u_s, u_r, slope,
           lh, lhp, cs_s, cs_r, own, s1y, s1y_r, s1x, s1x_r, s2x, s2x_r, s2y, s2y_r,
           zf, z2, z2_r, gw_v, send_sems, recv_sems, loc_sems):
    n_pass = ny * NC
    v = lax.axis_index("vocab")
    p = lax.axis_index("pass")
    z, x = lax.div(v, NX), lax.rem(v, NX)
    y, c = lax.div(p, NC), lax.rem(p, NC)
    sib = 1 - c
    voc = w_v.shape[1]
    group = n_queries // NX
    rows = NX * PAD
    hz = nz // 2
    tok = gath.shape[0] * gath.shape[1]
    half = tok // 2
    ro = tok // (nz * NX)
    part = hz * ro
    cols = ny * 128

    def around(value, shift, size):
        return lax.rem(value + (shift + size), size)

    def pass_dev(dy, dc):
        return (v, around(y, dy, ny) * NC + around(c, dc, NC))

    def x_dev(dx):
        return (z * NX + around(x, dx, NX), p)

    def z_dev(dz):
        return (around(z, dz, nz) * NX + x, p)

    pass_peers = [(dy, dc) for dy in range(ny) for dc in range(NC) if dy or dc]
    started = []

    def remote(src, dst, device):
        i = len(started)
        copy = pltpu.make_async_remote_copy(
            src_ref=src, dst_ref=dst, send_sem=send_sems.at[i], recv_sem=recv_sems.at[i],
            device_id=device, device_id_type=MESH,
        )
        copy.start()
        started.append(copy)
        return copy

    local = [pltpu.make_async_copy(hidden, gath.at[p], loc_sems.at[0]),
             pltpu.make_async_copy(weight, w_v, loc_sems.at[1])]
    for j in range(n_pass):
        local.append(pltpu.make_async_copy(
            passages.at[:, pl.ds(j * voc, voc)], pas.at[j], loc_sems.at[2 + j]))
    for copy in local:
        copy.start()

    barrier = pltpu.get_barrier_semaphore()
    peers = ([pass_dev(dy, dc) for dy, dc in pass_peers] + [x_dev(d) for d in range(1, NX)]
             + [z_dev(d) for d in range(1, nz)])
    for device in peers:
        pl.semaphore_signal(barrier, inc=1, device_id=device, device_id_type=MESH)
    pl.semaphore_wait(barrier, len(peers))

    to_y = {}
    for dy in sorted(range(1, ny), key=lambda d: -min(d, ny - d)):
        to_y[dy] = remote(hidden, gath.at[p], pass_dev(dy, 0))
    to_sib = {0: remote(hidden, gath.at[p], pass_dev(0, 1))}

    maxl[...] = jnp.zeros_like(maxl)
    sell[...] = jnp.zeros_like(sell)
    selp[...] = jnp.zeros_like(selp)
    lenp[...] = jnp.zeros_like(lenp)
    zf[...] = jnp.zeros_like(zf)
    lengths = jnp.sum((tokens[...] != 1).astype(f32), axis=1, keepdims=True)
    lengths = jnp.broadcast_to(lengths, (n_queries, voc))
    for g in range(NX):
        selp[g, 0:group, :] = selected[g * group:(g + 1) * group, :]
        lenp[g, 0:group, :] = lengths[g * group:(g + 1) * group, :].astype(jnp.int32)

    def block(yy):
        first = yy * NC
        got = gath[pl.ds(first, NC)].reshape(NC * gath.shape[1], gath.shape[2])
        logits = dot(got, w_v[...])
        qlen = logits.shape[0] // group
        logits = logits.reshape(group, qlen, voc)
        at = iota((group, qlen, voc), 1)
        valid = at < lenp[yy][0:group].reshape(group, 1, voc)
        chosen = at == selp[yy][0:group].reshape(group, 1, voc)
        maxl[yy, 0:group, :] = jnp.max(jnp.where(valid, logits, -jnp.inf), axis=1)
        sell[yy, 0:group, :] = jnp.sum(jnp.where(chosen, logits, 0.0), axis=1)

    def arrive(dy):
        to_y[dy].wait_recv()
        at = around(y, -dy, ny) * NC + c
        to_sib[dy] = remote(gath.at[at], gath.at[at], pass_dev(0, 1))

    local[0].wait()
    local[1].wait()
    to_sib[0].wait_recv()
    block(y)
    order = sorted(range(1, ny), key=lambda d: min(d, ny - d))
    for i, dy in enumerate(order):
        if i == 0:
            arrive(dy)
        if i + 1 < len(order):
            arrive(order[i + 1])
        to_sib[dy].wait_recv()
        block(around(y, -dy, ny))

    most = maxl[...] + bias[...].reshape(1, 1, voc)
    pool[p] = jnp.log1p(jax.nn.softplus(most)).reshape(rows, voc).astype(bf16)
    far_first = sorted(pass_peers, key=lambda d: -min(d[0], ny - d[0]))
    to_pool = {d: remote(pool.at[p], pool.at[p], pass_dev(*d)) for d in far_first}

    for copy in local[2:]:
        copy.wait()
    row, lane = iota((rows, 128), 0), iota((rows, 128), 1)
    in_group = lax.bitwise_and(row, PAD - 1)
    query = lax.shift_right_logical(row, 3) * group + in_group
    listed = jnp.broadcast_to(positive[...], (rows, positive.shape[1])).astype(f32)
    picked = jnp.where((query == lane) & (in_group < group), listed, 0.0)
    pos_col = jnp.sum(picked, axis=1, keepdims=True).astype(jnp.int32)
    is_pos = (lane + p * 128) == pos_col
    onehot = is_pos.astype(f32).astype(bf16)
    for j in range(n_pass):
        pos_s[j] = dot(onehot, pas[j]).astype(bf16)
    to_pos = {}
    for dy, dc in far_first:
        there = around(y, dy, ny) * NC + around(c, dc, NC)
        to_pos[dy, dc] = remote(pos_s.at[there], pos_r.at[dy * NC + dc], pass_dev(dy, dc))

    score = dot_nt(pool[p], pas[p])
    for dy, dc in reversed(far_first):
        to_pool[dy, dc].wait_recv()
        there = around(y, -dy, ny) * NC + around(c, -dc, NC)
        score = score + dot_nt(pool[there], pas[there])
    sc_s[...] = score.reshape(NX, PAD, 128)

    to_x = [remote(sc_s.at[around(x, d, NX)], sc_x.at[d], x_dev(d)) for d in range(1, NX)]
    for yy in range(ny):
        at = pl.multiple_of(yy * 256 + sib * 128, 128)
        ws_t[:, yy * 128:(yy + 1) * 128] = w_v[pl.ds(at, 128), :].T
        at = pl.multiple_of(yy * 256 + c * 128, 128)
        wo_t[:, yy * 128:(yy + 1) * 128] = w_v[pl.ds(at, 128), :].T
    mine = sc_s[x]
    for copy in to_x:
        copy.wait_recv()
    for d in range(1, NX):
        mine = mine + sc_x[d]
    zs[...] = mine
    to_z = [remote(zs, zr.at[d], z_dev(d)) for d in sorted(range(1, nz), key=lambda d: -min(d, nz - d))]
    gath_t[...] = gath[...].reshape(tok, gath.shape[2]).T
    prow = iota((tok, 128), 0)
    chunk = jnp.floor((prow.astype(f32) + 0.5) * (1.0 / ro)).astype(jnp.int32)
    zl = lax.bitwise_and(chunk, hz - 1)
    xx = lax.bitwise_and(lax.shift_right_logical(chunk, hz.bit_length() - 1), NX - 1)
    hh = lax.shift_right_logical(chunk, (hz * NX).bit_length() - 1)
    natural = prow + ro * ((hh * hz + zl) * NX + xx - chunk)
    plane = iota((tok, 128), 1)
    for j in range(tok // 128):
        perm[:, j * 128:(j + 1) * 128] = (natural == plane + j * 128).astype(f32).astype(bf16)
    at_sel = sell[...] + bias[...].reshape(1, 1, voc)
    slope[...] = (jax.nn.sigmoid(at_sel) / (1.0 + jax.nn.softplus(at_sel))).reshape(rows, voc)
    for copy in to_z:
        copy.wait_recv()
    for d in range(1, nz):
        mine = mine + zr[d]
    fin[x] = mine
    to_fin = [remote(fin.at[x], fin.at[x], x_dev(d)) for d in range(1, NX)]
    for copy in to_pos.values():
        copy.wait_recv()
    pos_entries = pos_s[p].astype(f32)
    for dy, dc in pass_peers:
        pos_entries = pos_entries + pos_r[dy * NC + dc].astype(f32)
    for copy in to_fin:
        copy.wait_recv()

    score = fin[...].reshape(rows, 128)
    peak = jnp.max(score, axis=1, keepdims=True)
    terms = jnp.exp(score - peak)
    other = jnp.where(is_pos, 0.0, terms)
    stats = [peak, jnp.sum(other, axis=1, keepdims=True),
             jnp.sum(jnp.where(is_pos, terms, 0.0), axis=1, keepdims=True),
             jnp.sum(jnp.where(is_pos, score, 0.0), axis=1, keepdims=True)]
    eye = row == lane
    turned = [jnp.sum(jnp.where(eye, s, 0.0), axis=0, keepdims=True) for s in stats]
    st_s[...] = jnp.concatenate(turned + [jnp.zeros((8 - len(turned), 128), f32)], axis=0)
    to_st = {d: remote(st_s, st.at[d[0] * NC + d[1]], pass_dev(*d)) for d in far_first}
    other = other.astype(bf16)
    to_u = {}
    for dy, dc in far_first:
        there = around(y, dy, ny) * NC + around(c, dc, NC)
        u_s[there] = dot(other, pas[there]).astype(bf16)
        to_u[dy, dc] = remote(u_s.at[there], u_r.at[dy * NC + dc], pass_dev(dy, dc))
    st[0] = st_s[...]
    mine_u = dot(other, pas[p])
    for copy in to_st.values():
        copy.wait_recv()
    peaks = [st[i][0:1] for i in range(n_pass)]
    top = functools.reduce(jnp.maximum, peaks)
    scale = [jnp.exp(k - top) for k in peaks]
    rest = sum(scale[i] * st[i][1:2] for i in range(n_pass))
    total = rest + sum(scale[i] * st[i][2:3] for i in range(n_pass))
    pos_score = sum(st[i][3:4] for i in range(n_pass))
    log_total = top + jnp.log(total)
    lane1 = iota((1, 128), 1)
    counted = (lax.bitwise_and(lane1, PAD - 1) < group) & (lane1 < rows)
    loss_o[...] = jnp.sum(jnp.where(counted, log_total - pos_score, 0.0), axis=1, keepdims=True) * (1.0 / n_queries)
    factor = (loss_scale / n_queries) / total

    def column(line):
        return jnp.sum(jnp.where(eye, line, 0.0), axis=1, keepdims=True)

    term = column(scale[0] * factor) * mine_u - column(rest * factor) * pos_entries
    for dy, dc in reversed(far_first):
        i = dy * NC + dc
        to_u[dy, dc].wait_recv()
        term = term + column(scale[i] * factor) * u_r[i].astype(f32)

    grad = term * slope[...]
    real = lax.bitwise_and(iota((rows, voc), 0), PAD - 1) < group
    gb_o[...] = jnp.sum(jnp.where(real, grad, 0.0), axis=0, keepdims=True)
    grad = grad.reshape(NX, PAD, voc)
    qlen = tok // n_queries
    at = iota((group, qlen, voc), 1)
    for g in range(NX):
        chosen = at == selp[g][0:group].reshape(group, 1, voc)
        some = jnp.where(chosen, grad[g][0:group].reshape(group, 1, voc), 0.0)
        lh[g * group * qlen:(g + 1) * group * qlen, :] = some.reshape(group * qlen, voc).astype(bf16)

    for h in range(2):
        lhp[h] = dot(perm[h * half:(h + 1) * half, :], lh[...]).astype(bf16)
    to_core = []
    for h in range(2):
        cs_s[h] = dot(lhp[h], ws_t[...]).astype(bf16)
        to_core.append(remote(cs_s.at[h], cs_r.at[h], pass_dev(0, 1)))
    for h in range(2):
        own[h] = dot(lhp[h], wo_t[...])
    to_core[0].wait_recv()
    both = own[0] + cs_r[0].astype(f32)
    for yy in range(ny):
        s1y[yy] = both[:, yy * 128:(yy + 1) * 128].astype(bf16)
    to_s1y = [remote(s1y.at[around(y, d, ny)], s1y_r.at[d], pass_dev(d, 0))
              for d in sorted(range(1, ny), key=lambda d: -min(d, ny - d))]
    to_core[1].wait_recv()
    both = own[1] + cs_r[1].astype(f32)
    for xx in range(NX):
        s1x[xx] = both[xx * part:(xx + 1) * part].astype(bf16)
    to_s1x = [remote(s1x.at[around(x, d, NX)], s1x_r.at[d], x_dev(d))
              for d in sorted(range(1, NX), key=lambda d: -min(d, NX - d))]

    gw_v[...] = dot(gath_t[...], lh[...])
    gw_out = pltpu.make_async_copy(gw_v, gw_o, loc_sems.at[0])
    gw_out.start()

    for copy in to_s1y:
        copy.wait_recv()
    both = s1y[y].astype(f32)
    for d in range(1, ny):
        both = both + s1y_r[d].astype(f32)
    s2x[...] = both.astype(bf16).reshape(NX, part, 128)
    to_s2x = [remote(s2x.at[around(x, d, NX)], s2x_r.at[d], x_dev(d)) for d in range(1, NX)]
    for copy in to_s1x:
        copy.wait_recv()
    both = s1x[x].astype(f32)
    for d in range(1, NX):
        both = both + s1x_r[d].astype(f32)
    for yy in range(ny):
        s2y[yy] = both[:, yy * 128:(yy + 1) * 128].astype(bf16)
    to_s2y = [remote(s2y.at[around(y, d, ny)], s2y_r.at[d], pass_dev(d, 0)) for d in range(1, ny)]
    for copy in to_s2x:
        copy.wait_recv()
    low = s2x[x].astype(f32)
    for d in range(1, NX):
        low = low + s2x_r[d].astype(f32)
    for k in range(hz):
        zf[k, 0:ro, :] = low[k * ro:(k + 1) * ro]
    for copy in to_s2y:
        copy.wait_recv()
    high = s2y[y].astype(f32)
    for d in range(1, ny):
        high = high + s2y_r[d].astype(f32)
    for k in range(hz):
        zf[hz + k, 0:ro, :] = high[k * ro:(k + 1) * ro]
    z2[...] = zf[...].astype(bf16)
    to_z2 = [remote(z2.at[around(z, d, nz)], z2_r.at[d], z_dev(d))
             for d in sorted(range(1, nz), key=lambda d: -min(d, nz - d))]
    total = zf[z]
    for copy in to_z2:
        copy.wait_recv()
    for d in range(1, nz):
        total = total + z2_r[d].astype(f32)
    gh_o[...] = total[0:ro].astype(bf16)

    for copy in started:
        copy.wait_send()
    gw_out.wait()


def local(nz, ny, hidden, weight, bias, token_ids, passages, positive, selected):
    n_queries, qlen = token_ids.shape
    own_rows, d = hidden.shape
    voc = weight.shape[1]
    n_pass = ny * NC
    tok = n_queries * qlen
    rows = NX * PAD
    hz = nz // 2
    ro = tok // (nz * NX)
    rp = -(-ro // 16) * 16
    part = hz * ro
    cols = ny * 128
    half = tok // 2
    n_copies = (2 * ny - 1) + 4 * (n_pass - 1) + 2 * (NX - 1) + 2 * (nz - 1) + 2 + 2 * (NX - 1) + 2 * (ny - 1)
    vmem = pl.BlockSpec(memory_space=pltpu.VMEM)
    anywhere = pl.BlockSpec(memory_space=pl.ANY)
    scratch = [
        ((n_pass, own_rows, d), bf16), ((d, tok), bf16), ((d, voc), bf16),
        ((voc, cols), bf16), ((voc, cols), bf16), ((n_pass, 128, voc), bf16), ((tok, tok), bf16),
        ((NX, PAD, voc), f32), ((NX, PAD, voc), f32), ((NX, PAD, voc), jnp.int32), ((NX, PAD, voc), jnp.int32),
        ((n_pass, rows, voc), bf16), ((n_pass, rows, voc), bf16), ((n_pass, rows, voc), bf16),
        ((NX, PAD, 128), f32), ((NX, PAD, 128), f32), ((PAD, 128), f32), ((nz, PAD, 128), f32),
        ((NX, PAD, 128), f32), ((8, 128), f32), ((n_pass, 8, 128), f32),
        ((n_pass, rows, voc), bf16), ((n_pass, rows, voc), bf16), ((rows, voc), f32),
        ((tok, voc), bf16), ((2, half, voc), bf16), ((2, half, cols), bf16), ((2, half, cols), bf16),
        ((2, half, cols), f32), ((ny, half, 128), bf16), ((ny, half, 128), bf16),
        ((NX, part, cols), bf16), ((NX, part, cols), bf16), ((NX, part, 128), bf16), ((NX, part, 128), bf16),
        ((ny, part, 128), bf16), ((ny, part, 128), bf16),
        ((nz, rp, 128), f32), ((nz, rp, 128), bf16), ((nz, rp, 128), bf16), ((d, voc), f32),
    ]
    loss, grad_hidden, grad_weight, grad_bias = pl.pallas_call(
        functools.partial(kernel, nz, ny, n_queries),
        out_shape=(
            jax.ShapeDtypeStruct((1, 1), f32),
            jax.ShapeDtypeStruct((ro, 128), bf16),
            jax.ShapeDtypeStruct((d, voc), f32),
            jax.ShapeDtypeStruct((1, voc), f32),
        ),
        in_specs=[anywhere, anywhere, vmem, vmem, anywhere, vmem, vmem],
        out_specs=(vmem, vmem, anywhere, vmem),
        scratch_shapes=[pltpu.VMEM(s, t) for s, t in scratch] + [
            pltpu.SemaphoreType.DMA((n_copies,)),
            pltpu.SemaphoreType.DMA((n_copies,)),
            pltpu.SemaphoreType.DMA((2 + n_pass,)),
        ],
        compiler_params=pltpu.CompilerParams(
            collective_id=0, has_side_effects=True, vmem_limit_bytes=48 * 1024 * 1024
        ),
    )(hidden, weight, bias.reshape(1, voc), token_ids, passages,
      jnp.pad(positive, (0, 128 - n_queries)).reshape(1, 128), selected)
    return loss.reshape(()), grad_hidden, grad_weight, grad_bias.reshape(voc)


def solution(mesh):
    in_specs = (
        P("pass", None),
        P(None, ("vocab", "pass")),
        P(("vocab", "pass")),
        P(),
        P("pass", "vocab"),
        P(),
        P(None, ("vocab", "pass")),
    )
    out_specs = (P(), P("vocab", "pass"), P(None, ("vocab", "pass")), P(("vocab", "pass")))
    body = functools.partial(local, mesh.shape["vocab"] // NX, mesh.shape["pass"] // NC)
    return jax.shard_map(body, mesh=mesh, in_specs=in_specs, out_specs=out_specs, check_vma=False)
```

```python
import functools

import jax
import jax.numpy as jnp
from jax import lax
from jax.experimental import pallas as pl
from jax.experimental.pallas import tpu as pltpu
from jax.sharding import PartitionSpec as P

loss_scale = 4096.0
NX = 4
NC = 2
PAD = 8
MESH = pl.DeviceIdType.MESH
f32 = jnp.float32
bf16 = jnp.bfloat16


def dot(a, b):
    return jnp.dot(a, b, preferred_element_type=f32)


def dot_nt(a, b):
    return lax.dot_general(a, b, (((1,), (1,)), ((), ())), preferred_element_type=f32)


def iota(shape, axis):
    return lax.broadcasted_iota(jnp.int32, shape, axis)


def kernel(nz, ny, n_queries, hidden, weight, bias, tokens, passages, positive, selected,
           loss_o, gh_o, gw_o, gb_o,
           gath, gath_t, w_v, ws_t, wo_t, pas, perm, maxl, sell, selp, lenp,
           pool, pos_s, pos_r, sc_s, sc_x, zs, zr, fin, st_s, st, u_s, u_r, slope,
           lh, lhp, cs_s, cs_r, own, s1y, s1y_r, s1x, s1x_r, s2x, s2x_r, s2y, s2y_r,
           zf, z2, z2_r, gw_v, bias_v, tokens_v, selected_v, send_sems, recv_sems, loc_sems):
    n_pass = ny * NC
    v = lax.axis_index("vocab")
    p = lax.axis_index("pass")
    z, x = lax.div(v, NX), lax.rem(v, NX)
    y, c = lax.div(p, NC), lax.rem(p, NC)
    sib = 1 - c
    voc = w_v.shape[1]
    group = n_queries // NX
    rows = NX * PAD
    hz = nz // 2
    tok = gath.shape[0] * gath.shape[1]
    half = tok // 2
    ro = tok // (nz * NX)
    part = hz * ro
    cols = ny * 128

    def around(value, shift, size):
        return lax.rem(value + (shift + size), size)

    def pass_dev(dy, dc):
        return (v, around(y, dy, ny) * NC + around(c, dc, NC))

    def x_dev(dx):
        return (z * NX + around(x, dx, NX), p)

    def z_dev(dz):
        return (around(z, dz, nz) * NX + x, p)

    pass_peers = [(dy, dc) for dy in range(ny) for dc in range(NC) if dy or dc]
    started = []

    def remote(src, dst, device):
        i = len(started)
        copy = pltpu.make_async_remote_copy(
            src_ref=src, dst_ref=dst, send_sem=send_sems.at[i], recv_sem=recv_sems.at[i],
            device_id=device, device_id_type=MESH,
        )
        copy.start()
        started.append(copy)
        return copy

    local = [pltpu.make_async_copy(hidden, gath.at[p], loc_sems.at[0]),
             pltpu.make_async_copy(weight, w_v, loc_sems.at[1]),
             pltpu.make_async_copy(tokens, tokens_v, loc_sems.at[2]),
             pltpu.make_async_copy(selected, selected_v, loc_sems.at[3]),
             pltpu.make_async_copy(bias, bias_v, loc_sems.at[4])]
    for j in range(n_pass):
        local.append(pltpu.make_async_copy(
            passages.at[:, pl.ds(j * voc, voc)], pas.at[j], loc_sems.at[5 + j]))
    for copy in local:
        copy.start()

    barrier = pltpu.get_barrier_semaphore()
    peers = ([pass_dev(dy, dc) for dy, dc in pass_peers] + [x_dev(d) for d in range(1, NX)]
             + [z_dev(d) for d in range(1, nz)])
    for device in peers:
        pl.semaphore_signal(barrier, inc=1, device_id=device, device_id_type=MESH)
    pl.semaphore_wait(barrier, len(peers))

    to_y = {}
    for dy in sorted(range(1, ny), key=lambda d: -min(d, ny - d)):
        to_y[dy] = remote(hidden, gath.at[p], pass_dev(dy, 0))
    to_sib = {0: remote(hidden, gath.at[p], pass_dev(0, 1))}

    maxl[...] = jnp.zeros_like(maxl)
    sell[...] = jnp.zeros_like(sell)
    selp[...] = jnp.zeros_like(selp)
    lenp[...] = jnp.zeros_like(lenp)
    zf[...] = jnp.zeros_like(zf)
    for copy in local[2:5]:
        copy.wait()
    lengths = jnp.sum((tokens_v[...] != 1).astype(f32), axis=1, keepdims=True)
    lengths = jnp.broadcast_to(lengths, (n_queries, voc))
    for g in range(NX):
        selp[g, 0:group, :] = selected_v[g * group:(g + 1) * group, :]
        lenp[g, 0:group, :] = lengths[g * group:(g + 1) * group, :].astype(jnp.int32)

    def block(yy):
        first = yy * NC
        got = gath[pl.ds(first, NC)].reshape(NC * gath.shape[1], gath.shape[2])
        logits = dot(got, w_v[...])
        qlen = logits.shape[0] // group
        logits = logits.reshape(group, qlen, voc)
        at = iota((group, qlen, voc), 1)
        valid = at < lenp[yy][0:group].reshape(group, 1, voc)
        chosen = at == selp[yy][0:group].reshape(group, 1, voc)
        maxl[yy, 0:group, :] = jnp.max(jnp.where(valid, logits, -jnp.inf), axis=1)
        sell[yy, 0:group, :] = jnp.sum(jnp.where(chosen, logits, 0.0), axis=1)

    def arrive(dy):
        to_y[dy].wait_recv()
        at = around(y, -dy, ny) * NC + c
        to_sib[dy] = remote(gath.at[at], gath.at[at], pass_dev(0, 1))

    local[0].wait()
    local[1].wait()
    to_sib[0].wait_recv()
    block(y)
    order = sorted(range(1, ny), key=lambda d: min(d, ny - d))
    for i, dy in enumerate(order):
        if i == 0:
            arrive(dy)
        if i + 1 < len(order):
            arrive(order[i + 1])
        to_sib[dy].wait_recv()
        block(around(y, -dy, ny))

    most = maxl[...] + bias_v[...].reshape(1, 1, voc)
    pool[p] = jnp.log1p(jax.nn.softplus(most)).reshape(rows, voc).astype(bf16)
    far_first = sorted(pass_peers, key=lambda d: -min(d[0], ny - d[0]))
    to_pool = {d: remote(pool.at[p], pool.at[p], pass_dev(*d)) for d in far_first}

    for copy in local[5:]:
        copy.wait()
    row, lane = iota((rows, 128), 0), iota((rows, 128), 1)
    in_group = lax.bitwise_and(row, PAD - 1)
    query = lax.shift_right_logical(row, 3) * group + in_group
    query = jnp.where(in_group < group, query, -1)
    pos_col = jnp.zeros((rows, 128), jnp.int32)
    for q in range(n_queries):
        pos_col = jnp.where(query == q, positive[q], pos_col)
    is_pos = (lane + p * 128) == pos_col
    onehot = is_pos.astype(f32).astype(bf16)
    for j in range(n_pass):
        pos_s[j] = dot(onehot, pas[j]).astype(bf16)
    to_pos = {}
    for dy, dc in far_first:
        there = around(y, dy, ny) * NC + around(c, dc, NC)
        to_pos[dy, dc] = remote(pos_s.at[there], pos_r.at[dy * NC + dc], pass_dev(dy, dc))

    score = dot_nt(pool[p], pas[p])
    for dy, dc in reversed(far_first):
        to_pool[dy, dc].wait_recv()
        there = around(y, -dy, ny) * NC + around(c, -dc, NC)
        score = score + dot_nt(pool[there], pas[there])
    sc_s[...] = score.reshape(NX, PAD, 128)

    to_x = [remote(sc_s.at[around(x, d, NX)], sc_x.at[d], x_dev(d)) for d in range(1, NX)]
    for yy in range(ny):
        at = pl.multiple_of(yy * 256 + sib * 128, 128)
        ws_t[:, yy * 128:(yy + 1) * 128] = w_v[pl.ds(at, 128), :].T
        at = pl.multiple_of(yy * 256 + c * 128, 128)
        wo_t[:, yy * 128:(yy + 1) * 128] = w_v[pl.ds(at, 128), :].T
    mine = sc_s[x]
    for copy in to_x:
        copy.wait_recv()
    for d in range(1, NX):
        mine = mine + sc_x[d]
    zs[...] = mine
    to_z = [remote(zs, zr.at[d], z_dev(d)) for d in sorted(range(1, nz), key=lambda d: -min(d, nz - d))]
    gath_t[...] = gath[...].reshape(tok, gath.shape[2]).T
    prow = iota((tok, 128), 0)
    chunk = jnp.floor((prow.astype(f32) + 0.5) * (1.0 / ro)).astype(jnp.int32)
    zl = lax.bitwise_and(chunk, hz - 1)
    xx = lax.bitwise_and(lax.shift_right_logical(chunk, hz.bit_length() - 1), NX - 1)
    hh = lax.shift_right_logical(chunk, (hz * NX).bit_length() - 1)
    natural = prow + ro * ((hh * hz + zl) * NX + xx - chunk)
    plane = iota((tok, 128), 1)
    for j in range(tok // 128):
        perm[:, j * 128:(j + 1) * 128] = (natural == plane + j * 128).astype(f32).astype(bf16)
    at_sel = sell[...] + bias_v[...].reshape(1, 1, voc)
    slope[...] = (jax.nn.sigmoid(at_sel) / (1.0 + jax.nn.softplus(at_sel))).reshape(rows, voc)
    for copy in to_z:
        copy.wait_recv()
    for d in range(1, nz):
        mine = mine + zr[d]
    fin[x] = mine
    to_fin = [remote(fin.at[x], fin.at[x], x_dev(d)) for d in range(1, NX)]
    for copy in to_pos.values():
        copy.wait_recv()
    pos_entries = pos_s[p].astype(f32)
    for dy, dc in pass_peers:
        pos_entries = pos_entries + pos_r[dy * NC + dc].astype(f32)
    for copy in to_fin:
        copy.wait_recv()

    score = fin[...].reshape(rows, 128)
    peak = jnp.max(score, axis=1, keepdims=True)
    terms = jnp.exp(score - peak)
    other = jnp.where(is_pos, 0.0, terms)
    stats = [peak, jnp.sum(other, axis=1, keepdims=True),
             jnp.sum(jnp.where(is_pos, terms, 0.0), axis=1, keepdims=True),
             jnp.sum(jnp.where(is_pos, score, 0.0), axis=1, keepdims=True)]
    eye = row == lane
    turned = [jnp.sum(jnp.where(eye, s, 0.0), axis=0, keepdims=True) for s in stats]
    st_s[...] = jnp.concatenate(turned + [jnp.zeros((8 - len(turned), 128), f32)], axis=0)
    to_st = {d: remote(st_s, st.at[d[0] * NC + d[1]], pass_dev(*d)) for d in far_first}
    other = other.astype(bf16)
    to_u = {}
    for dy, dc in far_first:
        there = around(y, dy, ny) * NC + around(c, dc, NC)
        u_s[there] = dot(other, pas[there]).astype(bf16)
        to_u[dy, dc] = remote(u_s.at[there], u_r.at[dy * NC + dc], pass_dev(dy, dc))
    st[0] = st_s[...]
    mine_u = dot(other, pas[p])
    for copy in to_st.values():
        copy.wait_recv()
    peaks = [st[i][0:1] for i in range(n_pass)]
    top = functools.reduce(jnp.maximum, peaks)
    scale = [jnp.exp(k - top) for k in peaks]
    rest = sum(scale[i] * st[i][1:2] for i in range(n_pass))
    total = rest + sum(scale[i] * st[i][2:3] for i in range(n_pass))
    pos_score = sum(st[i][3:4] for i in range(n_pass))
    log_total = top + jnp.log(total)
    lane1 = iota((1, 128), 1)
    counted = (lax.bitwise_and(lane1, PAD - 1) < group) & (lane1 < rows)
    loss_o[...] = jnp.sum(jnp.where(counted, log_total - pos_score, 0.0), axis=1, keepdims=True) * (1.0 / n_queries)
    factor = (loss_scale / n_queries) / total

    def column(line):
        return jnp.sum(jnp.where(eye, line, 0.0), axis=1, keepdims=True)

    term = column(scale[0] * factor) * mine_u - column(rest * factor) * pos_entries
    for dy, dc in reversed(far_first):
        i = dy * NC + dc
        to_u[dy, dc].wait_recv()
        term = term + column(scale[i] * factor) * u_r[i].astype(f32)

    grad = term * slope[...]
    real = lax.bitwise_and(iota((rows, voc), 0), PAD - 1) < group
    gb_o[...] = jnp.sum(jnp.where(real, grad, 0.0), axis=0)
    grad = grad.reshape(NX, PAD, voc)
    qlen = tok // n_queries
    at = iota((group, qlen, voc), 1)
    for g in range(NX):
        chosen = at == selp[g][0:group].reshape(group, 1, voc)
        some = jnp.where(chosen, grad[g][0:group].reshape(group, 1, voc), 0.0)
        lh[g * group * qlen:(g + 1) * group * qlen, :] = some.reshape(group * qlen, voc).astype(bf16)

    for h in range(2):
        lhp[h] = dot(perm[h * half:(h + 1) * half, :], lh[...]).astype(bf16)
    to_core = []
    for h in range(2):
        cs_s[h] = dot(lhp[h], ws_t[...]).astype(bf16)
        to_core.append(remote(cs_s.at[h], cs_r.at[h], pass_dev(0, 1)))
    for h in range(2):
        own[h] = dot(lhp[h], wo_t[...])
    to_core[0].wait_recv()
    both = own[0] + cs_r[0].astype(f32)
    for yy in range(ny):
        s1y[yy] = both[:, yy * 128:(yy + 1) * 128].astype(bf16)
    to_s1y = [remote(s1y.at[around(y, d, ny)], s1y_r.at[d], pass_dev(d, 0))
              for d in sorted(range(1, ny), key=lambda d: -min(d, ny - d))]
    to_core[1].wait_recv()
    both = own[1] + cs_r[1].astype(f32)
    for xx in range(NX):
        s1x[xx] = both[xx * part:(xx + 1) * part].astype(bf16)
    to_s1x = [remote(s1x.at[around(x, d, NX)], s1x_r.at[d], x_dev(d))
              for d in sorted(range(1, NX), key=lambda d: -min(d, NX - d))]

    gw_v[...] = dot(gath_t[...], lh[...])
    gw_out = pltpu.make_async_copy(gw_v, gw_o, loc_sems.at[0])
    gw_out.start()

    for copy in to_s1y:
        copy.wait_recv()
    both = s1y[y].astype(f32)
    for d in range(1, ny):
        both = both + s1y_r[d].astype(f32)
    s2x[...] = both.astype(bf16).reshape(NX, part, 128)
    to_s2x = [remote(s2x.at[around(x, d, NX)], s2x_r.at[d], x_dev(d)) for d in range(1, NX)]
    for copy in to_s1x:
        copy.wait_recv()
    both = s1x[x].astype(f32)
    for d in range(1, NX):
        both = both + s1x_r[d].astype(f32)
    for yy in range(ny):
        s2y[yy] = both[:, yy * 128:(yy + 1) * 128].astype(bf16)
    to_s2y = [remote(s2y.at[around(y, d, ny)], s2y_r.at[d], pass_dev(d, 0)) for d in range(1, ny)]
    for copy in to_s2x:
        copy.wait_recv()
    low = s2x[x].astype(f32)
    for d in range(1, NX):
        low = low + s2x_r[d].astype(f32)
    for k in range(hz):
        zf[k, 0:ro, :] = low[k * ro:(k + 1) * ro]
    for copy in to_s2y:
        copy.wait_recv()
    high = s2y[y].astype(f32)
    for d in range(1, ny):
        high = high + s2y_r[d].astype(f32)
    for k in range(hz):
        zf[hz + k, 0:ro, :] = high[k * ro:(k + 1) * ro]
    z2[...] = zf[...].astype(bf16)
    to_z2 = [remote(z2.at[around(z, d, nz)], z2_r.at[d], z_dev(d))
             for d in sorted(range(1, nz), key=lambda d: -min(d, nz - d))]
    total = zf[z]
    for copy in to_z2:
        copy.wait_recv()
    for d in range(1, nz):
        total = total + z2_r[d].astype(f32)
    gh_o[...] = total[0:ro].astype(bf16)

    for copy in started:
        copy.wait_send()
    gw_out.wait()


def hand_out(*refs):
    sems = refs[8]
    copies = [pltpu.make_async_copy(refs[i], refs[4 + i], sems.at[i]) for i in range(4)]
    for copy in copies:
        copy.start()
    for copy in copies:
        copy.wait()


def local(nz, ny, hidden, weight, bias, token_ids, passages, positive, selected):
    n_queries, qlen = token_ids.shape
    own_rows, d = hidden.shape
    voc = weight.shape[1]
    n_pass = ny * NC
    tok = n_queries * qlen
    rows = NX * PAD
    hz = nz // 2
    ro = tok // (nz * NX)
    rp = -(-ro // 16) * 16
    part = hz * ro
    cols = ny * 128
    half = tok // 2
    n_copies = (2 * ny - 1) + 4 * (n_pass - 1) + 2 * (NX - 1) + 2 * (nz - 1) + 2 + 2 * (NX - 1) + 2 * (ny - 1)
    vmem = pl.BlockSpec(memory_space=pltpu.VMEM)
    anywhere = pl.BlockSpec(memory_space=pl.ANY)
    hbm = pl.BlockSpec(memory_space=pltpu.HBM)
    scratch = [
        ((n_pass, own_rows, d), bf16), ((d, tok), bf16), ((d, voc), bf16),
        ((voc, cols), bf16), ((voc, cols), bf16), ((n_pass, 128, voc), bf16), ((tok, tok), bf16),
        ((NX, PAD, voc), f32), ((NX, PAD, voc), f32), ((NX, PAD, voc), jnp.int32), ((NX, PAD, voc), jnp.int32),
        ((n_pass, rows, voc), bf16), ((n_pass, rows, voc), bf16), ((n_pass, rows, voc), bf16),
        ((NX, PAD, 128), f32), ((NX, PAD, 128), f32), ((PAD, 128), f32), ((nz, PAD, 128), f32),
        ((NX, PAD, 128), f32), ((8, 128), f32), ((n_pass, 8, 128), f32),
        ((n_pass, rows, voc), bf16), ((n_pass, rows, voc), bf16), ((rows, voc), f32),
        ((tok, voc), bf16), ((2, half, voc), bf16), ((2, half, cols), bf16), ((2, half, cols), bf16),
        ((2, half, cols), f32), ((ny, half, 128), bf16), ((ny, half, 128), bf16),
        ((NX, part, cols), bf16), ((NX, part, cols), bf16), ((NX, part, 128), bf16), ((NX, part, 128), bf16),
        ((ny, part, 128), bf16), ((ny, part, 128), bf16),
        ((nz, rp, 128), f32), ((nz, rp, 128), bf16), ((nz, rp, 128), bf16), ((d, voc), f32),
        ((voc,), f32), ((n_queries, qlen), jnp.int32), ((n_queries, voc), jnp.int32),
    ]
    results = pl.pallas_call(
        functools.partial(kernel, nz, ny, n_queries),
        out_shape=(
            jax.ShapeDtypeStruct((1, 1), f32),
            jax.ShapeDtypeStruct((ro, 128), bf16),
            jax.ShapeDtypeStruct((d, voc), f32),
            jax.ShapeDtypeStruct((voc,), f32),
        ),
        in_specs=[hbm, hbm, hbm, hbm, hbm, pl.BlockSpec(memory_space=pltpu.SMEM), hbm],
        out_specs=(vmem, vmem, anywhere, vmem),
        scratch_shapes=[pltpu.VMEM(s, t) for s, t in scratch] + [
            pltpu.SemaphoreType.DMA((n_copies,)),
            pltpu.SemaphoreType.DMA((n_copies,)),
            pltpu.SemaphoreType.DMA((5 + n_pass,)),
        ],
        compiler_params=pltpu.CompilerParams(
            collective_id=0, has_side_effects=True, vmem_limit_bytes=48 * 1024 * 1024
        ),
    )(*(pltpu.with_memory_space_constraint(a, pltpu.HBM)
        for a in (hidden, weight, bias, token_ids, passages, positive, selected)))
    loss, grad_hidden, grad_weight, grad_bias = pl.pallas_call(
        hand_out,
        out_shape=tuple(jax.ShapeDtypeStruct(r.shape, r.dtype) for r in results),
        in_specs=[anywhere] * 4,
        out_specs=(hbm,) * 4,
        scratch_shapes=[pltpu.SemaphoreType.DMA((4,))],
    )(*results)
    return loss.reshape(()), grad_hidden, grad_weight, grad_bias


def solution(mesh):
    in_specs = (
        P("pass", None),
        P(None, ("vocab", "pass")),
        P(("vocab", "pass")),
        P(),
        P("pass", "vocab"),
        P(),
        P(None, ("vocab", "pass")),
    )
    out_specs = (P(), P("vocab", "pass"), P(None, ("vocab", "pass")), P(("vocab", "pass")))
    body = functools.partial(local, mesh.shape["vocab"] // NX, mesh.shape["pass"] // NC)
    return jax.shard_map(body, mesh=mesh, in_specs=in_specs, out_specs=out_specs, check_vma=False)
```

```python
import functools

import jax
import jax.numpy as jnp
from jax import lax
from jax.experimental import pallas as pl
from jax.experimental.pallas import tpu as pltpu
from jax.sharding import PartitionSpec as P

loss_scale = 4096.0
NX = 4
NC = 2
SLOT = 4
ROWS = 16
MAX_COPIES = 112
MESH = pl.DeviceIdType.MESH
f32 = jnp.float32
bf16 = jnp.bfloat16


def dot(a, b):
    return jnp.dot(a, b, preferred_element_type=f32)


def iota(shape, axis):
    return lax.broadcasted_iota(jnp.int32, shape, axis)


def near_last(size):
    return sorted(range(1, size), key=lambda d: -min(d, size - d))


def kernel(nz, ny, n_queries, hidden, weight, bias, tokens, passages, positive, selected,
           loss_o, gh_o, gw_o, gb_o,
           gath, gath_o, gath_t, w_v, w_t, pas, pas_t, perm, bias_v, bias_b, tokens_v, sel_v, selp, lenp,
           maxl, sell, maxa, sela, pool, pos_s, pos_r, sc_s, sc_x, zs, zr, fin, st_s, st, u_s, u_r, slope,
           lh, lh_o, lhp, gs, gs_r, s1y, s1y_r, s1x, s1x_r, s2x, s2x_r, s2y, s2y_r, high,
           zf, z2, z2_r, gw_v, send_sems, recv_sems, loc_sems):
    n_pass = ny * NC
    v = lax.axis_index("vocab")
    p = lax.axis_index("pass")
    z, x = lax.div(v, NX), lax.rem(v, NX)
    y, c = lax.div(p, NC), lax.rem(p, NC)
    sib = 1 - c
    own_rows = gath.shape[1]
    d_model = gath.shape[2]
    voc = w_v.shape[1] // NC
    wide = NC * voc
    qlen = tokens_v.shape[1]
    per_block = n_queries // n_pass
    tok = ny * own_rows
    half = tok // 2
    ro = (NC * tok) // (nz * NX)
    per_half = nz // 4
    z_block = nz // n_pass
    part = per_half * ro
    tile = sc_s.shape[1]

    def around(value, shift, size):
        return lax.rem(value + (shift + size), size)

    def pass_index(dy, dc):
        return around(y, dy, ny) * NC + around(c, dc, NC)

    def pass_dev(dy, dc):
        return (v, pass_index(dy, dc))

    def x_dev(dx):
        return (z * NX + around(x, dx, NX), p)

    def z_dev(dz):
        return (around(z, dz, nz) * NX + x, p)

    sibling = (v, y * NC + sib)
    pass_peers = [(dy, dc) for dy in near_last(ny) + [0] for dc in range(NC) if dy or dc]
    y_far, x_far, z_far = near_last(ny), near_last(NX), near_last(nz)
    started = []

    def remote(src, dst, device):
        i = len(started)
        copy = pltpu.make_async_remote_copy(
            src_ref=src, dst_ref=dst, send_sem=send_sems.at[i], recv_sem=recv_sems.at[i],
            device_id=device, device_id_type=MESH,
        )
        copy.start()
        started.append(copy)
        return copy

    mine = pl.ds(pl.multiple_of(c * voc, 128), voc)
    theirs = pl.ds(pl.multiple_of(sib * voc, 128), voc)
    mine_pas = pl.ds(pl.multiple_of(c * 128, 128), 128)
    local = [pltpu.make_async_copy(bias, bias_v, loc_sems.at[0]),
             pltpu.make_async_copy(tokens, tokens_v, loc_sems.at[1]),
             pltpu.make_async_copy(selected, sel_v.at[c], loc_sems.at[2]),
             pltpu.make_async_copy(hidden, gath.at[y], loc_sems.at[3]),
             pltpu.make_async_copy(weight, w_v.at[:, mine], loc_sems.at[4])]
    for j in range(ny):
        local.append(pltpu.make_async_copy(
            passages.at[:, pl.ds(j * wide, wide)], pas.at[j, mine_pas], loc_sems.at[5 + j]))
    for copy in local:
        copy.start()

    barrier = pltpu.get_barrier_semaphore()
    peers = ([z_dev(d) for d in z_far] + [x_dev(d) for d in x_far] + [pass_dev(*d) for d in pass_peers])
    for device in peers:
        pl.semaphore_signal(barrier, inc=1, device_id=device, device_id_type=MESH)
    for ref in (maxl, sell, maxa, sela, selp, lenp, zf):
        ref[...] = jnp.zeros_like(ref)
    for copy in local[:3]:
        copy.wait()
    bias_b[c] = jnp.broadcast_to(bias_v[...].reshape(1, voc), (8, voc))
    pl.semaphore_wait(barrier, len(peers))

    hr = own_rows // 2
    top, bottom = pl.ds(0, hr), pl.ds(hr, hr)
    if ny == 4:
        first_up = remote(hidden.at[top], gath.at[y, top], pass_dev(1, 0))
        first_down = remote(hidden.at[bottom], gath.at[y, bottom], pass_dev(-1, 0))
        then_up = remote(hidden.at[bottom], gath.at[y, bottom], pass_dev(1, 0))
        then_down = remote(hidden.at[top], gath.at[y, top], pass_dev(-1, 0))
    else:
        direct = [remote(hidden, gath.at[y], pass_dev(d, 0)) for d in y_far]
    to_w = remote(weight, w_v.at[:, mine], sibling)
    to_small = [remote(selected, sel_v.at[c], sibling), remote(bias_b.at[c], bias_b.at[c], sibling)]
    to_pas = [remote(passages.at[:, pl.ds(j * wide, wide)], pas.at[j, mine_pas], sibling) for j in range(ny)]

    lengths = jnp.sum((tokens_v[...] != 1).astype(f32), axis=1, keepdims=True).astype(jnp.int32)
    lengths = jnp.broadcast_to(lengths, (n_queries, wide))
    for copy in to_small:
        copy.wait_recv()
    picks = jnp.concatenate([sel_v[0], sel_v[1]], axis=1)
    for j in range(ny):
        a = 2 * j * per_block
        b = a + per_block
        selp[j, 0:per_block, :] = jnp.where(c == 0, picks[a:b], picks[b:b + per_block])
        lenp[j, 0:per_block, :] = jnp.where(c == 0, lengths[a:b], lengths[b:b + per_block])

    def block(yy):
        logits = dot(gath[yy], w_v[...]).reshape(per_block, qlen, wide)
        at = iota((per_block, qlen, wide), 1)
        valid = at < lenp[yy][0:per_block].reshape(per_block, 1, wide)
        chosen = at == selp[yy][0:per_block].reshape(per_block, 1, wide)
        maxl[yy, 0:per_block, :] = jnp.max(jnp.where(valid, logits, -jnp.inf), axis=1)
        sell[yy, 0:per_block, :] = jnp.sum(jnp.where(chosen, logits, 0.0), axis=1)

    local[3].wait()
    local[4].wait()
    if ny == 4:
        up, down, far = around(y, -1, ny), around(y, 1, ny), around(y, 2, ny)
        first_up.wait_recv()
        relay_up = remote(gath.at[up, top], gath.at[up, top], pass_dev(1, 0))
        first_down.wait_recv()
        relay_down = remote(gath.at[down, bottom], gath.at[down, bottom], pass_dev(-1, 0))
        to_w.wait_recv()
        block(y)
        then_up.wait_recv()
        block(up)
        then_down.wait_recv()
        block(down)
    else:
        to_w.wait_recv()
        block(y)
    for copy in local[5:]:
        copy.wait()
    for copy in to_pas:
        copy.wait_recv()
    for j in range(ny):
        pas_t[j] = pas[j].T
    if ny == 4:
        relay_up.wait_recv()
        relay_down.wait_recv()
        block(far)
    else:
        for d, copy in zip(y_far, direct):
            copy.wait_recv()
            block(around(y, -d, ny))

    wide_bias = jnp.concatenate([bias_b[0], bias_b[1]], axis=1)[0:1]
    for j in range(ny):
        maxa[j * SLOT:(j + 1) * SLOT, :] = maxl[j, 0:SLOT, :]
    pool[y] = jnp.log1p(jax.nn.softplus(maxa[...] + wide_bias)).astype(bf16)
    to_pool = {d: remote(pool.at[y], pool.at[y], pass_dev(d, 0)) for d in y_far}
    row, lane = iota((ROWS, 256), 0), iota((ROWS, 256), 1)
    place = lax.bitwise_and(row, SLOT - 1)
    query = (lax.shift_right_logical(row, 2) * NC + c) * per_block + place
    query = jnp.where((place < per_block) & (row < ny * SLOT), query, -1)
    pos_col = jnp.zeros((ROWS, 256), jnp.int32)
    for q in range(n_queries):
        pos_col = jnp.where(query == q, positive[q], pos_col)
    is_pos = (lane + y * 256) == pos_col
    onehot = is_pos.astype(f32).astype(bf16)

    score = dot(pool[y], pas_t[y])
    for d in reversed(y_far):
        to_pool[d].wait_recv()
        there = around(y, -d, ny)
        score = score + dot(pool[there], pas_t[there])

    for j in range(NX):
        a, b = (j // 2) * tile, (j % 2) * 128
        sc_s[j] = score[a:a + tile, b:b + 128]
    to_x = [remote(sc_s.at[around(x, d, NX)], sc_x.at[d], x_dev(d)) for d in x_far]
    for j in range(ny):
        pos_s[j] = dot(onehot, pas[j]).astype(bf16)
    to_pos = [remote(pos_s.at[around(y, d, ny)], pos_r.at[d], pass_dev(d, 0)) for d in y_far]
    to_other = remote(gath, gath_o, sibling)
    total = sc_s[x]
    for copy in to_x:
        copy.wait_recv()
    for d in range(1, NX):
        total = total + sc_x[d]
    zs[...] = total
    to_z = [remote(zs, zr.at[d], z_dev(d)) for d in z_far]
    w_t[...] = w_v[...].T
    prow = iota((tok, 128), 0)
    chunk = jnp.floor((prow.astype(f32) + 0.5) * (1.0 / ro)).astype(jnp.int32)
    zl = lax.bitwise_and(chunk, per_half - 1)
    xx = lax.bitwise_and(lax.shift_right_logical(chunk, per_half.bit_length() - 1), NX - 1)
    hh = lax.shift_right_logical(chunk, (per_half * NX).bit_length() - 1)
    natural = prow + ro * ((hh * per_half + zl) * NX + xx - chunk)
    plane = iota((tok, 128), 1)
    for j in range(tok // 128):
        perm[:, j * 128:(j + 1) * 128] = (natural == plane + j * 128).astype(f32).astype(bf16)
    for j in range(ny):
        sela[j * SLOT:(j + 1) * SLOT, :] = sell[j, 0:SLOT, :]
    at_sel = sela[...] + wide_bias
    slope[...] = jax.nn.sigmoid(at_sel) / (1.0 + jax.nn.softplus(at_sel))
    gath_t[0] = gath[...].reshape(tok, d_model).T
    for copy in to_z:
        copy.wait_recv()
    for d in range(1, nz):
        total = total + zr[d]
    fin[x] = total
    to_fin = [remote(fin.at[x], fin.at[x], x_dev(d)) for d in x_far]
    for copy in to_pos:
        copy.wait_recv()
    pos_entries = pos_s[y].astype(f32)
    for d in range(1, ny):
        pos_entries = pos_entries + pos_r[d].astype(f32)
    for copy in to_fin:
        copy.wait_recv()

    score = jnp.concatenate([jnp.concatenate([fin[j], fin[j + 1]], axis=1) for j in range(0, NX, 2)], axis=0)
    peak = jnp.max(score, axis=1, keepdims=True)
    terms = jnp.exp(score - peak)
    other = jnp.where(is_pos, 0.0, terms)
    stats = [peak, jnp.sum(other, axis=1, keepdims=True),
             jnp.sum(jnp.where(is_pos, terms, 0.0), axis=1, keepdims=True),
             jnp.sum(jnp.where(is_pos, score, 0.0), axis=1, keepdims=True)]
    eye = iota((ROWS, 128), 0) == iota((ROWS, 128), 1)
    turned = [jnp.sum(jnp.where(eye, s, 0.0), axis=0, keepdims=True) for s in stats]
    st_s[...] = jnp.concatenate(turned + [jnp.zeros((8 - len(turned), 128), f32)], axis=0)
    other = other.astype(bf16)
    to_u = {}
    for d in y_far:
        there = around(y, d, ny)
        u_s[there] = dot(other, pas[there]).astype(bf16)
        to_u[d] = remote(u_s.at[there], u_r.at[d], pass_dev(d, 0))
    to_st = [remote(st_s, st.at[d], pass_dev(d, 0)) for d in y_far]
    st[0] = st_s[...]
    mine_u = dot(other, pas[y])
    for copy in to_st:
        copy.wait_recv()
    peaks = [st[i][0:1] for i in range(ny)]
    highest = functools.reduce(jnp.maximum, peaks)
    scale = [jnp.exp(k - highest) for k in peaks]
    rest = sum(scale[i] * st[i][1:2] for i in range(ny))
    denom = rest + sum(scale[i] * st[i][2:3] for i in range(ny))
    pos_score = sum(st[i][3:4] for i in range(ny))
    log_total = highest + jnp.log(denom)
    lane1 = iota((1, 128), 1)
    counted = (lax.bitwise_and(lane1, SLOT - 1) < per_block) & (lane1 < ny * SLOT)
    loss = jnp.sum(jnp.where(counted, log_total - pos_score, 0.0), axis=1, keepdims=True)
    factor = (loss_scale / n_queries) / denom

    def column(line):
        return jnp.sum(jnp.where(eye, line, 0.0), axis=1, keepdims=True)

    term = column(scale[0] * factor) * mine_u - column(rest * factor) * pos_entries
    for d in reversed(y_far):
        to_u[d].wait_recv()
        term = term + column(scale[d] * factor) * u_r[d].astype(f32)

    grad = term * slope[...]
    at = iota((per_block, qlen, wide), 1)
    for j in range(ny):
        chosen = at == selp[j][0:per_block].reshape(per_block, 1, wide)
        some = grad[j * SLOT:j * SLOT + per_block].reshape(per_block, 1, wide)
        lh[j * own_rows:(j + 1) * own_rows, :] = jnp.where(chosen, some, 0.0).reshape(own_rows, wide).astype(bf16)

    lhp[0] = dot(perm[0:half, :], lh[...]).astype(bf16)
    out = dot(lhp[0], w_t[...])
    for j in range(n_pass):
        s1y[j] = out[:, j * 128:(j + 1) * 128].astype(bf16)
    to_s1y = {d: remote(s1y.at[pass_index(*d)], s1y_r.at[d[0] * NC + d[1]], pass_dev(*d)) for d in pass_peers}
    lhp[1] = dot(perm[half:tok, :], lh[...]).astype(bf16)
    out = dot(lhp[1], w_t[...])
    for j in range(NX):
        s1x[j] = out[j * part:(j + 1) * part].astype(bf16)
    to_s1x = [remote(s1x.at[around(x, d, NX)], s1x_r.at[d], x_dev(d)) for d in x_far]

    at_row = iota((ROWS, wide), 0)
    real = (lax.bitwise_and(at_row, SLOT - 1) < per_block) & (at_row < ny * SLOT)
    summed = jnp.sum(jnp.where(real, grad, 0.0), axis=0, keepdims=True)
    first = iota((8, voc), 0) == 0
    for j in range(NC):
        gs[j] = jnp.where(first, summed[:, j * voc:(j + 1) * voc], loss)
    to_gs = remote(gs.at[sib], gs_r, sibling)
    to_lh = remote(lh.at[:, theirs], lh_o, sibling)
    to_other.wait_recv()
    gath_t[1] = gath_o[...].reshape(tok, d_model).T
    gw_v[...] = dot(gath_t[0], lh[:, mine])

    for copy in to_s1y.values():
        copy.wait_recv()
    same, cross = s1y[p].astype(f32), s1y_r[1].astype(f32)
    for d in range(1, ny):
        same = same + s1y_r[d * NC].astype(f32)
        cross = cross + s1y_r[d * NC + 1].astype(f32)
    s2x[c] = same.astype(bf16).reshape(NX, part, 128)
    s2x[sib] = cross.astype(bf16).reshape(NX, part, 128)
    to_s2x = [remote(s2x.at[:, around(x, d, NX)], s2x_r.at[d], x_dev(d)) for d in x_far]
    for copy in to_s1x:
        copy.wait_recv()
    both = s1x[x].astype(f32)
    for d in range(1, NX):
        both = both + s1x_r[d].astype(f32)
    for j in range(n_pass):
        s2y[j] = both[:, j * 128:(j + 1) * 128].astype(bf16)
    to_s2y = {d: remote(s2y.at[pass_index(*d)], s2y_r.at[d[0] * NC + d[1]], pass_dev(*d)) for d in pass_peers}
    for copy in to_s2x:
        copy.wait_recv()

    def to_rows(core, k):
        return (NC * (k // z_block) + core) * z_block + k % z_block

    for core in range(NC):
        low = s2x[core, x].astype(f32)
        for d in range(1, NX):
            low = low + s2x_r[d, core].astype(f32)
        for k in range(per_half):
            zf[to_rows(core, k), 0:ro, :] = low[k * ro:(k + 1) * ro]
    for copy in to_s2y.values():
        copy.wait_recv()
    same, cross = s2y[p].astype(f32), s2y_r[1].astype(f32)
    for d in range(1, ny):
        same = same + s2y_r[d * NC].astype(f32)
        cross = cross + s2y_r[d * NC + 1].astype(f32)
    high[c] = same
    high[sib] = cross
    for core in range(NC):
        for k in range(per_half):
            zf[to_rows(core, per_half + k), 0:ro, :] = high[core, k * ro:(k + 1) * ro]
    z2[...] = zf[...].astype(bf16)
    to_z2 = [remote(z2.at[around(z, d, nz)], z2_r.at[d], z_dev(d)) for d in z_far]
    to_lh.wait_recv()
    gw_v[...] += dot(gath_t[1], lh_o[...])
    gw_out = pltpu.make_async_copy(gw_v, gw_o, loc_sems.at[0])
    gw_out.start()
    to_gs.wait_recv()
    gb_o[...] = (gs[c][0:1] + gs_r[0:1]).reshape(voc)
    loss_o[...] = (gs[c][1:2, 0:1] + gs_r[1:2, 0:1]) * (1.0 / n_queries)
    total = zf[z]
    for copy in to_z2:
        copy.wait_recv()
    for d in range(1, nz):
        total = total + z2_r[d].astype(f32)
    gh_o[...] = total[0:ro].astype(bf16)

    for copy in started:
        copy.wait_send()
    gw_out.wait()


def hand_out(*refs):
    sems = refs[8]
    copies = [pltpu.make_async_copy(refs[i], refs[4 + i], sems.at[i]) for i in range(4)]
    for copy in copies:
        copy.start()
    for copy in copies:
        copy.wait()


def local(nz, ny, hidden, weight, bias, token_ids, passages, positive, selected):
    n_queries, qlen = token_ids.shape
    own_rows, d = hidden.shape
    voc = weight.shape[1]
    wide = NC * voc
    n_pass = ny * NC
    tok = ny * own_rows
    half = tok // 2
    ro = (NC * tok) // (nz * NX)
    rp = -(-ro // 16) * 16
    part = (nz // 4) * ro
    tile = ROWS * 2 // NX
    i32 = jnp.int32
    vmem = pl.BlockSpec(memory_space=pltpu.VMEM)
    smem = pl.BlockSpec(memory_space=pltpu.SMEM)
    anywhere = pl.BlockSpec(memory_space=pl.ANY)
    hbm = pl.BlockSpec(memory_space=pltpu.HBM)
    scratch = [
        ((ny, own_rows, d), bf16), ((ny, own_rows, d), bf16), ((NC, d, tok), bf16),
        ((d, wide), bf16), ((wide, d), bf16),
        ((ny, NC * 128, wide), bf16), ((ny, wide, NC * 128), bf16), ((tok, tok), bf16),
        ((voc,), f32), ((NC, 8, voc), f32), ((n_queries, qlen), i32), ((NC, n_queries, voc), i32),
        ((ny, 8, wide), i32), ((ny, 8, wide), i32),
        ((ny, 8, wide), f32), ((ny, 8, wide), f32), ((ROWS, wide), f32), ((ROWS, wide), f32),
        ((ny, ROWS, wide), bf16), ((ny, ROWS, wide), bf16), ((ny, ROWS, wide), bf16),
        ((NX, tile, 128), f32), ((NX, tile, 128), f32), ((tile, 128), f32), ((nz, tile, 128), f32),
        ((NX, tile, 128), f32), ((8, 128), f32), ((ny, 8, 128), f32),
        ((ny, ROWS, wide), bf16), ((ny, ROWS, wide), bf16), ((ROWS, wide), f32),
        ((tok, wide), bf16), ((tok, voc), bf16), ((2, half, wide), bf16),
        ((NC, 8, voc), f32), ((8, voc), f32),
        ((n_pass, half, 128), bf16), ((n_pass, half, 128), bf16),
        ((NX, part, d), bf16), ((NX, part, d), bf16),
        ((NC, NX, part, 128), bf16), ((NX, NC, part, 128), bf16),
        ((n_pass, part, 128), bf16), ((n_pass, part, 128), bf16), ((NC, part, 128), f32),
        ((nz, rp, 128), f32), ((nz, rp, 128), bf16), ((nz, rp, 128), bf16), ((d, voc), f32),
    ]
    results = pl.pallas_call(
        functools.partial(kernel, nz, ny, n_queries),
        out_shape=(
            jax.ShapeDtypeStruct((1, 1), f32),
            jax.ShapeDtypeStruct((ro, 128), bf16),
            jax.ShapeDtypeStruct((d, voc), f32),
            jax.ShapeDtypeStruct((voc,), f32),
        ),
        in_specs=[hbm, hbm, hbm, hbm, hbm, smem, hbm],
        out_specs=(vmem, vmem, anywhere, vmem),
        scratch_shapes=[pltpu.VMEM(s, t) for s, t in scratch] + [
            pltpu.SemaphoreType.DMA((MAX_COPIES,)),
            pltpu.SemaphoreType.DMA((MAX_COPIES,)),
            pltpu.SemaphoreType.DMA((5 + ny,)),
        ],
        compiler_params=pltpu.CompilerParams(
            collective_id=0, has_side_effects=True, vmem_limit_bytes=48 * 1024 * 1024
        ),
    )(*(pltpu.with_memory_space_constraint(a, pltpu.HBM)
        for a in (hidden, weight, bias, token_ids, passages, positive, selected)))
    loss, grad_hidden, grad_weight, grad_bias = pl.pallas_call(
        hand_out,
        out_shape=tuple(jax.ShapeDtypeStruct(r.shape, r.dtype) for r in results),
        in_specs=[vmem] * 4,
        out_specs=(hbm,) * 4,
        scratch_shapes=[pltpu.SemaphoreType.DMA((4,))],
    )(*results)
    return loss.reshape(()), grad_hidden, grad_weight, grad_bias


def solution(mesh):
    in_specs = (
        P("pass", None),
        P(None, ("vocab", "pass")),
        P(("vocab", "pass")),
        P(),
        P("pass", "vocab"),
        P(),
        P(None, ("vocab", "pass")),
    )
    out_specs = (P(), P("vocab", "pass"), P(None, ("vocab", "pass")), P(("vocab", "pass")))
    body = functools.partial(local, mesh.shape["vocab"] // NX, mesh.shape["pass"] // NC)
    return jax.shard_map(body, mesh=mesh, in_specs=in_specs, out_specs=out_specs, check_vma=False)
```

```python
import functools

import jax
import jax.numpy as jnp
from jax import lax
from jax.experimental import pallas as pl
from jax.experimental.pallas import tpu as pltpu
from jax.sharding import PartitionSpec as P

loss_scale = 4096.0
NX = 4
NC = 2
SLOT = 4
ROWS = 16
MAX_COPIES = 112
MESH = pl.DeviceIdType.MESH
f32 = jnp.float32
bf16 = jnp.bfloat16


def dot(a, b):
    return jnp.dot(a, b, preferred_element_type=f32)


def iota(shape, axis):
    return lax.broadcasted_iota(jnp.int32, shape, axis)


def near_last(size):
    return sorted(range(1, size), key=lambda d: -min(d, size - d))


def kernel(nz, ny, n_queries, hidden, weight, bias, tokens, passages, positive, selected,
           loss_o, gh_o, gw_o, gb_o,
           gath, gath_o, gath_t, w_v, w_t, pas, pas_t, perm, bias_v, bias_b, tokens_v, sel_v, selp, lenp,
           maxl, sell, maxa, sela, pool, pos_s, pos_r, sc_s, sc_x, zs, zr, fin, st_s, st, u_s, u_r, slope,
           lh, lh_o, lhp, gs, gs_r, s1y, s1y_r, s1x, s1x_r, s2x, s2x_r, s2y, s2y_r, high,
           zf, z2, z2_r, gw_v, send_sems, recv_sems, loc_sems, entry):
    n_pass = ny * NC
    v = lax.axis_index("vocab")
    p = lax.axis_index("pass")
    z, x = lax.div(v, NX), lax.rem(v, NX)
    y, c = lax.div(p, NC), lax.rem(p, NC)
    sib = 1 - c
    own_rows = gath.shape[1]
    d_model = gath.shape[2]
    voc = w_v.shape[1] // NC
    wide = NC * voc
    qlen = tokens_v.shape[1]
    per_block = n_queries // n_pass
    tok = ny * own_rows
    half = tok // 2
    ro = (NC * tok) // (nz * NX)
    per_half = nz // 4
    z_block = nz // n_pass
    part = per_half * ro
    tile = sc_s.shape[1]

    def around(value, shift, size):
        return lax.rem(value + (shift + size), size)

    def pass_index(dy, dc):
        return around(y, dy, ny) * NC + around(c, dc, NC)

    def pass_dev(dy, dc):
        return (v, pass_index(dy, dc))

    def x_dev(dx):
        return (z * NX + around(x, dx, NX), p)

    def z_dev(dz):
        return (around(z, dz, nz) * NX + x, p)

    sibling = (v, y * NC + sib)
    pass_peers = [(dy, dc) for dy in near_last(ny) + [0] for dc in range(NC) if dy or dc]
    y_far, x_far, z_far = near_last(ny), near_last(NX), near_last(nz)
    started = []

    def remote(src, dst, device):
        i = len(started)
        copy = pltpu.make_async_remote_copy(
            src_ref=src, dst_ref=dst, send_sem=send_sems.at[i], recv_sem=recv_sems.at[i],
            device_id=device, device_id_type=MESH,
        )
        copy.start()
        started.append(copy)
        return copy

    mine = pl.ds(pl.multiple_of(c * voc, 128), voc)
    theirs = pl.ds(pl.multiple_of(sib * voc, 128), voc)
    mine_pas = pl.ds(pl.multiple_of(c * 128, 128), 128)
    local = [pltpu.make_async_copy(bias, bias_v, loc_sems.at[0]),
             pltpu.make_async_copy(tokens, tokens_v, loc_sems.at[1]),
             pltpu.make_async_copy(selected, sel_v.at[c], loc_sems.at[2]),
             pltpu.make_async_copy(hidden, gath.at[y], loc_sems.at[3]),
             pltpu.make_async_copy(weight, w_v.at[:, mine], loc_sems.at[4])]
    for j in range(ny):
        local.append(pltpu.make_async_copy(
            passages.at[:, pl.ds(j * wide, wide)], pas.at[j, mine_pas], loc_sems.at[5 + j]))
    for copy in local:
        copy.start()

    barrier = pltpu.get_barrier_semaphore()
    passed_on = nz == 16
    z_near = (2, -2, 1, -1) if passed_on else z_far
    peers = ([z_dev(d) for d in z_near] + [pass_dev(*d) for d in pass_peers] + [x_dev(d) for d in x_far])
    for device in peers:
        pl.semaphore_signal(barrier, inc=1, device_id=device, device_id_type=MESH)
    pl.semaphore_wait(barrier, len(peers))

    hr = own_rows // 2
    top, bottom = pl.ds(0, hr), pl.ds(hr, hr)
    if ny == 4:
        pieces = [(pl.ds(i, 16), pl.ds(hr + i, 16)) for i in range(0, hr, 16)]
        first = []
        for a, b in pieces:
            first.append((remote(hidden.at[a], gath.at[y, a], pass_dev(1, 0)),
                          remote(hidden.at[b], gath.at[y, b], pass_dev(-1, 0))))
        then_up = remote(hidden.at[bottom], gath.at[y, bottom], pass_dev(1, 0))
        then_down = remote(hidden.at[top], gath.at[y, top], pass_dev(-1, 0))
    else:
        direct = [remote(hidden, gath.at[y], pass_dev(d, 0)) for d in y_far]
    if passed_on:
        pl.semaphore_signal(entry.at[0], inc=1, device_id=z_dev(2), device_id_type=MESH)
        pl.semaphore_signal(entry.at[1], inc=1, device_id=z_dev(-2), device_id_type=MESH)
    to_w = remote(weight, w_v.at[:, mine], sibling)
    for copy in local[:3]:
        copy.wait()
    bias_b[c] = jnp.broadcast_to(bias_v[...].reshape(1, voc), (8, voc))
    to_small = [remote(selected, sel_v.at[c], sibling), remote(bias_b.at[c], bias_b.at[c], sibling)]
    to_pas = [remote(passages.at[:, pl.ds(j * wide, wide)], pas.at[j, mine_pas], sibling) for j in range(ny)]

    if ny == 4:
        up, down, far = around(y, -1, ny), around(y, 1, ny), around(y, 2, ny)
        relayed = []
        for (a, b), (to_up, to_down) in zip(pieces, first):
            to_up.wait_recv()
            relayed.append(remote(gath.at[up, a], gath.at[up, a], pass_dev(1, 0)))
            to_down.wait_recv()
            relayed.append(remote(gath.at[down, b], gath.at[down, b], pass_dev(-1, 0)))
    if passed_on:
        pl.semaphore_wait(entry.at[0], 1)
        pl.semaphore_wait(entry.at[1], 1)
        pl.semaphore_signal(entry.at[2], inc=1, device_id=z_dev(4), device_id_type=MESH)
        pl.semaphore_signal(entry.at[3], inc=1, device_id=z_dev(-4), device_id_type=MESH)
    for ref in (maxl, sell, maxa, sela, selp, lenp, zf):
        ref[...] = jnp.zeros_like(ref)

    lengths = jnp.sum((tokens_v[...] != 1).astype(f32), axis=1, keepdims=True).astype(jnp.int32)
    lengths = jnp.broadcast_to(lengths, (n_queries, wide))
    for copy in to_small:
        copy.wait_recv()
    picks = jnp.concatenate([sel_v[0], sel_v[1]], axis=1)
    for j in range(ny):
        a = 2 * j * per_block
        b = a + per_block
        selp[j, 0:per_block, :] = jnp.where(c == 0, picks[a:b], picks[b:b + per_block])
        lenp[j, 0:per_block, :] = jnp.where(c == 0, lengths[a:b], lengths[b:b + per_block])

    def block(yy):
        logits = dot(gath[yy], w_v[...]).reshape(per_block, qlen, wide)
        at = iota((per_block, qlen, wide), 1)
        valid = at < lenp[yy][0:per_block].reshape(per_block, 1, wide)
        chosen = at == selp[yy][0:per_block].reshape(per_block, 1, wide)
        maxl[yy, 0:per_block, :] = jnp.max(jnp.where(valid, logits, -jnp.inf), axis=1)
        sell[yy, 0:per_block, :] = jnp.sum(jnp.where(chosen, logits, 0.0), axis=1)

    local[3].wait()
    local[4].wait()
    if ny == 4:
        to_w.wait_recv()
        block(y)
        then_up.wait_recv()
        block(up)
        then_down.wait_recv()
        block(down)
    else:
        to_w.wait_recv()
        block(y)
    for copy in local[5:]:
        copy.wait()
    for copy in to_pas:
        copy.wait_recv()
    for j in range(ny):
        pas_t[j] = pas[j].T
    if ny == 4:
        for copy in relayed:
            copy.wait_recv()
        block(far)
    else:
        for d, copy in zip(y_far, direct):
            copy.wait_recv()
            block(around(y, -d, ny))

    wide_bias = jnp.concatenate([bias_b[0], bias_b[1]], axis=1)[0:1]
    for j in range(ny):
        maxa[j * SLOT:(j + 1) * SLOT, :] = maxl[j, 0:SLOT, :]
    pool[y] = jnp.log1p(jax.nn.softplus(maxa[...] + wide_bias)).astype(bf16)
    to_pool = {d: remote(pool.at[y], pool.at[y], pass_dev(d, 0)) for d in y_far}
    row, lane = iota((ROWS, 256), 0), iota((ROWS, 256), 1)
    place = lax.bitwise_and(row, SLOT - 1)
    query = (lax.shift_right_logical(row, 2) * NC + c) * per_block + place
    query = jnp.where((place < per_block) & (row < ny * SLOT), query, -1)
    pos_col = jnp.zeros((ROWS, 256), jnp.int32)
    for q in range(n_queries):
        pos_col = jnp.where(query == q, positive[q], pos_col)
    is_pos = (lane + y * 256) == pos_col
    onehot = is_pos.astype(f32).astype(bf16)

    score = dot(pool[y], pas_t[y])
    for d in reversed(y_far):
        to_pool[d].wait_recv()
        there = around(y, -d, ny)
        score = score + dot(pool[there], pas_t[there])

    for j in range(NX):
        a, b = (j // 2) * tile, (j % 2) * 128
        sc_s[j] = score[a:a + tile, b:b + 128]
    to_x = [remote(sc_s.at[around(x, d, NX)], sc_x.at[d], x_dev(d)) for d in x_far]
    for j in range(ny):
        pos_s[j] = dot(onehot, pas[j]).astype(bf16)
    to_pos = [remote(pos_s.at[around(y, d, ny)], pos_r.at[d], pass_dev(d, 0)) for d in y_far]
    to_other = remote(gath, gath_o, sibling)
    total = sc_s[x]
    for copy in to_x:
        copy.wait_recv()
    for d in range(1, NX):
        total = total + sc_x[d]
    zs[...] = total
    if passed_on:
        pl.semaphore_wait(entry.at[2], 1)
        pl.semaphore_wait(entry.at[3], 1)
    to_z = [remote(zs, zr.at[d], z_dev(d)) for d in z_far]
    w_t[...] = w_v[...].T
    prow = iota((tok, 128), 0)
    chunk = jnp.floor((prow.astype(f32) + 0.5) * (1.0 / ro)).astype(jnp.int32)
    zl = lax.bitwise_and(chunk, per_half - 1)
    xx = lax.bitwise_and(lax.shift_right_logical(chunk, per_half.bit_length() - 1), NX - 1)
    hh = lax.shift_right_logical(chunk, (per_half * NX).bit_length() - 1)
    natural = prow + ro * ((hh * per_half + zl) * NX + xx - chunk)
    plane = iota((tok, 128), 1)
    for j in range(tok // 128):
        perm[:, j * 128:(j + 1) * 128] = (natural == plane + j * 128).astype(f32).astype(bf16)
    for j in range(ny):
        sela[j * SLOT:(j + 1) * SLOT, :] = sell[j, 0:SLOT, :]
    at_sel = sela[...] + wide_bias
    slope[...] = jax.nn.sigmoid(at_sel) / (1.0 + jax.nn.softplus(at_sel))
    gath_t[0] = gath[...].reshape(tok, d_model).T
    for copy in to_z:
        copy.wait_recv()
    for d in range(1, nz):
        total = total + zr[d]
    fin[x] = total
    to_fin = [remote(fin.at[x], fin.at[x], x_dev(d)) for d in x_far]
    for copy in to_pos:
        copy.wait_recv()
    pos_entries = pos_s[y].astype(f32)
    for d in range(1, ny):
        pos_entries = pos_entries + pos_r[d].astype(f32)
    for copy in to_fin:
        copy.wait_recv()

    score = jnp.concatenate([jnp.concatenate([fin[j], fin[j + 1]], axis=1) for j in range(0, NX, 2)], axis=0)
    peak = jnp.max(score, axis=1, keepdims=True)
    terms = jnp.exp(score - peak)
    other = jnp.where(is_pos, 0.0, terms)
    stats = [peak, jnp.sum(other, axis=1, keepdims=True),
             jnp.sum(jnp.where(is_pos, terms, 0.0), axis=1, keepdims=True),
             jnp.sum(jnp.where(is_pos, score, 0.0), axis=1, keepdims=True)]
    eye = iota((ROWS, 128), 0) == iota((ROWS, 128), 1)
    turned = [jnp.sum(jnp.where(eye, s, 0.0), axis=0, keepdims=True) for s in stats]
    st_s[...] = jnp.concatenate(turned + [jnp.zeros((8 - len(turned), 128), f32)], axis=0)
    other = other.astype(bf16)
    to_u = {}
    for d in y_far:
        there = around(y, d, ny)
        u_s[there] = dot(other, pas[there]).astype(bf16)
        to_u[d] = remote(u_s.at[there], u_r.at[d], pass_dev(d, 0))
    to_st = [remote(st_s, st.at[d], pass_dev(d, 0)) for d in y_far]
    st[0] = st_s[...]
    mine_u = dot(other, pas[y])
    for copy in to_st:
        copy.wait_recv()
    peaks = [st[i][0:1] for i in range(ny)]
    highest = functools.reduce(jnp.maximum, peaks)
    scale = [jnp.exp(k - highest) for k in peaks]
    rest = sum(scale[i] * st[i][1:2] for i in range(ny))
    denom = rest + sum(scale[i] * st[i][2:3] for i in range(ny))
    pos_score = sum(st[i][3:4] for i in range(ny))
    log_total = highest + jnp.log(denom)
    lane1 = iota((1, 128), 1)
    counted = (lax.bitwise_and(lane1, SLOT - 1) < per_block) & (lane1 < ny * SLOT)
    loss = jnp.sum(jnp.where(counted, log_total - pos_score, 0.0), axis=1, keepdims=True)
    factor = (loss_scale / n_queries) / denom

    def column(line):
        return jnp.sum(jnp.where(eye, line, 0.0), axis=1, keepdims=True)

    term = column(scale[0] * factor) * mine_u - column(rest * factor) * pos_entries
    for d in reversed(y_far):
        to_u[d].wait_recv()
        term = term + column(scale[d] * factor) * u_r[d].astype(f32)

    grad = term * slope[...]
    at = iota((per_block, qlen, wide), 1)
    for j in range(ny):
        chosen = at == selp[j][0:per_block].reshape(per_block, 1, wide)
        some = grad[j * SLOT:j * SLOT + per_block].reshape(per_block, 1, wide)
        lh[j * own_rows:(j + 1) * own_rows, :] = jnp.where(chosen, some, 0.0).reshape(own_rows, wide).astype(bf16)

    lhp[0] = dot(perm[0:half, :], lh[...]).astype(bf16)
    out = dot(lhp[0], w_t[...])
    for j in range(n_pass):
        s1y[j] = out[:, j * 128:(j + 1) * 128].astype(bf16)
    to_s1y = {d: remote(s1y.at[pass_index(*d)], s1y_r.at[d[0] * NC + d[1]], pass_dev(*d)) for d in pass_peers}
    lhp[1] = dot(perm[half:tok, :], lh[...]).astype(bf16)
    out = dot(lhp[1], w_t[...])
    for j in range(NX):
        s1x[j] = out[j * part:(j + 1) * part].astype(bf16)
    to_s1x = [remote(s1x.at[around(x, d, NX)], s1x_r.at[d], x_dev(d)) for d in x_far]

    at_row = iota((ROWS, wide), 0)
    real = (lax.bitwise_and(at_row, SLOT - 1) < per_block) & (at_row < ny * SLOT)
    summed = jnp.sum(jnp.where(real, grad, 0.0), axis=0, keepdims=True)
    first = iota((8, voc), 0) == 0
    for j in range(NC):
        gs[j] = jnp.where(first, summed[:, j * voc:(j + 1) * voc], loss)
    to_gs = remote(gs.at[sib], gs_r, sibling)
    to_lh = remote(lh.at[:, theirs], lh_o, sibling)
    to_other.wait_recv()
    gath_t[1] = gath_o[...].reshape(tok, d_model).T
    gw_v[...] = dot(gath_t[0], lh[:, mine])

    for copy in to_s1y.values():
        copy.wait_recv()
    same, cross = s1y[p].astype(f32), s1y_r[1].astype(f32)
    for d in range(1, ny):
        same = same + s1y_r[d * NC].astype(f32)
        cross = cross + s1y_r[d * NC + 1].astype(f32)
    s2x[c] = same.astype(bf16).reshape(NX, part, 128)
    s2x[sib] = cross.astype(bf16).reshape(NX, part, 128)
    to_s2x = [remote(s2x.at[:, around(x, d, NX)], s2x_r.at[d], x_dev(d)) for d in x_far]
    for copy in to_s1x:
        copy.wait_recv()
    both = s1x[x].astype(f32)
    for d in range(1, NX):
        both = both + s1x_r[d].astype(f32)
    for j in range(n_pass):
        s2y[j] = both[:, j * 128:(j + 1) * 128].astype(bf16)
    to_s2y = {d: remote(s2y.at[pass_index(*d)], s2y_r.at[d[0] * NC + d[1]], pass_dev(*d)) for d in pass_peers}
    for copy in to_s2x:
        copy.wait_recv()

    def to_rows(core, k):
        return (NC * (k // z_block) + core) * z_block + k % z_block

    for core in range(NC):
        low = s2x[core, x].astype(f32)
        for d in range(1, NX):
            low = low + s2x_r[d, core].astype(f32)
        for k in range(per_half):
            zf[to_rows(core, k), 0:ro, :] = low[k * ro:(k + 1) * ro]
    for copy in to_s2y.values():
        copy.wait_recv()
    same, cross = s2y[p].astype(f32), s2y_r[1].astype(f32)
    for d in range(1, ny):
        same = same + s2y_r[d * NC].astype(f32)
        cross = cross + s2y_r[d * NC + 1].astype(f32)
    high[c] = same
    high[sib] = cross
    for core in range(NC):
        for k in range(per_half):
            zf[to_rows(core, per_half + k), 0:ro, :] = high[core, k * ro:(k + 1) * ro]
    z2[...] = zf[...].astype(bf16)
    to_z2 = [remote(z2.at[around(z, d, nz)], z2_r.at[d], z_dev(d)) for d in z_far]
    for copy in started[:-len(to_z2)]:
        copy.wait_send()
    to_lh.wait_recv()
    gw_v[...] += dot(gath_t[1], lh_o[...])
    gw_out = pltpu.make_async_copy(gw_v, gw_o, loc_sems.at[0])
    gw_out.start()
    to_gs.wait_recv()
    gb_o[...] = (gs[c][0:1] + gs_r[0:1]).reshape(voc)
    loss_o[...] = (gs[c][1:2, 0:1] + gs_r[1:2, 0:1]) * (1.0 / n_queries)
    total = zf[z]
    for copy in to_z2:
        copy.wait_recv()
    for d in range(1, nz):
        total = total + z2_r[d].astype(f32)
    gh_o[...] = total[0:ro].astype(bf16)

    for copy in to_z2:
        copy.wait_send()
    gw_out.wait()


def hand_out(*refs):
    sems = refs[8]
    copies = [pltpu.make_async_copy(refs[i], refs[4 + i], sems.at[i]) for i in range(4)]
    for copy in copies:
        copy.start()
    for copy in copies:
        copy.wait()


def local(nz, ny, hidden, weight, bias, token_ids, passages, positive, selected):
    n_queries, qlen = token_ids.shape
    own_rows, d = hidden.shape
    voc = weight.shape[1]
    wide = NC * voc
    n_pass = ny * NC
    tok = ny * own_rows
    half = tok // 2
    ro = (NC * tok) // (nz * NX)
    rp = -(-ro // 16) * 16
    part = (nz // 4) * ro
    tile = ROWS * 2 // NX
    i32 = jnp.int32
    vmem = pl.BlockSpec(memory_space=pltpu.VMEM)
    smem = pl.BlockSpec(memory_space=pltpu.SMEM)
    anywhere = pl.BlockSpec(memory_space=pl.ANY)
    hbm = pl.BlockSpec(memory_space=pltpu.HBM)
    scratch = [
        ((ny, own_rows, d), bf16), ((ny, own_rows, d), bf16), ((NC, d, tok), bf16),
        ((d, wide), bf16), ((wide, d), bf16),
        ((ny, NC * 128, wide), bf16), ((ny, wide, NC * 128), bf16), ((tok, tok), bf16),
        ((voc,), f32), ((NC, 8, voc), f32), ((n_queries, qlen), i32), ((NC, n_queries, voc), i32),
        ((ny, 8, wide), i32), ((ny, 8, wide), i32),
        ((ny, 8, wide), f32), ((ny, 8, wide), f32), ((ROWS, wide), f32), ((ROWS, wide), f32),
        ((ny, ROWS, wide), bf16), ((ny, ROWS, wide), bf16), ((ny, ROWS, wide), bf16),
        ((NX, tile, 128), f32), ((NX, tile, 128), f32), ((tile, 128), f32), ((nz, tile, 128), f32),
        ((NX, tile, 128), f32), ((8, 128), f32), ((ny, 8, 128), f32),
        ((ny, ROWS, wide), bf16), ((ny, ROWS, wide), bf16), ((ROWS, wide), f32),
        ((tok, wide), bf16), ((tok, voc), bf16), ((2, half, wide), bf16),
        ((NC, 8, voc), f32), ((8, voc), f32),
        ((n_pass, half, 128), bf16), ((n_pass, half, 128), bf16),
        ((NX, part, d), bf16), ((NX, part, d), bf16),
        ((NC, NX, part, 128), bf16), ((NX, NC, part, 128), bf16),
        ((n_pass, part, 128), bf16), ((n_pass, part, 128), bf16), ((NC, part, 128), f32),
        ((nz, rp, 128), f32), ((nz, rp, 128), bf16), ((nz, rp, 128), bf16), ((d, voc), f32),
    ]
    results = pl.pallas_call(
        functools.partial(kernel, nz, ny, n_queries),
        out_shape=(
            jax.ShapeDtypeStruct((1, 1), f32),
            jax.ShapeDtypeStruct((ro, 128), bf16),
            jax.ShapeDtypeStruct((d, voc), f32),
            jax.ShapeDtypeStruct((voc,), f32),
        ),
        in_specs=[hbm, hbm, hbm, hbm, hbm, smem, hbm],
        out_specs=(vmem, vmem, anywhere, vmem),
        scratch_shapes=[pltpu.VMEM(s, t) for s, t in scratch] + [
            pltpu.SemaphoreType.DMA((MAX_COPIES,)),
            pltpu.SemaphoreType.DMA((MAX_COPIES,)),
            pltpu.SemaphoreType.DMA((5 + ny,)),
            pltpu.SemaphoreType.REGULAR((4,)),
        ],
        compiler_params=pltpu.CompilerParams(
            collective_id=0, has_side_effects=True, vmem_limit_bytes=48 * 1024 * 1024
        ),
    )(*(pltpu.with_memory_space_constraint(a, pltpu.HBM)
        for a in (hidden, weight, bias, token_ids, passages, positive, selected)))
    loss, grad_hidden, grad_weight, grad_bias = pl.pallas_call(
        hand_out,
        out_shape=tuple(jax.ShapeDtypeStruct(r.shape, r.dtype) for r in results),
        in_specs=[anywhere] * 4,
        out_specs=(hbm,) * 4,
        scratch_shapes=[pltpu.SemaphoreType.DMA((4,))],
        compiler_params=pltpu.CompilerParams(vmem_limit_bytes=1024 * 1024),
    )(*results)
    return loss.reshape(()), grad_hidden, grad_weight, grad_bias


def solution(mesh):
    in_specs = (
        P("pass", None),
        P(None, ("vocab", "pass")),
        P(("vocab", "pass")),
        P(),
        P("pass", "vocab"),
        P(),
        P(None, ("vocab", "pass")),
    )
    out_specs = (P(), P("vocab", "pass"), P(None, ("vocab", "pass")), P(("vocab", "pass")))
    body = functools.partial(local, mesh.shape["vocab"] // NX, mesh.shape["pass"] // NC)
    return jax.shard_map(body, mesh=mesh, in_specs=in_specs, out_specs=out_specs, check_vma=False)
```

```python
import functools

import jax
import jax.numpy as jnp
from jax import lax
from jax.experimental import pallas as pl
from jax.experimental.pallas import tpu as pltpu
from jax.sharding import PartitionSpec as P

loss_scale = 4096.0
NX = 4
NC = 2
SLOT = 4
ROWS = 16
MAX_COPIES = 112
MESH = pl.DeviceIdType.MESH
f32 = jnp.float32
bf16 = jnp.bfloat16


def dot(a, b):
    return jnp.dot(a, b, preferred_element_type=f32)


def iota(shape, axis):
    return lax.broadcasted_iota(jnp.int32, shape, axis)


def near_last(size):
    return sorted(range(1, size), key=lambda d: -min(d, size - d))


def kernel(nz, ny, n_queries, hidden, weight, bias, tokens, passages, positive, selected,
           loss_o, gh_o, gw_o, gb_o,
           gath, gath_o, gath_t, w_v, wr, wr_t, pas, pas_t, perm, bias_v, bias_b, tokens_v, sel_v, selp, lenp,
           maxl, sell, maxa, sela, pool, pos_s, pos_r, sc_s, sc_x, zs, zr, fin, st_s, st, u_s, u_r, slope,
           sel_r, g_r, lh, lh_y, lh_o, gs, gs_r, s1, s1_r, high,
           zf, z2, z2_r, gw_v, send_sems, recv_sems, loc_sems, entry):
    n_pass = ny * NC
    v = lax.axis_index("vocab")
    p = lax.axis_index("pass")
    z, x = lax.div(v, NX), lax.rem(v, NX)
    y, c = lax.div(p, NC), lax.rem(p, NC)
    sib = 1 - c
    own_rows = gath.shape[1]
    d_model = gath.shape[2]
    voc = w_v.shape[1] // NC
    wide = NC * voc
    qlen = tokens_v.shape[1]
    per_block = n_queries // n_pass
    tok = ny * own_rows
    ro = (NC * tok) // (nz * NX)
    per_core = nz // 2
    z_block = nz // n_pass
    part = per_core * ro
    chip_cols = NC * 128
    tile = sc_s.shape[1]

    def around(value, shift, size):
        return lax.rem(value + (shift + size), size)

    def pass_index(dy, dc):
        return around(y, dy, ny) * NC + around(c, dc, NC)

    def pass_dev(dy, dc):
        return (v, pass_index(dy, dc))

    def x_dev(dx, dc=0):
        return (z * NX + around(x, dx, NX), pass_index(0, dc))

    def z_dev(dz):
        return (around(z, dz, nz) * NX + x, p)

    sibling = (v, y * NC + sib)
    x_peers = [(dx, dc) for dx in near_last(NX) + [0] for dc in range(NC) if dx or dc]
    y_far, x_far, z_far = near_last(ny), near_last(NX), near_last(nz)
    started = []

    def remote(src, dst, device):
        i = len(started)
        copy = pltpu.make_async_remote_copy(
            src_ref=src, dst_ref=dst, send_sem=send_sems.at[i], recv_sem=recv_sems.at[i],
            device_id=device, device_id_type=MESH,
        )
        copy.start()
        started.append(copy)
        return copy

    mine = pl.ds(pl.multiple_of(c * voc, 128), voc)
    theirs = pl.ds(pl.multiple_of(sib * voc, 128), voc)
    mine_pas = pl.ds(pl.multiple_of(c * 128, 128), 128)
    local = [pltpu.make_async_copy(bias, bias_v, loc_sems.at[0]),
             pltpu.make_async_copy(tokens, tokens_v, loc_sems.at[1]),
             pltpu.make_async_copy(selected, sel_v.at[c], loc_sems.at[2]),
             pltpu.make_async_copy(hidden, gath.at[y], loc_sems.at[3]),
             pltpu.make_async_copy(weight, w_v.at[:, mine], loc_sems.at[4])]
    for j in range(ny):
        local.append(pltpu.make_async_copy(
            passages.at[:, pl.ds(j * wide, wide)], pas.at[j, mine_pas], loc_sems.at[5 + j]))
    for copy in local:
        copy.start()

    barrier = pltpu.get_barrier_semaphore()
    passed_on = nz == 16
    z_near = (2, -2, 1, -1) if passed_on else z_far
    peers = ([z_dev(d) for d in z_near] + [pass_dev(d, 0) for d in y_far] + [x_dev(*d) for d in x_peers])
    for device in peers:
        pl.semaphore_signal(barrier, inc=1, device_id=device, device_id_type=MESH)
    pl.semaphore_wait(barrier, len(peers))

    hr = own_rows // 2
    top, bottom = pl.ds(0, hr), pl.ds(hr, hr)
    if ny == 4:
        pieces = [(pl.ds(i, 16), pl.ds(hr + i, 16)) for i in range(0, hr, 16)]
        first = []
        for a, b in pieces:
            first.append((remote(hidden.at[a], gath.at[y, a], pass_dev(1, 0)),
                          remote(hidden.at[b], gath.at[y, b], pass_dev(-1, 0))))
        then_up = remote(hidden.at[bottom], gath.at[y, bottom], pass_dev(1, 0))
        then_down = remote(hidden.at[top], gath.at[y, top], pass_dev(-1, 0))
    else:
        direct = [remote(hidden, gath.at[y], pass_dev(d, 0)) for d in y_far]
    if passed_on:
        pl.semaphore_signal(entry.at[0], inc=1, device_id=z_dev(2), device_id_type=MESH)
        pl.semaphore_signal(entry.at[1], inc=1, device_id=z_dev(-2), device_id_type=MESH)
    to_w = remote(weight, w_v.at[:, mine], sibling)
    for copy in local[:3]:
        copy.wait()
    bias_b[c] = jnp.broadcast_to(bias_v[...].reshape(1, voc), (8, voc))
    to_small = [remote(selected, sel_v.at[c], sibling), remote(bias_b.at[c], bias_b.at[c], sibling)]
    to_pas = [remote(passages.at[:, pl.ds(j * wide, wide)], pas.at[j, mine_pas], sibling) for j in range(ny)]

    if ny == 4:
        up, down, far = around(y, -1, ny), around(y, 1, ny), around(y, 2, ny)
        relayed = []
        for (a, b), (to_up, to_down) in zip(pieces, first):
            to_up.wait_recv()
            relayed.append(remote(gath.at[up, a], gath.at[up, a], pass_dev(1, 0)))
            to_down.wait_recv()
            relayed.append(remote(gath.at[down, b], gath.at[down, b], pass_dev(-1, 0)))
    if passed_on:
        pl.semaphore_wait(entry.at[0], 1)
        pl.semaphore_wait(entry.at[1], 1)
        pl.semaphore_signal(entry.at[2], inc=1, device_id=z_dev(4), device_id_type=MESH)
        pl.semaphore_signal(entry.at[3], inc=1, device_id=z_dev(-4), device_id_type=MESH)
    for ref in (maxl, sell, maxa, sela, selp, lenp, zf):
        ref[...] = jnp.zeros_like(ref)

    lengths = jnp.sum((tokens_v[...] != 1).astype(f32), axis=1, keepdims=True).astype(jnp.int32)
    lengths = jnp.broadcast_to(lengths, (n_queries, wide))
    for copy in to_small:
        copy.wait_recv()
    picks = jnp.concatenate([sel_v[0], sel_v[1]], axis=1)
    for j in range(ny):
        a = 2 * j * per_block
        b = a + per_block
        selp[j, 0:per_block, :] = jnp.where(c == 0, picks[a:b], picks[b:b + per_block])
        lenp[j, 0:per_block, :] = jnp.where(c == 0, lengths[a:b], lengths[b:b + per_block])

    def block(yy):
        logits = dot(gath[yy], w_v[...]).reshape(per_block, qlen, wide)
        at = iota((per_block, qlen, wide), 1)
        valid = at < lenp[yy][0:per_block].reshape(per_block, 1, wide)
        chosen = at == selp[yy][0:per_block].reshape(per_block, 1, wide)
        maxl[yy, 0:per_block, :] = jnp.max(jnp.where(valid, logits, -jnp.inf), axis=1)
        sell[yy, 0:per_block, :] = jnp.sum(jnp.where(chosen, logits, 0.0), axis=1)

    local[3].wait()
    local[4].wait()
    if ny == 4:
        to_w.wait_recv()
        block(y)
        then_up.wait_recv()
        block(up)
        then_down.wait_recv()
        block(down)
    else:
        to_w.wait_recv()
        block(y)
    for copy in local[5:]:
        copy.wait()
    for copy in to_pas:
        copy.wait_recv()
    for j in range(ny):
        pas_t[j] = pas[j].T
    if ny == 4:
        for copy in relayed:
            copy.wait_recv()
        block(far)
    else:
        for d, copy in zip(y_far, direct):
            copy.wait_recv()
            block(around(y, -d, ny))

    wide_bias = jnp.concatenate([bias_b[0], bias_b[1]], axis=1)[0:1]
    for j in range(ny):
        maxa[j * SLOT:(j + 1) * SLOT, :] = maxl[j, 0:SLOT, :]
    pool[y] = jnp.log1p(jax.nn.softplus(maxa[...] + wide_bias)).astype(bf16)
    to_pool = {d: remote(pool.at[y], pool.at[y], pass_dev(d, 0)) for d in y_far}
    row, lane = iota((ROWS, 256), 0), iota((ROWS, 256), 1)
    place = lax.bitwise_and(row, SLOT - 1)
    query = (lax.shift_right_logical(row, 2) * NC + c) * per_block + place
    query = jnp.where((place < per_block) & (row < ny * SLOT), query, -1)
    pos_col = jnp.zeros((ROWS, 256), jnp.int32)
    for q in range(n_queries):
        pos_col = jnp.where(query == q, positive[q], pos_col)
    is_pos = (lane + y * 256) == pos_col
    onehot = is_pos.astype(f32).astype(bf16)

    score = dot(pool[y], pas_t[y])
    for d in reversed(y_far):
        to_pool[d].wait_recv()
        there = around(y, -d, ny)
        score = score + dot(pool[there], pas_t[there])

    for j in range(NX):
        a, b = (j // 2) * tile, (j % 2) * 128
        sc_s[j] = score[a:a + tile, b:b + 128]
    to_x = [remote(sc_s.at[around(x, d, NX)], sc_x.at[d], x_dev(d)) for d in x_far]
    for j in range(ny):
        pos_s[j] = dot(onehot, pas[j]).astype(bf16)
    to_pos = [remote(pos_s.at[around(y, d, ny)], pos_r.at[d], pass_dev(d, 0)) for d in y_far]
    to_wr = {}
    for d in y_far:
        rows = pl.ds(pl.multiple_of(around(y, d, ny) * chip_cols, chip_cols), chip_cols)
        to_wr[d] = remote(w_v.at[rows, mine], wr.at[y, :, mine], pass_dev(d, 0))
    for j in range(ny):
        sel_r[y, j * SLOT:(j + 1) * SLOT, :] = selp[j, 0:SLOT, :]
    to_sel = [remote(sel_r.at[y], sel_r.at[y], pass_dev(d, 0)) for d in y_far]
    to_other = remote(gath, gath_o, sibling)
    total = sc_s[x]
    for copy in to_x:
        copy.wait_recv()
    for d in range(1, NX):
        total = total + sc_x[d]
    zs[...] = total
    if passed_on:
        pl.semaphore_wait(entry.at[2], 1)
        pl.semaphore_wait(entry.at[3], 1)
    to_z = [remote(zs, zr.at[d], z_dev(d)) for d in z_far]
    wr_t[y] = w_v[pl.ds(pl.multiple_of(y * chip_cols, chip_cols), chip_cols), :].T
    prow = iota((tok, 128), 0)
    chunk = jnp.floor((prow.astype(f32) + 0.5) * (1.0 / ro)).astype(jnp.int32)
    zl = lax.bitwise_and(chunk, per_core - 1)
    xx = lax.shift_right_logical(chunk, per_core.bit_length() - 1)
    natural = prow + ro * (zl * NX + xx - chunk)
    plane = iota((tok, 128), 1)
    for j in range(tok // 128):
        perm[:, j * 128:(j + 1) * 128] = (natural == plane + j * 128).astype(f32).astype(bf16)
    for j in range(ny):
        sela[j * SLOT:(j + 1) * SLOT, :] = sell[j, 0:SLOT, :]
    at_sel = sela[...] + wide_bias
    slope[...] = jax.nn.sigmoid(at_sel) / (1.0 + jax.nn.softplus(at_sel))
    gath_t[0] = gath[...].reshape(tok, d_model).T
    for copy in to_z:
        copy.wait_recv()
    for d in range(1, nz):
        total = total + zr[d]
    fin[x] = total
    to_fin = [remote(fin.at[x], fin.at[x], x_dev(d)) for d in x_far]
    to_wr_sib = []
    for d in reversed(y_far):
        to_wr[d].wait_recv()
        there = around(y, -d, ny)
        to_wr_sib.append(remote(wr.at[there, :, mine], wr.at[there, :, mine], sibling))
    for copy in to_pos:
        copy.wait_recv()
    pos_entries = pos_s[y].astype(f32)
    for d in range(1, ny):
        pos_entries = pos_entries + pos_r[d].astype(f32)
    for copy in to_fin:
        copy.wait_recv()

    score = jnp.concatenate([jnp.concatenate([fin[j], fin[j + 1]], axis=1) for j in range(0, NX, 2)], axis=0)
    peak = jnp.max(score, axis=1, keepdims=True)
    terms = jnp.exp(score - peak)
    other = jnp.where(is_pos, 0.0, terms)
    stats = [peak, jnp.sum(other, axis=1, keepdims=True),
             jnp.sum(jnp.where(is_pos, terms, 0.0), axis=1, keepdims=True),
             jnp.sum(jnp.where(is_pos, score, 0.0), axis=1, keepdims=True)]
    eye = iota((ROWS, 128), 0) == iota((ROWS, 128), 1)
    turned = [jnp.sum(jnp.where(eye, s, 0.0), axis=0, keepdims=True) for s in stats]
    st_s[...] = jnp.concatenate(turned + [jnp.zeros((8 - len(turned), 128), f32)], axis=0)
    other = other.astype(bf16)
    to_u = {}
    for d in y_far:
        there = around(y, d, ny)
        u_s[there] = dot(other, pas[there]).astype(bf16)
        to_u[d] = remote(u_s.at[there], u_r.at[d], pass_dev(d, 0))
    to_st = [remote(st_s, st.at[d], pass_dev(d, 0)) for d in y_far]
    st[0] = st_s[...]
    mine_u = dot(other, pas[y])
    for d, copy in zip(reversed(y_far), to_wr_sib):
        copy.wait_recv()
        there = around(y, -d, ny)
        wr_t[there] = wr[there].T
    for copy in to_st:
        copy.wait_recv()
    peaks = [st[i][0:1] for i in range(ny)]
    highest = functools.reduce(jnp.maximum, peaks)
    scale = [jnp.exp(k - highest) for k in peaks]
    rest = sum(scale[i] * st[i][1:2] for i in range(ny))
    denom = rest + sum(scale[i] * st[i][2:3] for i in range(ny))
    pos_score = sum(st[i][3:4] for i in range(ny))
    log_total = highest + jnp.log(denom)
    lane1 = iota((1, 128), 1)
    counted = (lax.bitwise_and(lane1, SLOT - 1) < per_block) & (lane1 < ny * SLOT)
    loss = jnp.sum(jnp.where(counted, log_total - pos_score, 0.0), axis=1, keepdims=True)
    factor = (loss_scale / n_queries) / denom

    def column(line):
        return jnp.sum(jnp.where(eye, line, 0.0), axis=1, keepdims=True)

    term = column(scale[0] * factor) * mine_u - column(rest * factor) * pos_entries
    for d in reversed(y_far):
        to_u[d].wait_recv()
        term = term + column(scale[d] * factor) * u_r[d].astype(f32)

    grad = term * slope[...]
    g_r[y] = grad.astype(bf16)
    to_g = {d: remote(g_r.at[y], g_r.at[y], pass_dev(d, 0)) for d in y_far}
    at = iota((per_block, qlen, wide), 1)

    def spread(yy, out):
        taken, picks = g_r[yy].astype(f32), sel_r[yy]
        for j in range(ny):
            some = taken[j * SLOT:j * SLOT + per_block].reshape(per_block, 1, wide)
            chosen = at == picks[j * SLOT:j * SLOT + per_block].reshape(per_block, 1, wide)
            out[j * own_rows:(j + 1) * own_rows, :] = jnp.where(chosen, some, 0.0).reshape(own_rows, wide).astype(bf16)

    spread(y, lh)
    to_lh = remote(lh.at[:, theirs], lh_o, sibling)

    out = dot(lh[...], wr_t[y])
    for copy in to_sel:
        copy.wait_recv()
    for d in reversed(y_far):
        to_g[d].wait_recv()
        there = around(y, -d, ny)
        spread(there, lh_y)
        out = out + dot(lh_y[...], wr_t[there])
    out = dot(perm[...], out.astype(bf16)).astype(bf16)
    for k in range(NC):
        for j in range(NX):
            s1[k, j] = out[j * part:(j + 1) * part, k * 128:(k + 1) * 128]
    to_s1 = [remote(s1.at[around(c, dc, NC), around(x, dx, NX)], s1_r.at[dx * NC + dc], x_dev(dx, dc))
             for dx, dc in x_peers]

    at_row = iota((ROWS, wide), 0)
    real = (lax.bitwise_and(at_row, SLOT - 1) < per_block) & (at_row < ny * SLOT)
    summed = jnp.sum(jnp.where(real, grad, 0.0), axis=0, keepdims=True)
    first = iota((8, voc), 0) == 0
    for j in range(NC):
        gs[j] = jnp.where(first, summed[:, j * voc:(j + 1) * voc], loss)
    to_gs = remote(gs.at[sib], gs_r, sibling)
    to_other.wait_recv()
    gath_t[1] = gath_o[...].reshape(tok, d_model).T
    gw_v[...] = dot(gath_t[0], lh[:, mine])

    for copy in to_s1:
        copy.wait_recv()
    same, cross = s1[c, x].astype(f32), s1_r[1].astype(f32)
    for d in range(1, NX):
        same = same + s1_r[d * NC].astype(f32)
        cross = cross + s1_r[d * NC + 1].astype(f32)
    high[c] = same
    high[sib] = cross
    for core in range(NC):
        for k in range(per_core):
            to_row = (NC * (k // z_block) + core) * z_block + k % z_block
            zf[to_row, 0:ro, :] = high[core, k * ro:(k + 1) * ro]
    z2[...] = zf[...].astype(bf16)
    to_z2 = [remote(z2.at[around(z, d, nz)], z2_r.at[d], z_dev(d)) for d in z_far]
    for copy in started[:-len(to_z2)]:
        copy.wait_send()
    to_lh.wait_recv()
    gw_v[...] += dot(gath_t[1], lh_o[...])
    gw_out = pltpu.make_async_copy(gw_v, gw_o, loc_sems.at[0])
    gw_out.start()
    to_gs.wait_recv()
    gb_o[...] = (gs[c][0:1] + gs_r[0:1]).reshape(voc)
    loss_o[...] = (gs[c][1:2, 0:1] + gs_r[1:2, 0:1]) * (1.0 / n_queries)
    total = zf[z]
    for copy in to_z2:
        copy.wait_recv()
    for d in range(1, nz):
        total = total + z2_r[d].astype(f32)
    gh_o[...] = total[0:ro].astype(bf16)

    for copy in to_z2:
        copy.wait_send()
    gw_out.wait()


def hand_out(*refs):
    sems = refs[8]
    copies = [pltpu.make_async_copy(refs[i], refs[4 + i], sems.at[i]) for i in range(4)]
    for copy in copies:
        copy.start()
    for copy in copies:
        copy.wait()


def local(nz, ny, hidden, weight, bias, token_ids, passages, positive, selected):
    n_queries, qlen = token_ids.shape
    own_rows, d = hidden.shape
    voc = weight.shape[1]
    wide = NC * voc
    tok = ny * own_rows
    ro = (NC * tok) // (nz * NX)
    rp = -(-ro // 16) * 16
    part = (nz // 2) * ro
    tile = ROWS * 2 // NX
    i32 = jnp.int32
    vmem = pl.BlockSpec(memory_space=pltpu.VMEM)
    smem = pl.BlockSpec(memory_space=pltpu.SMEM)
    anywhere = pl.BlockSpec(memory_space=pl.ANY)
    hbm = pl.BlockSpec(memory_space=pltpu.HBM)
    scratch = [
        ((ny, own_rows, d), bf16), ((ny, own_rows, d), bf16), ((NC, d, tok), bf16),
        ((d, wide), bf16), ((ny, NC * 128, wide), bf16), ((ny, wide, NC * 128), bf16),
        ((ny, NC * 128, wide), bf16), ((ny, wide, NC * 128), bf16), ((tok, tok), bf16),
        ((voc,), f32), ((NC, 8, voc), f32), ((n_queries, qlen), i32), ((NC, n_queries, voc), i32),
        ((ny, 8, wide), i32), ((ny, 8, wide), i32),
        ((ny, 8, wide), f32), ((ny, 8, wide), f32), ((ROWS, wide), f32), ((ROWS, wide), f32),
        ((ny, ROWS, wide), bf16), ((ny, ROWS, wide), bf16), ((ny, ROWS, wide), bf16),
        ((NX, tile, 128), f32), ((NX, tile, 128), f32), ((tile, 128), f32), ((nz, tile, 128), f32),
        ((NX, tile, 128), f32), ((8, 128), f32), ((ny, 8, 128), f32),
        ((ny, ROWS, wide), bf16), ((ny, ROWS, wide), bf16), ((ROWS, wide), f32),
        ((ny, ROWS, wide), i32), ((ny, ROWS, wide), bf16),
        ((tok, wide), bf16), ((tok, wide), bf16), ((tok, voc), bf16),
        ((NC, 8, voc), f32), ((8, voc), f32),
        ((NC, NX, part, 128), bf16), ((NX * NC, part, 128), bf16), ((NC, part, 128), f32),
        ((nz, rp, 128), f32), ((nz, rp, 128), bf16), ((nz, rp, 128), bf16), ((d, voc), f32),
    ]
    results = pl.pallas_call(
        functools.partial(kernel, nz, ny, n_queries),
        out_shape=(
            jax.ShapeDtypeStruct((1, 1), f32),
            jax.ShapeDtypeStruct((ro, 128), bf16),
            jax.ShapeDtypeStruct((d, voc), f32),
            jax.ShapeDtypeStruct((voc,), f32),
        ),
        in_specs=[hbm, hbm, hbm, hbm, hbm, smem, hbm],
        out_specs=(vmem, vmem, anywhere, vmem),
        scratch_shapes=[pltpu.VMEM(s, t) for s, t in scratch] + [
            pltpu.SemaphoreType.DMA((MAX_COPIES,)),
            pltpu.SemaphoreType.DMA((MAX_COPIES,)),
            pltpu.SemaphoreType.DMA((5 + ny,)),
            pltpu.SemaphoreType.REGULAR((4,)),
        ],
        compiler_params=pltpu.CompilerParams(
            collective_id=0, has_side_effects=True, vmem_limit_bytes=48 * 1024 * 1024
        ),
    )(*(pltpu.with_memory_space_constraint(a, pltpu.HBM)
        for a in (hidden, weight, bias, token_ids, passages, positive, selected)))
    loss, grad_hidden, grad_weight, grad_bias = pl.pallas_call(
        hand_out,
        out_shape=tuple(jax.ShapeDtypeStruct(r.shape, r.dtype) for r in results),
        in_specs=[anywhere] * 4,
        out_specs=(hbm,) * 4,
        scratch_shapes=[pltpu.SemaphoreType.DMA((4,))],
        compiler_params=pltpu.CompilerParams(vmem_limit_bytes=1024 * 1024),
    )(*results)
    return loss.reshape(()), grad_hidden, grad_weight, grad_bias


def solution(mesh):
    in_specs = (
        P("pass", None),
        P(None, ("vocab", "pass")),
        P(("vocab", "pass")),
        P(),
        P("pass", "vocab"),
        P(),
        P(None, ("vocab", "pass")),
    )
    out_specs = (P(), P("vocab", "pass"), P(None, ("vocab", "pass")), P(("vocab", "pass")))
    body = functools.partial(local, mesh.shape["vocab"] // NX, mesh.shape["pass"] // NC)
    return jax.shard_map(body, mesh=mesh, in_specs=in_specs, out_specs=out_specs, check_vma=False)
```

```python
import functools

import jax
import jax.numpy as jnp
from jax import lax
from jax.experimental import pallas as pl
from jax.experimental.pallas import tpu as pltpu
from jax.sharding import PartitionSpec as P

loss_scale = 4096.0
NX = 4
NC = 2
SLOT = 4
ROWS = 16
MAX_SEMS = 37
MESH = pl.DeviceIdType.MESH
f32 = jnp.float32
bf16 = jnp.bfloat16


def dot(a, b):
    return jnp.dot(a, b, preferred_element_type=f32)


def iota(shape, axis):
    return lax.broadcasted_iota(jnp.int32, shape, axis)


def near_last(size):
    return sorted(range(1, size), key=lambda d: -min(d, size - d))


def kernel(nz, ny, n_queries, hidden, weight, bias, tokens, passages, positive_h, selected,
           loss_o, gh_o, gw_o, gb_o,
           gath, gath_o, gath_t, w_v, wr, wr_t, pas, pas_t, perm, bias_v, bias_b, positive, tokens_v, sel_v, selp, lenp,
           maxl, sell, maxa, sela, pool, pos_s, pos_r, sc_s, sc_x, zs, zr, fin, st_s, st, u_s, u_r, slope,
           sel_r, g_r, lh, lh_y, lh_o, gs, gs_r, s1, s1_r, high,
           zf, z2, z2_r, gw_v, send_sems, recv_sems, loc_sems, entry):
    n_pass = ny * NC
    v = lax.axis_index("vocab")
    p = lax.axis_index("pass")
    z, x = lax.div(v, NX), lax.rem(v, NX)
    y, c = lax.div(p, NC), lax.rem(p, NC)
    sib = 1 - c
    own_rows = gath.shape[1]
    d_model = gath.shape[2]
    voc = w_v.shape[1] // NC
    wide = NC * voc
    qlen = tokens_v.shape[1]
    per_block = n_queries // n_pass
    tok = ny * own_rows
    ro = (NC * tok) // (nz * NX)
    per_core = nz // 2
    z_block = nz // n_pass
    part = per_core * ro
    chip_cols = NC * 128
    tile = sc_s.shape[1]

    def around(value, shift, size):
        return lax.rem(value + (shift + size), size)

    def pass_index(dy, dc):
        return around(y, dy, ny) * NC + around(c, dc, NC)

    def pass_dev(dy, dc):
        return (v, pass_index(dy, dc))

    def x_dev(dx, dc=0):
        return (z * NX + around(x, dx, NX), pass_index(0, dc))

    def z_dev(dz):
        return (around(z, dz, nz) * NX + x, p)

    sibling = (v, y * NC + sib)
    x_peers = [(dx, dc) for dx in near_last(NX) + [0] for dc in range(NC) if dx or dc]
    y_far, x_far, z_far = near_last(ny), near_last(NX), near_last(nz)
    started, taken_sems = [], []

    def take():
        taken_sems.append(0)
        return len(taken_sems) - 1

    def describe(src, dst, device, i):
        return pltpu.make_async_remote_copy(
            src_ref=src, dst_ref=dst, send_sem=send_sems.at[i], recv_sem=recv_sems.at[i],
            device_id=device, device_id_type=MESH,
        )

    def remote(src, dst, device, i=None):
        copy = describe(src, dst, device, take() if i is None else i)
        copy.start()
        if i is None:
            started.append(copy)
        return copy

    def together(i, ref):
        whole = describe(ref, ref, sibling, i)
        started.append(whole)
        return whole

    def remotes(copies, ref):
        i = take()
        for src, dst, device in copies:
            remote(src, dst, device, i)
        return together(i, ref)

    mine = pl.ds(pl.multiple_of(c * voc, 128), voc)
    theirs = pl.ds(pl.multiple_of(sib * voc, 128), voc)
    mine_pas = pl.ds(pl.multiple_of(c * 128, 128), 128)
    local = [pltpu.make_async_copy(bias, bias_v, loc_sems.at[0]),
             pltpu.make_async_copy(tokens, tokens_v, loc_sems.at[1]),
             pltpu.make_async_copy(selected, sel_v.at[c], loc_sems.at[2]),
             pltpu.make_async_copy(hidden, gath.at[y], loc_sems.at[3]),
             pltpu.make_async_copy(weight, w_v.at[:, mine], loc_sems.at[4])]
    for j in range(ny):
        local.append(pltpu.make_async_copy(
            passages.at[:, pl.ds(j * wide, wide)], pas.at[j, mine_pas], loc_sems.at[5 + j]))
    local.append(pltpu.make_async_copy(positive_h, positive, loc_sems.at[5 + ny]))
    for copy in local:
        copy.start()

    barrier = pltpu.get_barrier_semaphore()
    passed_on = nz == 16
    z_near = (2, -2, 1, -1) if passed_on else z_far
    peers = ([z_dev(d) for d in z_near] + [pass_dev(d, 0) for d in y_far] + [x_dev(*d) for d in x_peers])
    for device in peers:
        pl.semaphore_signal(barrier, inc=1, device_id=device, device_id_type=MESH)
    pl.semaphore_wait(barrier, len(peers))

    hr = own_rows // 2
    top, bottom = pl.ds(0, hr), pl.ds(hr, hr)
    if ny == 4:
        pieces = [(pl.ds(i, 16), pl.ds(hr + i, 16)) for i in range(0, hr, 16)]
        first = []
        for a, b in pieces:
            first.append((remote(hidden.at[a], gath.at[y, a], pass_dev(1, 0)),
                          remote(hidden.at[b], gath.at[y, b], pass_dev(-1, 0))))
        then_up = remote(hidden.at[bottom], gath.at[y, bottom], pass_dev(1, 0))
        then_down = remote(hidden.at[top], gath.at[y, top], pass_dev(-1, 0))
    else:
        direct = [remote(hidden, gath.at[y], pass_dev(d, 0)) for d in y_far]
    if passed_on:
        pl.semaphore_signal(entry.at[0], inc=1, device_id=z_dev(2), device_id_type=MESH)
        pl.semaphore_signal(entry.at[1], inc=1, device_id=z_dev(-2), device_id_type=MESH)
    to_w = remote(weight, w_v.at[:, mine], sibling)
    for copy in local[:3]:
        copy.wait()
    bias_b[c] = jnp.broadcast_to(bias_v[...].reshape(1, voc), (8, voc))
    to_small = [remote(selected, sel_v.at[c], sibling), remote(bias_b.at[c], bias_b.at[c], sibling)]
    to_pas = remotes([(passages.at[:, pl.ds(j * wide, wide)], pas.at[j, mine_pas], sibling) for j in range(ny)],
                     pas.at[pl.ds(0, ny // 2)])

    if ny == 4:
        up, down, far = around(y, -1, ny), around(y, 1, ny), around(y, 2, ny)
        i = take()
        for (a, b), (to_up, to_down) in zip(pieces, first):
            to_up.wait_recv()
            remote(gath.at[up, a], gath.at[up, a], pass_dev(1, 0), i)
            to_down.wait_recv()
            remote(gath.at[down, b], gath.at[down, b], pass_dev(-1, 0), i)
        relayed = together(i, gath.at[far])
    if passed_on:
        pl.semaphore_wait(entry.at[0], 1)
        pl.semaphore_wait(entry.at[1], 1)
        pl.semaphore_signal(entry.at[2], inc=1, device_id=z_dev(4), device_id_type=MESH)
        pl.semaphore_signal(entry.at[3], inc=1, device_id=z_dev(-4), device_id_type=MESH)
    for ref in (maxl, sell, maxa, sela, selp, lenp, zf):
        ref[...] = jnp.zeros_like(ref)

    lengths = jnp.sum((tokens_v[...] != 1).astype(f32), axis=1, keepdims=True).astype(jnp.int32)
    lengths = jnp.broadcast_to(lengths, (n_queries, wide))
    for copy in to_small:
        copy.wait_recv()
    picks = jnp.concatenate([sel_v[0], sel_v[1]], axis=1)
    for j in range(ny):
        a = 2 * j * per_block
        b = a + per_block
        selp[j, 0:per_block, :] = jnp.where(c == 0, picks[a:b], picks[b:b + per_block])
        lenp[j, 0:per_block, :] = jnp.where(c == 0, lengths[a:b], lengths[b:b + per_block])

    def block(yy):
        logits = dot(gath[yy], w_v[...]).reshape(per_block, qlen, wide)
        at = iota((per_block, qlen, wide), 1)
        valid = at < lenp[yy][0:per_block].reshape(per_block, 1, wide)
        chosen = at == selp[yy][0:per_block].reshape(per_block, 1, wide)
        maxl[yy, 0:per_block, :] = jnp.max(jnp.where(valid, logits, -jnp.inf), axis=1)
        sell[yy, 0:per_block, :] = jnp.sum(jnp.where(chosen, logits, 0.0), axis=1)

    local[3].wait()
    local[4].wait()
    if ny == 4:
        to_w.wait_recv()
        block(y)
        then_up.wait_recv()
        block(up)
        then_down.wait_recv()
        block(down)
    else:
        to_w.wait_recv()
        block(y)
    for copy in local[5:]:
        copy.wait()
    to_pas.wait_recv()
    for j in range(ny):
        pas_t[j] = pas[j].T
    if ny == 4:
        relayed.wait_recv()
        block(far)
    else:
        for d, copy in zip(y_far, direct):
            copy.wait_recv()
            block(around(y, -d, ny))

    wide_bias = jnp.concatenate([bias_b[0], bias_b[1]], axis=1)[0:1]
    for j in range(ny):
        maxa[j * SLOT:(j + 1) * SLOT, :] = maxl[j, 0:SLOT, :]
    pool[y] = jnp.log1p(jax.nn.softplus(maxa[...] + wide_bias)).astype(bf16)
    to_pool = {d: remote(pool.at[y], pool.at[y], pass_dev(d, 0)) for d in y_far}
    row, lane = iota((ROWS, 256), 0), iota((ROWS, 256), 1)
    place = lax.bitwise_and(row, SLOT - 1)
    query = (lax.shift_right_logical(row, 2) * NC + c) * per_block + place
    query = jnp.where((place < per_block) & (row < ny * SLOT), query, -1)
    pos_col = jnp.zeros((ROWS, 256), jnp.int32)
    for q in range(n_queries):
        pos_col = jnp.where(query == q, positive[q], pos_col)
    is_pos = (lane + y * 256) == pos_col
    onehot = is_pos.astype(f32).astype(bf16)

    score = dot(pool[y], pas_t[y])
    for d in reversed(y_far):
        to_pool[d].wait_recv()
        there = around(y, -d, ny)
        score = score + dot(pool[there], pas_t[there])

    for j in range(NX):
        a, b = (j // 2) * tile, (j % 2) * 128
        sc_s[j] = score[a:a + tile, b:b + 128]
    to_x = remotes([(sc_s.at[around(x, d, NX)], sc_x.at[d], x_dev(d)) for d in x_far], sc_x.at[pl.ds(1, NX - 1)])
    for j in range(ny):
        pos_s[j] = dot(onehot, pas[j]).astype(bf16)
    to_pos = remotes([(pos_s.at[around(y, d, ny)], pos_r.at[d], pass_dev(d, 0)) for d in y_far],
                     pos_r.at[pl.ds(1, ny - 1)])
    to_wr = {}
    for d in y_far:
        rows = pl.ds(pl.multiple_of(around(y, d, ny) * chip_cols, chip_cols), chip_cols)
        to_wr[d] = remote(w_v.at[rows, mine], wr.at[y, :, mine], pass_dev(d, 0))
    for j in range(ny):
        sel_r[y, j * SLOT:(j + 1) * SLOT, :] = selp[j, 0:SLOT, :]
    to_sel = remotes([(sel_r.at[y], sel_r.at[y], pass_dev(d, 0)) for d in y_far], sel_r.at[pl.ds(0, ny - 1)])
    to_other = remote(gath, gath_o, sibling)
    total = sc_s[x]
    to_x.wait_recv()
    for d in range(1, NX):
        total = total + sc_x[d]
    zs[...] = total
    if passed_on:
        pl.semaphore_wait(entry.at[2], 1)
        pl.semaphore_wait(entry.at[3], 1)
    to_z = remotes([(zs, zr.at[d], z_dev(d)) for d in z_far], zr.at[pl.ds(1, nz - 1)])
    wr_t[y] = w_v[pl.ds(pl.multiple_of(y * chip_cols, chip_cols), chip_cols), :].T
    prow = iota((tok, 128), 0)
    chunk = jnp.floor((prow.astype(f32) + 0.5) * (1.0 / ro)).astype(jnp.int32)
    zl = lax.bitwise_and(chunk, per_core - 1)
    xx = lax.shift_right_logical(chunk, per_core.bit_length() - 1)
    natural = prow + ro * (zl * NX + xx - chunk)
    plane = iota((tok, 128), 1)
    for j in range(tok // 128):
        perm[:, j * 128:(j + 1) * 128] = (natural == plane + j * 128).astype(f32).astype(bf16)
    for j in range(ny):
        sela[j * SLOT:(j + 1) * SLOT, :] = sell[j, 0:SLOT, :]
    at_sel = sela[...] + wide_bias
    slope[...] = jax.nn.sigmoid(at_sel) / (1.0 + jax.nn.softplus(at_sel))
    gath_t[0] = gath[...].reshape(tok, d_model).T
    to_z.wait_recv()
    for d in range(1, nz):
        total = total + zr[d]
    fin[x] = total
    to_fin = remotes([(fin.at[x], fin.at[x], x_dev(d)) for d in x_far], fin.at[pl.ds(0, NX - 1)])
    i = take()
    for d in reversed(y_far):
        to_wr[d].wait_recv()
        there = around(y, -d, ny)
        remote(wr.at[there, :, mine], wr.at[there, :, mine], sibling, i)
    to_wr_sib = together(i, wr.at[pl.ds(0, ny - 1), :, mine])
    to_pos.wait_recv()
    pos_entries = pos_s[y].astype(f32)
    for d in range(1, ny):
        pos_entries = pos_entries + pos_r[d].astype(f32)
    to_fin.wait_recv()

    score = jnp.concatenate([jnp.concatenate([fin[j], fin[j + 1]], axis=1) for j in range(0, NX, 2)], axis=0)
    peak = jnp.max(score, axis=1, keepdims=True)
    terms = jnp.exp(score - peak)
    other = jnp.where(is_pos, 0.0, terms)
    stats = [peak, jnp.sum(other, axis=1, keepdims=True),
             jnp.sum(jnp.where(is_pos, terms, 0.0), axis=1, keepdims=True),
             jnp.sum(jnp.where(is_pos, score, 0.0), axis=1, keepdims=True)]
    eye = iota((ROWS, 128), 0) == iota((ROWS, 128), 1)
    turned = [jnp.sum(jnp.where(eye, s, 0.0), axis=0, keepdims=True) for s in stats]
    st_s[...] = jnp.concatenate(turned + [jnp.zeros((8 - len(turned), 128), f32)], axis=0)
    other = other.astype(bf16)
    to_u = {}
    for d in y_far:
        there = around(y, d, ny)
        u_s[there] = dot(other, pas[there]).astype(bf16)
        to_u[d] = remote(u_s.at[there], u_r.at[d], pass_dev(d, 0))
    to_st = remotes([(st_s, st.at[d], pass_dev(d, 0)) for d in y_far], st.at[pl.ds(1, ny - 1)])
    st[0] = st_s[...]
    mine_u = dot(other, pas[y])
    to_wr_sib.wait_recv()
    for d in y_far:
        there = around(y, -d, ny)
        wr_t[there] = wr[there].T
    to_st.wait_recv()
    peaks = [st[i][0:1] for i in range(ny)]
    highest = functools.reduce(jnp.maximum, peaks)
    scale = [jnp.exp(k - highest) for k in peaks]
    rest = sum(scale[i] * st[i][1:2] for i in range(ny))
    denom = rest + sum(scale[i] * st[i][2:3] for i in range(ny))
    pos_score = sum(st[i][3:4] for i in range(ny))
    log_total = highest + jnp.log(denom)
    lane1 = iota((1, 128), 1)
    counted = (lax.bitwise_and(lane1, SLOT - 1) < per_block) & (lane1 < ny * SLOT)
    loss = jnp.sum(jnp.where(counted, log_total - pos_score, 0.0), axis=1, keepdims=True)
    factor = (loss_scale / n_queries) / denom

    def column(line):
        return jnp.sum(jnp.where(eye, line, 0.0), axis=1, keepdims=True)

    term = column(scale[0] * factor) * mine_u - column(rest * factor) * pos_entries
    for d in reversed(y_far):
        to_u[d].wait_recv()
        term = term + column(scale[d] * factor) * u_r[d].astype(f32)

    grad = term * slope[...]
    g_r[y] = grad.astype(bf16)
    to_g = {d: remote(g_r.at[y], g_r.at[y], pass_dev(d, 0)) for d in y_far}
    at = iota((per_block, qlen, wide), 1)

    def spread(yy, out):
        taken, picks = g_r[yy].astype(f32), sel_r[yy]
        for j in range(ny):
            some = taken[j * SLOT:j * SLOT + per_block].reshape(per_block, 1, wide)
            chosen = at == picks[j * SLOT:j * SLOT + per_block].reshape(per_block, 1, wide)
            out[j * own_rows:(j + 1) * own_rows, :] = jnp.where(chosen, some, 0.0).reshape(own_rows, wide).astype(bf16)

    spread(y, lh)
    to_lh = remote(lh.at[:, theirs], lh_o, sibling)

    out = dot(lh[...], wr_t[y])
    to_sel.wait_recv()
    for d in reversed(y_far):
        to_g[d].wait_recv()
        there = around(y, -d, ny)
        spread(there, lh_y)
        out = out + dot(lh_y[...], wr_t[there])
    out = dot(perm[...], out.astype(bf16)).astype(bf16)
    for k in range(NC):
        for j in range(NX):
            s1[k, j] = out[j * part:(j + 1) * part, k * 128:(k + 1) * 128]
    to_s1 = remotes([(s1.at[around(c, dc, NC), around(x, dx, NX)], s1_r.at[dx * NC + dc], x_dev(dx, dc))
                     for dx, dc in x_peers], s1_r.at[pl.ds(1, NX * NC - 1)])

    at_row = iota((ROWS, wide), 0)
    real = (lax.bitwise_and(at_row, SLOT - 1) < per_block) & (at_row < ny * SLOT)
    summed = jnp.sum(jnp.where(real, grad, 0.0), axis=0, keepdims=True)
    first = iota((8, voc), 0) == 0
    for j in range(NC):
        gs[j] = jnp.where(first, summed[:, j * voc:(j + 1) * voc], loss)
    to_gs = remote(gs.at[sib], gs_r, sibling)
    to_other.wait_recv()
    gath_t[1] = gath_o[...].reshape(tok, d_model).T
    gw_v[...] = dot(gath_t[0], lh[:, mine])

    to_s1.wait_recv()
    same, cross = s1[c, x].astype(f32), s1_r[1].astype(f32)
    for d in range(1, NX):
        same = same + s1_r[d * NC].astype(f32)
        cross = cross + s1_r[d * NC + 1].astype(f32)
    high[c] = same
    high[sib] = cross
    for core in range(NC):
        for k in range(per_core):
            to_row = (NC * (k // z_block) + core) * z_block + k % z_block
            zf[to_row, 0:ro, :] = high[core, k * ro:(k + 1) * ro]
    z2[...] = zf[...].astype(bf16)
    to_z2 = remotes([(z2.at[around(z, d, nz)], z2_r.at[d], z_dev(d)) for d in z_far], z2_r.at[pl.ds(1, nz - 1)])
    for copy in started[:-1]:
        copy.wait_send()
    to_lh.wait_recv()
    gw_v[...] += dot(gath_t[1], lh_o[...])
    gw_out = pltpu.make_async_copy(gw_v, gw_o, loc_sems.at[0])
    gw_out.start()
    to_gs.wait_recv()
    gb_o[...] = (gs[c][0:1] + gs_r[0:1]).reshape(voc)
    loss_o[...] = (gs[c][1:2, 0:1] + gs_r[1:2, 0:1]) * (1.0 / n_queries)
    total = zf[z]
    to_z2.wait_recv()
    for d in range(1, nz):
        total = total + z2_r[d].astype(f32)
    gh_o[...] = total[0:ro].astype(bf16)

    to_z2.wait_send()
    gw_out.wait()


def hand_out(*refs):
    sems = refs[8]
    pairs = [(refs[i], refs[4 + i]) for i in (0, 1, 3)]
    rows = refs[2].shape[0] // 4
    pairs += [(refs[2].at[pl.ds(i * rows, rows)], refs[6].at[pl.ds(i * rows, rows)]) for i in range(4)]
    copies = [pltpu.make_async_copy(a, b, sems.at[i]) for i, (a, b) in enumerate(pairs)]
    for copy in reversed(copies):
        copy.start()
    for copy in copies:
        copy.wait()


def local(nz, ny, hidden, weight, bias, token_ids, passages, positive, selected):
    n_queries, qlen = token_ids.shape
    own_rows, d = hidden.shape
    voc = weight.shape[1]
    wide = NC * voc
    tok = ny * own_rows
    ro = (NC * tok) // (nz * NX)
    rp = -(-ro // 16) * 16
    part = (nz // 2) * ro
    tile = ROWS * 2 // NX
    i32 = jnp.int32
    vmem = pl.BlockSpec(memory_space=pltpu.VMEM)
    anywhere = pl.BlockSpec(memory_space=pl.ANY)
    hbm = pl.BlockSpec(memory_space=pltpu.HBM)
    scratch = [
        ((ny, own_rows, d), bf16), ((ny, own_rows, d), bf16), ((NC, d, tok), bf16),
        ((d, wide), bf16), ((ny, NC * 128, wide), bf16), ((ny, wide, NC * 128), bf16),
        ((ny, NC * 128, wide), bf16), ((ny, wide, NC * 128), bf16), ((tok, tok), bf16),
        ((voc,), f32), ((NC, 8, voc), f32), None, ((n_queries, qlen), i32), ((NC, n_queries, voc), i32),
        ((ny, 8, wide), i32), ((ny, 8, wide), i32),
        ((ny, 8, wide), f32), ((ny, 8, wide), f32), ((ROWS, wide), f32), ((ROWS, wide), f32),
        ((ny, ROWS, wide), bf16), ((ny, ROWS, wide), bf16), ((ny, ROWS, wide), bf16),
        ((NX, tile, 128), f32), ((NX, tile, 128), f32), ((tile, 128), f32), ((nz, tile, 128), f32),
        ((NX, tile, 128), f32), ((8, 128), f32), ((ny, 8, 128), f32),
        ((ny, ROWS, wide), bf16), ((ny, ROWS, wide), bf16), ((ROWS, wide), f32),
        ((ny, ROWS, wide), i32), ((ny, ROWS, wide), bf16),
        ((tok, wide), bf16), ((tok, wide), bf16), ((tok, voc), bf16),
        ((NC, 8, voc), f32), ((8, voc), f32),
        ((NC, NX, part, 128), bf16), ((NX * NC, part, 128), bf16), ((NC, part, 128), f32),
        ((nz, rp, 128), f32), ((nz, rp, 128), bf16), ((nz, rp, 128), bf16), ((d, voc), f32),
    ]
    results = pl.pallas_call(
        functools.partial(kernel, nz, ny, n_queries),
        out_shape=(
            jax.ShapeDtypeStruct((1, 1), f32),
            jax.ShapeDtypeStruct((ro, 128), bf16),
            jax.ShapeDtypeStruct((d, voc), f32),
            jax.ShapeDtypeStruct((voc,), f32),
        ),
        in_specs=[hbm] * 7,
        out_specs=(vmem, vmem, anywhere, vmem),
        scratch_shapes=[pltpu.VMEM(*k) if k else pltpu.SMEM((n_queries,), i32) for k in scratch] + [
            pltpu.SemaphoreType.DMA((MAX_SEMS,)),
            pltpu.SemaphoreType.DMA((MAX_SEMS,)),
            pltpu.SemaphoreType.DMA((6 + ny,)),
            pltpu.SemaphoreType.REGULAR((4,)),
        ],
        compiler_params=pltpu.CompilerParams(
            collective_id=0, has_side_effects=True, vmem_limit_bytes=48 * 1024 * 1024
        ),
    )(*(pltpu.with_memory_space_constraint(a, pltpu.HBM)
        for a in (hidden, weight, bias, token_ids, passages, positive, selected)))
    loss, grad_hidden, grad_weight, grad_bias = pl.pallas_call(
        hand_out,
        out_shape=tuple(jax.ShapeDtypeStruct(r.shape, r.dtype) for r in results),
        in_specs=[anywhere] * 4,
        out_specs=(hbm,) * 4,
        scratch_shapes=[pltpu.SemaphoreType.DMA((7,))],
        compiler_params=pltpu.CompilerParams(vmem_limit_bytes=1024 * 1024),
    )(*results)
    return loss.reshape(()), grad_hidden, grad_weight, grad_bias


def solution(mesh):
    in_specs = (
        P("pass", None),
        P(None, ("vocab", "pass")),
        P(("vocab", "pass")),
        P(),
        P("pass", "vocab"),
        P(),
        P(None, ("vocab", "pass")),
    )
    out_specs = (P(), P("vocab", "pass"), P(None, ("vocab", "pass")), P(("vocab", "pass")))
    body = functools.partial(local, mesh.shape["vocab"] // NX, mesh.shape["pass"] // NC)
    return jax.shard_map(body, mesh=mesh, in_specs=in_specs, out_specs=out_specs, check_vma=False)
```

```python
import functools

import jax
import jax.numpy as jnp
from jax import lax
from jax.experimental import pallas as pl
from jax.experimental.pallas import tpu as pltpu
from jax.sharding import PartitionSpec as P

loss_scale = 4096.0
NX = 4
NC = 2
SLOT = 4
ROWS = 16
MAX_SEMS = 40
MESH = pl.DeviceIdType.MESH
f32 = jnp.float32
bf16 = jnp.bfloat16


def dot(a, b):
    return jnp.dot(a, b, preferred_element_type=f32)


def iota(shape, axis):
    return lax.broadcasted_iota(jnp.int32, shape, axis)


def near_last(size):
    return sorted(range(1, size), key=lambda d: -min(d, size - d))


def kernel(nz, ny, n_queries, hidden, weight, bias, tokens, passages, positive_h, selected,
           loss_o, gh_o, gw_o, gb_o,
           gath, gath_o, gath_t, w_v, wr, wr_t, pas, pas_t, perm, bias_v, bias_b, positive, tokens_v, sel_v, selp, lenp,
           maxl, sell, maxa, sela, pool, pos_s, pos_r, sc_s, sc_x, zs, zr, fin, st_s, st, u_s, u_r, slope,
           sel_r, g_r, lh, lh_y, lh_o, gs, gs_r, s1, s1_r, high,
           zf, z2, z2_r, gw_v, send_sems, recv_sems, loc_sems, entry):
    n_pass = ny * NC
    v = lax.axis_index("vocab")
    p = lax.axis_index("pass")
    z, x = lax.div(v, NX), lax.rem(v, NX)
    y, c = lax.div(p, NC), lax.rem(p, NC)
    sib = 1 - c
    own_rows = gath.shape[1]
    d_model = gath.shape[2]
    voc = w_v.shape[1] // NC
    wide = NC * voc
    qlen = tokens_v.shape[1]
    per_block = n_queries // n_pass
    tok = ny * own_rows
    ro = (NC * tok) // (nz * NX)
    per_core = nz // 2
    z_block = nz // n_pass
    part = per_core * ro
    chip_cols = NC * 128
    tile = sc_s.shape[1]

    def around(value, shift, size):
        return lax.rem(value + (shift + size), size)

    def pass_index(dy, dc):
        return around(y, dy, ny) * NC + around(c, dc, NC)

    def pass_dev(dy, dc):
        return (v, pass_index(dy, dc))

    def x_dev(dx, dc=0):
        return (z * NX + around(x, dx, NX), pass_index(0, dc))

    def z_dev(dz):
        return (around(z, dz, nz) * NX + x, p)

    sibling = (v, y * NC + sib)
    x_peers = [(dx, dc) for dx in near_last(NX) + [0] for dc in range(NC) if dx or dc]
    y_far, x_far, z_far = near_last(ny), near_last(NX), near_last(nz)
    started, taken_sems = [], []

    def take():
        taken_sems.append(0)
        return len(taken_sems) - 1

    def describe(src, dst, device, i):
        return pltpu.make_async_remote_copy(
            src_ref=src, dst_ref=dst, send_sem=send_sems.at[i], recv_sem=recv_sems.at[i],
            device_id=device, device_id_type=MESH,
        )

    def remote(src, dst, device, i=None):
        copy = describe(src, dst, device, take() if i is None else i)
        copy.start()
        if i is None:
            started.append(copy)
        return copy

    def together(i, ref):
        whole = describe(ref, ref, sibling, i)
        started.append(whole)
        return whole

    def remotes(copies, ref):
        i = take()
        for src, dst, device in copies:
            remote(src, dst, device, i)
        return together(i, ref)

    mine = pl.ds(pl.multiple_of(c * voc, 128), voc)
    theirs = pl.ds(pl.multiple_of(sib * voc, 128), voc)
    mine_pas = pl.ds(pl.multiple_of(c * 128, 128), 128)
    local = [pltpu.make_async_copy(bias, bias_v, loc_sems.at[0]),
             pltpu.make_async_copy(tokens, tokens_v, loc_sems.at[1]),
             pltpu.make_async_copy(selected, sel_v.at[c], loc_sems.at[2]),
             pltpu.make_async_copy(hidden, gath.at[y], loc_sems.at[3]),
             pltpu.make_async_copy(weight, w_v.at[:, mine], loc_sems.at[4])]
    for j in range(ny):
        local.append(pltpu.make_async_copy(
            passages.at[:, pl.ds(j * wide, wide)], pas.at[j, mine_pas], loc_sems.at[5 + j]))
    local.append(pltpu.make_async_copy(positive_h, positive, loc_sems.at[5 + ny]))
    for copy in local:
        copy.start()

    barrier = pltpu.get_barrier_semaphore()
    passed_on = nz == 16
    z_near = (1, -1) if passed_on else z_far
    peers = ([z_dev(d) for d in z_near] + [pass_dev(d, 0) for d in y_far] + [x_dev(*d) for d in x_peers])
    for device in peers:
        pl.semaphore_signal(barrier, inc=1, device_id=device, device_id_type=MESH)
    pl.semaphore_wait(barrier, len(peers))

    hr, hc = own_rows // 2, d_model // 2
    top, bottom = pl.ds(0, hr), pl.ds(hr, hr)
    odd = lax.rem(x, 2)
    kept = pl.ds(pl.multiple_of(odd * hc, 128), hc)
    others = pl.ds(pl.multiple_of((1 - odd) * hc, 128), hc)

    def to_plane(rows, dy):
        return remote(hidden.at[rows, kept], gath.at[y, rows, kept], pass_dev(dy, 0))

    def relay(yy, rows, dy, i):
        remote(gath.at[yy, rows, kept], gath.at[yy, rows, kept], pass_dev(dy, 0), i)

    def forward(yy, rows, dx, i):
        remote(gath.at[yy, rows, kept], gath.at[yy, rows, kept], x_dev(dx), i)

    if ny == 4:
        up, down, far = around(y, -1, ny), around(y, 1, ny), around(y, 2, ny)
        pieces = [(pl.ds(i, 16), pl.ds(hr + i, 16)) for i in range(0, hr, 16)]
        first = [(to_plane(a, 1), to_plane(b, -1)) for a, b in pieces]
        then_up, then_down = to_plane(bottom, 1), to_plane(top, -1)
    else:
        direct = [to_plane(pl.ds(0, own_rows), d) for d in y_far]
    if passed_on:
        pl.semaphore_signal(entry.at[0], inc=1, device_id=z_dev(1), device_id_type=MESH)
        pl.semaphore_signal(entry.at[1], inc=1, device_id=z_dev(-1), device_id_type=MESH)
    to_w = remote(weight, w_v.at[:, mine], sibling)
    if ny == 4:
        i, i_up, i_down, i_far = take(), take(), take(), take()
        for (a, b), (to_up, to_down) in zip(pieces, first):
            to_up.wait_recv()
            relay(up, a, 1, i)
            to_down.wait_recv()
            relay(down, b, -1, i)
        relayed = together(i, gath.at[far, :, kept])
        forward(up, top, 1, i_up)
        forward(down, bottom, -1, i_down)
    if passed_on:
        pl.semaphore_wait(entry.at[0], 1)
        pl.semaphore_wait(entry.at[1], 1)
        pl.semaphore_signal(entry.at[2], inc=1, device_id=z_dev(2), device_id_type=MESH)
        pl.semaphore_signal(entry.at[3], inc=1, device_id=z_dev(-2), device_id_type=MESH)
    for copy in local[:3]:
        copy.wait()
    bias_b[c] = jnp.broadcast_to(bias_v[...].reshape(1, voc), (8, voc))
    to_small = [remote(selected, sel_v.at[c], sibling), remote(bias_b.at[c], bias_b.at[c], sibling)]
    to_pas = remotes([(passages.at[:, pl.ds(j * wide, wide)], pas.at[j, mine_pas], sibling) for j in range(ny)],
                     pas.at[pl.ds(0, ny // 2)])
    for ref in (maxl, sell, maxa, sela, selp, lenp, zf):
        ref[...] = jnp.zeros_like(ref)

    lengths = jnp.sum((tokens_v[...] != 1).astype(f32), axis=1, keepdims=True).astype(jnp.int32)
    lengths = jnp.broadcast_to(lengths, (n_queries, wide))
    for copy in to_small:
        copy.wait_recv()
    picks = jnp.concatenate([sel_v[0], sel_v[1]], axis=1)
    for j in range(ny):
        a = 2 * j * per_block
        b = a + per_block
        selp[j, 0:per_block, :] = jnp.where(c == 0, picks[a:b], picks[b:b + per_block])
        lenp[j, 0:per_block, :] = jnp.where(c == 0, lengths[a:b], lengths[b:b + per_block])

    def block(yy):
        logits = dot(gath[yy], w_v[...]).reshape(per_block, qlen, wide)
        at = iota((per_block, qlen, wide), 1)
        valid = at < lenp[yy][0:per_block].reshape(per_block, 1, wide)
        chosen = at == selp[yy][0:per_block].reshape(per_block, 1, wide)
        maxl[yy, 0:per_block, :] = jnp.max(jnp.where(valid, logits, -jnp.inf), axis=1)
        sell[yy, 0:per_block, :] = jnp.sum(jnp.where(chosen, logits, 0.0), axis=1)

    if ny == 4:
        then_up.wait_recv()
        forward(up, bottom, -1, i_up)
        from_x = [(up, together(i_up, gath.at[up, :, others]))]
        then_down.wait_recv()
        forward(down, top, 1, i_down)
        from_x.append((down, together(i_down, gath.at[down, :, others])))
    local[3].wait()
    local[4].wait()
    to_w.wait_recv()
    block(y)
    if ny == 4:
        relayed.wait_recv()
        forward(far, top, 1, i_far)
        forward(far, bottom, -1, i_far)
        from_x.append((far, together(i_far, gath.at[far, :, others])))
    else:
        from_x = []
        for d, copy in zip(y_far, direct):
            copy.wait_recv()
            there, i = around(y, -d, ny), take()
            forward(there, top, 1, i)
            forward(there, bottom, -1, i)
            from_x.append((there, together(i, gath.at[there, :, others])))
    for copy in local[5:]:
        copy.wait()
    to_pas.wait_recv()
    for j in range(ny):
        pas_t[j] = pas[j].T
    for n, (there, copy) in enumerate(from_x):
        if n == 2 and passed_on:
            pl.semaphore_wait(entry.at[2], 1)
            pl.semaphore_wait(entry.at[3], 1)
            pl.semaphore_signal(entry.at[4], inc=1, device_id=z_dev(4), device_id_type=MESH)
            pl.semaphore_signal(entry.at[5], inc=1, device_id=z_dev(-4), device_id_type=MESH)
        copy.wait_recv()
        block(there)

    wide_bias = jnp.concatenate([bias_b[0], bias_b[1]], axis=1)[0:1]
    for j in range(ny):
        maxa[j * SLOT:(j + 1) * SLOT, :] = maxl[j, 0:SLOT, :]
    pool[y] = jnp.log1p(jax.nn.softplus(maxa[...] + wide_bias)).astype(bf16)
    to_pool = {d: remote(pool.at[y], pool.at[y], pass_dev(d, 0)) for d in y_far}
    row, lane = iota((ROWS, 256), 0), iota((ROWS, 256), 1)
    place = lax.bitwise_and(row, SLOT - 1)
    query = (lax.shift_right_logical(row, 2) * NC + c) * per_block + place
    query = jnp.where((place < per_block) & (row < ny * SLOT), query, -1)
    pos_col = jnp.zeros((ROWS, 256), jnp.int32)
    for q in range(n_queries):
        pos_col = jnp.where(query == q, positive[q], pos_col)
    is_pos = (lane + y * 256) == pos_col
    onehot = is_pos.astype(f32).astype(bf16)

    score = dot(pool[y], pas_t[y])
    for d in reversed(y_far):
        to_pool[d].wait_recv()
        there = around(y, -d, ny)
        score = score + dot(pool[there], pas_t[there])

    for j in range(NX):
        a, b = (j // 2) * tile, (j % 2) * 128
        sc_s[j] = score[a:a + tile, b:b + 128]
    to_x = remotes([(sc_s.at[around(x, d, NX)], sc_x.at[d], x_dev(d)) for d in x_far], sc_x.at[pl.ds(1, NX - 1)])
    for j in range(ny):
        pos_s[j] = dot(onehot, pas[j]).astype(bf16)
    to_pos = remotes([(pos_s.at[around(y, d, ny)], pos_r.at[d], pass_dev(d, 0)) for d in y_far],
                     pos_r.at[pl.ds(1, ny - 1)])
    to_wr = {}
    for d in y_far:
        rows = pl.ds(pl.multiple_of(around(y, d, ny) * chip_cols, chip_cols), chip_cols)
        to_wr[d] = remote(w_v.at[rows, mine], wr.at[y, :, mine], pass_dev(d, 0))
    for j in range(ny):
        sel_r[y, j * SLOT:(j + 1) * SLOT, :] = selp[j, 0:SLOT, :]
    to_sel = remotes([(sel_r.at[y], sel_r.at[y], pass_dev(d, 0)) for d in y_far], sel_r.at[pl.ds(0, ny - 1)])
    to_other = remote(gath, gath_o, sibling)
    total = sc_s[x]
    to_x.wait_recv()
    for d in range(1, NX):
        total = total + sc_x[d]
    zs[...] = total
    if passed_on:
        pl.semaphore_wait(entry.at[4], 1)
        pl.semaphore_wait(entry.at[5], 1)
    to_z = remotes([(zs, zr.at[d], z_dev(d)) for d in z_far], zr.at[pl.ds(1, nz - 1)])
    wr_t[y] = w_v[pl.ds(pl.multiple_of(y * chip_cols, chip_cols), chip_cols), :].T
    prow = iota((tok, 128), 0)
    chunk = jnp.floor((prow.astype(f32) + 0.5) * (1.0 / ro)).astype(jnp.int32)
    zl = lax.bitwise_and(chunk, per_core - 1)
    xx = lax.shift_right_logical(chunk, per_core.bit_length() - 1)
    natural = prow + ro * (zl * NX + xx - chunk)
    plane = iota((tok, 128), 1)
    for j in range(tok // 128):
        perm[:, j * 128:(j + 1) * 128] = (natural == plane + j * 128).astype(f32).astype(bf16)
    for j in range(ny):
        sela[j * SLOT:(j + 1) * SLOT, :] = sell[j, 0:SLOT, :]
    at_sel = sela[...] + wide_bias
    slope[...] = jax.nn.sigmoid(at_sel) / (1.0 + jax.nn.softplus(at_sel))
    gath_t[0] = gath[...].reshape(tok, d_model).T
    to_z.wait_recv()
    for d in range(1, nz):
        total = total + zr[d]
    fin[x] = total
    to_fin = remotes([(fin.at[x], fin.at[x], x_dev(d)) for d in x_far], fin.at[pl.ds(0, NX - 1)])
    i = take()
    for d in reversed(y_far):
        to_wr[d].wait_recv()
        there = around(y, -d, ny)
        remote(wr.at[there, :, mine], wr.at[there, :, mine], sibling, i)
    to_wr_sib = together(i, wr.at[pl.ds(0, ny - 1), :, mine])
    to_pos.wait_recv()
    pos_entries = pos_s[y].astype(f32)
    for d in range(1, ny):
        pos_entries = pos_entries + pos_r[d].astype(f32)
    to_fin.wait_recv()

    score = jnp.concatenate([jnp.concatenate([fin[j], fin[j + 1]], axis=1) for j in range(0, NX, 2)], axis=0)
    peak = jnp.max(score, axis=1, keepdims=True)
    terms = jnp.exp(score - peak)
    other = jnp.where(is_pos, 0.0, terms)
    half_other = other.astype(bf16)
    to_u = {}
    for d in y_far:
        there = around(y, d, ny)
        u_s[there] = dot(half_other, pas[there]).astype(bf16)
        to_u[d] = remote(u_s.at[there], u_r.at[d], pass_dev(d, 0))
    stats = [peak, jnp.sum(other, axis=1, keepdims=True),
             jnp.sum(jnp.where(is_pos, terms, 0.0), axis=1, keepdims=True),
             jnp.sum(jnp.where(is_pos, score, 0.0), axis=1, keepdims=True)]
    eye = iota((ROWS, 128), 0) == iota((ROWS, 128), 1)
    turned = [jnp.sum(jnp.where(eye, s, 0.0), axis=0, keepdims=True) for s in stats]
    st_s[...] = jnp.concatenate(turned + [jnp.zeros((8 - len(turned), 128), f32)], axis=0)
    to_st = remotes([(st_s, st.at[d], pass_dev(d, 0)) for d in y_far], st.at[pl.ds(1, ny - 1)])
    st[0] = st_s[...]
    mine_u = dot(half_other, pas[y])
    to_wr_sib.wait_recv()
    for d in y_far:
        there = around(y, -d, ny)
        wr_t[there] = wr[there].T
    to_st.wait_recv()
    peaks = [st[i][0:1] for i in range(ny)]
    highest = functools.reduce(jnp.maximum, peaks)
    scale = [jnp.exp(k - highest) for k in peaks]
    rest = sum(scale[i] * st[i][1:2] for i in range(ny))
    denom = rest + sum(scale[i] * st[i][2:3] for i in range(ny))
    pos_score = sum(st[i][3:4] for i in range(ny))
    log_total = highest + jnp.log(denom)
    lane1 = iota((1, 128), 1)
    counted = (lax.bitwise_and(lane1, SLOT - 1) < per_block) & (lane1 < ny * SLOT)
    loss = jnp.sum(jnp.where(counted, log_total - pos_score, 0.0), axis=1, keepdims=True)
    factor = (loss_scale / n_queries) / denom

    def column(line):
        return jnp.sum(jnp.where(eye, line, 0.0), axis=1, keepdims=True)

    term = column(scale[0] * factor) * mine_u - column(rest * factor) * pos_entries
    for d in reversed(y_far):
        to_u[d].wait_recv()
        term = term + column(scale[d] * factor) * u_r[d].astype(f32)

    grad = term * slope[...]
    g_r[y] = grad.astype(bf16)
    to_g = {d: remote(g_r.at[y], g_r.at[y], pass_dev(d, 0)) for d in y_far}
    at = iota((per_block, qlen, wide), 1)

    def spread(yy, out):
        taken, picks = g_r[yy].astype(f32), sel_r[yy]
        for j in range(ny):
            some = taken[j * SLOT:j * SLOT + per_block].reshape(per_block, 1, wide)
            chosen = at == picks[j * SLOT:j * SLOT + per_block].reshape(per_block, 1, wide)
            out[j * own_rows:(j + 1) * own_rows, :] = jnp.where(chosen, some, 0.0).reshape(own_rows, wide).astype(bf16)

    spread(y, lh)
    to_lh = remote(lh.at[:, theirs], lh_o, sibling)

    out = dot(lh[...], wr_t[y])
    to_sel.wait_recv()
    for d in reversed(y_far):
        to_g[d].wait_recv()
        there = around(y, -d, ny)
        spread(there, lh_y)
        out = out + dot(lh_y[...], wr_t[there])
    out = dot(perm[...], out.astype(bf16)).astype(bf16)
    for k in range(NC):
        for j in range(NX):
            s1[k, j] = out[j * part:(j + 1) * part, k * 128:(k + 1) * 128]
    to_s1 = remotes([(s1.at[around(c, dc, NC), around(x, dx, NX)], s1_r.at[dx * NC + dc], x_dev(dx, dc))
                     for dx, dc in x_peers], s1_r.at[pl.ds(1, NX * NC - 1)])

    at_row = iota((ROWS, wide), 0)
    real = (lax.bitwise_and(at_row, SLOT - 1) < per_block) & (at_row < ny * SLOT)
    summed = jnp.sum(jnp.where(real, grad, 0.0), axis=0, keepdims=True)
    first = iota((8, voc), 0) == 0
    for j in range(NC):
        gs[j] = jnp.where(first, summed[:, j * voc:(j + 1) * voc], loss)
    to_gs = remote(gs.at[sib], gs_r, sibling)
    to_other.wait_recv()
    gath_t[1] = gath_o[...].reshape(tok, d_model).T
    gw_v[...] = dot(gath_t[0], lh[:, mine])

    to_s1.wait_recv()
    same, cross = s1[c, x].astype(f32), s1_r[1].astype(f32)
    for d in range(1, NX):
        same = same + s1_r[d * NC].astype(f32)
        cross = cross + s1_r[d * NC + 1].astype(f32)
    high[c] = same
    high[sib] = cross
    for core in range(NC):
        for k in range(per_core):
            to_row = (NC * (k // z_block) + core) * z_block + k % z_block
            zf[to_row, 0:ro, :] = high[core, k * ro:(k + 1) * ro]
    z2[...] = zf[...].astype(bf16)
    to_z2 = remotes([(z2.at[around(z, d, nz)], z2_r.at[d], z_dev(d)) for d in z_far], z2_r.at[pl.ds(1, nz - 1)])
    for copy in started[:-1]:
        copy.wait_send()
    to_lh.wait_recv()
    gw_v[...] += dot(gath_t[1], lh_o[...])
    gw_out = pltpu.make_async_copy(gw_v, gw_o, loc_sems.at[0])
    gw_out.start()
    to_gs.wait_recv()
    gb_o[...] = (gs[c][0:1] + gs_r[0:1]).reshape(voc)
    loss_o[...] = (gs[c][1:2, 0:1] + gs_r[1:2, 0:1]) * (1.0 / n_queries)
    total = zf[z]
    to_z2.wait_recv()
    for d in range(1, nz):
        total = total + z2_r[d].astype(f32)
    gh_o[...] = total[0:ro].astype(bf16)

    to_z2.wait_send()
    gw_out.wait()


def hand_out(*refs):
    sems = refs[8]
    pairs = [(refs[i], refs[4 + i]) for i in (0, 1, 3)]
    rows = refs[2].shape[0] // 4
    pairs += [(refs[2].at[pl.ds(i * rows, rows)], refs[6].at[pl.ds(i * rows, rows)]) for i in range(4)]
    copies = [pltpu.make_async_copy(a, b, sems.at[i]) for i, (a, b) in enumerate(pairs)]
    for copy in reversed(copies):
        copy.start()
    for copy in copies:
        copy.wait()


def local(nz, ny, hidden, weight, bias, token_ids, passages, positive, selected):
    n_queries, qlen = token_ids.shape
    own_rows, d = hidden.shape
    voc = weight.shape[1]
    wide = NC * voc
    tok = ny * own_rows
    ro = (NC * tok) // (nz * NX)
    rp = -(-ro // 16) * 16
    part = (nz // 2) * ro
    tile = ROWS * 2 // NX
    i32 = jnp.int32
    vmem = pl.BlockSpec(memory_space=pltpu.VMEM)
    anywhere = pl.BlockSpec(memory_space=pl.ANY)
    hbm = pl.BlockSpec(memory_space=pltpu.HBM)
    scratch = [
        ((ny, own_rows, d), bf16), ((ny, own_rows, d), bf16), ((NC, d, tok), bf16),
        ((d, wide), bf16), ((ny, NC * 128, wide), bf16), ((ny, wide, NC * 128), bf16),
        ((ny, NC * 128, wide), bf16), ((ny, wide, NC * 128), bf16), ((tok, tok), bf16),
        ((voc,), f32), ((NC, 8, voc), f32), None, ((n_queries, qlen), i32), ((NC, n_queries, voc), i32),
        ((ny, 8, wide), i32), ((ny, 8, wide), i32),
        ((ny, 8, wide), f32), ((ny, 8, wide), f32), ((ROWS, wide), f32), ((ROWS, wide), f32),
        ((ny, ROWS, wide), bf16), ((ny, ROWS, wide), bf16), ((ny, ROWS, wide), bf16),
        ((NX, tile, 128), f32), ((NX, tile, 128), f32), ((tile, 128), f32), ((nz, tile, 128), f32),
        ((NX, tile, 128), f32), ((8, 128), f32), ((ny, 8, 128), f32),
        ((ny, ROWS, wide), bf16), ((ny, ROWS, wide), bf16), ((ROWS, wide), f32),
        ((ny, ROWS, wide), i32), ((ny, ROWS, wide), bf16),
        ((tok, wide), bf16), ((tok, wide), bf16), ((tok, voc), bf16),
        ((NC, 8, voc), f32), ((8, voc), f32),
        ((NC, NX, part, 128), bf16), ((NX * NC, part, 128), bf16), ((NC, part, 128), f32),
        ((nz, rp, 128), f32), ((nz, rp, 128), bf16), ((nz, rp, 128), bf16), ((d, voc), f32),
    ]
    results = pl.pallas_call(
        functools.partial(kernel, nz, ny, n_queries),
        out_shape=(
            jax.ShapeDtypeStruct((1, 1), f32),
            jax.ShapeDtypeStruct((ro, 128), bf16),
            jax.ShapeDtypeStruct((d, voc), f32),
            jax.ShapeDtypeStruct((voc,), f32),
        ),
        in_specs=[hbm] * 7,
        out_specs=(vmem, vmem, anywhere, vmem),
        scratch_shapes=[pltpu.VMEM(*k) if k else pltpu.SMEM((n_queries,), i32) for k in scratch] + [
            pltpu.SemaphoreType.DMA((MAX_SEMS,)),
            pltpu.SemaphoreType.DMA((MAX_SEMS,)),
            pltpu.SemaphoreType.DMA((6 + ny,)),
            pltpu.SemaphoreType.REGULAR((6,)),
        ],
        compiler_params=pltpu.CompilerParams(
            collective_id=0, has_side_effects=True, vmem_limit_bytes=48 * 1024 * 1024
        ),
    )(*(pltpu.with_memory_space_constraint(a, pltpu.HBM)
        for a in (hidden, weight, bias, token_ids, passages, positive, selected)))
    loss, grad_hidden, grad_weight, grad_bias = pl.pallas_call(
        hand_out,
        out_shape=tuple(jax.ShapeDtypeStruct(r.shape, r.dtype) for r in results),
        in_specs=[anywhere] * 4,
        out_specs=(hbm,) * 4,
        scratch_shapes=[pltpu.SemaphoreType.DMA((7,))],
        compiler_params=pltpu.CompilerParams(vmem_limit_bytes=1024 * 1024),
    )(*results)
    return loss.reshape(()), grad_hidden, grad_weight, grad_bias


def solution(mesh):
    in_specs = (
        P("pass", None),
        P(None, ("vocab", "pass")),
        P(("vocab", "pass")),
        P(),
        P("pass", "vocab"),
        P(),
        P(None, ("vocab", "pass")),
    )
    out_specs = (P(), P("vocab", "pass"), P(None, ("vocab", "pass")), P(("vocab", "pass")))
    body = functools.partial(local, mesh.shape["vocab"] // NX, mesh.shape["pass"] // NC)
    return jax.shard_map(body, mesh=mesh, in_specs=in_specs, out_specs=out_specs, check_vma=False)
```

```python
import functools

import jax
import jax.numpy as jnp
from jax import lax
from jax.experimental import pallas as pl
from jax.experimental.pallas import tpu as pltpu
from jax.sharding import PartitionSpec as P

loss_scale = 4096.0
NX = 4
NC = 2
SLOT = 4
ROWS = 16
MAX_SEMS = 35
MESH = pl.DeviceIdType.MESH
f32 = jnp.float32
bf16 = jnp.bfloat16


def dot(a, b):
    return jnp.dot(a, b, preferred_element_type=f32)


def iota(shape, axis):
    return lax.broadcasted_iota(jnp.int32, shape, axis)


def near_last(size):
    return sorted(range(1, size), key=lambda d: -min(d, size - d))


def kernel(nz, ny, n_queries, hidden, weight, bias, tokens, passages, positive_h, selected,
           loss_o, gh_o, gw_o, gb_o,
           gath, gath_o, gath_t, w_v, wr, wr_t, pas, pas_t, perm, bias_v, bias_b, positive, tokens_v, sel_v, selp, lenp,
           maxl, sell, maxa, sela, pool, pos_s, pos_r, sc_s, sc_x, zs, zr, fin, st_s, st, u_s, u_r, slope, pos_f, grads,
           sel_r, g_r, lh, lh_y, lh_o, gs, gs_r, s1, s1_r, high,
           zf, z2, z2_r, gw_v, send_sems, recv_sems, loc_sems, entry):
    n_pass = ny * NC
    v = lax.axis_index("vocab")
    p = lax.axis_index("pass")
    z, x = lax.div(v, NX), lax.rem(v, NX)
    y, c = lax.div(p, NC), lax.rem(p, NC)
    sib = 1 - c
    own_rows = gath.shape[1]
    d_model = gath.shape[2]
    voc = w_v.shape[1] // NC
    wide = NC * voc
    qlen = tokens_v.shape[1]
    per_block = n_queries // n_pass
    tok = ny * own_rows
    ro = (NC * tok) // (nz * NX)
    per_core = nz // 2
    z_block = nz // n_pass
    part = per_core * ro
    chip_cols = NC * 128
    tile = sc_s.shape[1]

    def around(value, shift, size):
        return lax.rem(value + (shift + size), size)

    def pass_index(dy, dc):
        return around(y, dy, ny) * NC + around(c, dc, NC)

    def pass_dev(dy, dc):
        return (v, pass_index(dy, dc))

    def x_dev(dx, dc=0):
        return (z * NX + around(x, dx, NX), pass_index(0, dc))

    def z_dev(dz):
        return (around(z, dz, nz) * NX + x, p)

    sibling = (v, y * NC + sib)
    x_peers = [(dx, dc) for dx in near_last(NX) + [0] for dc in range(NC) if dx or dc]
    y_far, x_far, z_far = near_last(ny), near_last(NX), near_last(nz)
    started, taken_sems = [], []

    def take():
        taken_sems.append(0)
        return len(taken_sems) - 1

    def describe(src, dst, device, i):
        return pltpu.make_async_remote_copy(
            src_ref=src, dst_ref=dst, send_sem=send_sems.at[i], recv_sem=recv_sems.at[i],
            device_id=device, device_id_type=MESH,
        )

    def remote(src, dst, device, i=None):
        copy = describe(src, dst, device, take() if i is None else i)
        copy.start()
        if i is None:
            started.append(copy)
        return copy

    def together(i, ref):
        whole = describe(ref, ref, sibling, i)
        started.append(whole)
        return whole

    def remotes(copies, ref):
        i = take()
        for src, dst, device in copies:
            remote(src, dst, device, i)
        return together(i, ref)

    mine = pl.ds(pl.multiple_of(c * voc, 128), voc)
    theirs = pl.ds(pl.multiple_of(sib * voc, 128), voc)
    mine_pas = pl.ds(pl.multiple_of(c * 128, 128), 128)
    local = [pltpu.make_async_copy(bias, bias_v, loc_sems.at[0]),
             pltpu.make_async_copy(tokens, tokens_v, loc_sems.at[1]),
             pltpu.make_async_copy(selected, sel_v.at[c], loc_sems.at[2]),
             pltpu.make_async_copy(hidden, gath.at[y], loc_sems.at[3]),
             pltpu.make_async_copy(weight, w_v.at[:, mine], loc_sems.at[4])]
    for j in range(ny):
        local.append(pltpu.make_async_copy(
            passages.at[:, pl.ds(j * wide, wide)], pas.at[j, mine_pas], loc_sems.at[5 + j]))
    local.append(pltpu.make_async_copy(positive_h, positive, loc_sems.at[5 + ny]))
    for copy in local:
        copy.start()

    barrier = pltpu.get_barrier_semaphore()
    passed_on = nz == 16
    z_near = (2, -2, 1, -1) if passed_on else z_far
    peers = ([z_dev(d) for d in z_near] + [pass_dev(d, 0) for d in y_far] + [x_dev(*d) for d in x_peers])
    for device in peers:
        pl.semaphore_signal(barrier, inc=1, device_id=device, device_id_type=MESH)
    pl.semaphore_wait(barrier, len(peers))

    hr = own_rows // 2
    top, bottom = pl.ds(0, hr), pl.ds(hr, hr)
    if ny == 4:
        pieces = [(pl.ds(i, 16), pl.ds(hr + i, 16)) for i in range(0, hr, 16)]
        first = []
        for a, b in pieces:
            first.append((remote(hidden.at[a], gath.at[y, a], pass_dev(1, 0)),
                          remote(hidden.at[b], gath.at[y, b], pass_dev(-1, 0))))
        then_up = remote(hidden.at[bottom], gath.at[y, bottom], pass_dev(1, 0))
        then_down = remote(hidden.at[top], gath.at[y, top], pass_dev(-1, 0))
    else:
        direct = [remote(hidden, gath.at[y], pass_dev(d, 0)) for d in y_far]
    if passed_on:
        pl.semaphore_signal(entry.at[0], inc=1, device_id=z_dev(2), device_id_type=MESH)
        pl.semaphore_signal(entry.at[1], inc=1, device_id=z_dev(-2), device_id_type=MESH)
    to_w = remote(weight, w_v.at[:, mine], sibling)
    for copy in local[:3]:
        copy.wait()
    bias_b[c] = jnp.broadcast_to(bias_v[...].reshape(1, voc), (8, voc))
    to_small = [remote(selected, sel_v.at[c], sibling), remote(bias_b.at[c], bias_b.at[c], sibling)]
    to_pas = remotes([(passages.at[:, pl.ds(j * wide, wide)], pas.at[j, mine_pas], sibling) for j in range(ny)],
                     pas.at[pl.ds(0, ny // 2)])

    if ny == 4:
        up, down, far = around(y, -1, ny), around(y, 1, ny), around(y, 2, ny)
        i = take()
        for (a, b), (to_up, to_down) in zip(pieces, first):
            to_up.wait_recv()
            remote(gath.at[up, a], gath.at[up, a], pass_dev(1, 0), i)
            to_down.wait_recv()
            remote(gath.at[down, b], gath.at[down, b], pass_dev(-1, 0), i)
        relayed = together(i, gath.at[far])
    if passed_on:
        pl.semaphore_wait(entry.at[0], 1)
        pl.semaphore_wait(entry.at[1], 1)
        pl.semaphore_signal(entry.at[2], inc=1, device_id=z_dev(4), device_id_type=MESH)
        pl.semaphore_signal(entry.at[3], inc=1, device_id=z_dev(-4), device_id_type=MESH)
    for ref in (maxl, sell, maxa, sela, selp, lenp, zf):
        ref[...] = jnp.zeros_like(ref)

    lengths = jnp.sum((tokens_v[...] != 1).astype(f32), axis=1, keepdims=True).astype(jnp.int32)
    lengths = jnp.broadcast_to(lengths, (n_queries, wide))
    for copy in to_small:
        copy.wait_recv()
    picks = jnp.concatenate([sel_v[0], sel_v[1]], axis=1)
    for j in range(ny):
        a = 2 * j * per_block
        b = a + per_block
        selp[j, 0:per_block, :] = jnp.where(c == 0, picks[a:b], picks[b:b + per_block])
        lenp[j, 0:per_block, :] = jnp.where(c == 0, lengths[a:b], lengths[b:b + per_block])

    def block(yy):
        logits = dot(gath[yy], w_v[...]).reshape(per_block, qlen, wide)
        at = iota((per_block, qlen, wide), 1)
        valid = at < lenp[yy][0:per_block].reshape(per_block, 1, wide)
        chosen = at == selp[yy][0:per_block].reshape(per_block, 1, wide)
        maxl[yy, 0:per_block, :] = jnp.max(jnp.where(valid, logits, -jnp.inf), axis=1)
        sell[yy, 0:per_block, :] = jnp.sum(jnp.where(chosen, logits, 0.0), axis=1)

    local[3].wait()
    local[4].wait()
    if ny == 4:
        to_w.wait_recv()
        block(y)
        then_up.wait_recv()
        block(up)
        then_down.wait_recv()
        block(down)
    else:
        to_w.wait_recv()
        block(y)
    for copy in local[5:]:
        copy.wait()
    to_pas.wait_recv()
    for j in range(ny):
        pas_t[j] = pas[j].T
    if ny == 4:
        relayed.wait_recv()
        block(far)
    else:
        for d, copy in zip(y_far, direct):
            copy.wait_recv()
            block(around(y, -d, ny))

    wide_bias = jnp.concatenate([bias_b[0], bias_b[1]], axis=1)[0:1]
    for j in range(ny):
        maxa[j * SLOT:(j + 1) * SLOT, :] = maxl[j, 0:SLOT, :]
    pool[y] = jnp.log1p(jax.nn.softplus(maxa[...] + wide_bias)).astype(bf16)
    to_pool = {d: remote(pool.at[y], pool.at[y], pass_dev(d, 0)) for d in y_far}
    row, lane = iota((ROWS, 256), 0), iota((ROWS, 256), 1)
    place = lax.bitwise_and(row, SLOT - 1)
    query = (lax.shift_right_logical(row, 2) * NC + c) * per_block + place
    query = jnp.where((place < per_block) & (row < ny * SLOT), query, -1)
    pos_col = jnp.zeros((ROWS, 256), jnp.int32)
    for q in range(n_queries):
        pos_col = jnp.where(query == q, positive[q], pos_col)
    is_pos = (lane + y * 256) == pos_col
    onehot = is_pos.astype(f32).astype(bf16)

    score = dot(pool[y], pas_t[y])
    for d in reversed(y_far):
        to_pool[d].wait_recv()
        there = around(y, -d, ny)
        score = score + dot(pool[there], pas_t[there])

    for j in range(NX):
        a, b = (j // 2) * tile, (j % 2) * 128
        sc_s[j] = score[a:a + tile, b:b + 128]
    to_x = remotes([(sc_s.at[around(x, d, NX)], sc_x.at[d], x_dev(d)) for d in x_far], sc_x.at[pl.ds(1, NX - 1)])
    for j in range(ny):
        pos_s[j] = dot(onehot, pas[j]).astype(bf16)
    to_pos = remotes([(pos_s, pos_r.at[d], pass_dev(d, 0)) for d in y_far],
                     pos_r.at[pl.ds(1, ny - 1)])
    to_wr = {}
    for d in y_far:
        rows = pl.ds(pl.multiple_of(around(y, d, ny) * chip_cols, chip_cols), chip_cols)
        to_wr[d] = remote(w_v.at[rows, mine], wr.at[y, :, mine], pass_dev(d, 0))
    for j in range(ny):
        sel_r[y, j * SLOT:(j + 1) * SLOT, :] = selp[j, 0:SLOT, :]
    to_sel = remotes([(sel_r.at[y], sel_r.at[y], pass_dev(d, 0)) for d in y_far], sel_r.at[pl.ds(0, ny - 1)])
    to_other = remote(gath, gath_o, sibling)
    total = sc_s[x]
    to_x.wait_recv()
    for d in range(1, NX):
        total = total + sc_x[d]
    zs[...] = total
    if passed_on:
        pl.semaphore_wait(entry.at[2], 1)
        pl.semaphore_wait(entry.at[3], 1)
    to_z = remotes([(zs, zr.at[d], z_dev(d)) for d in z_far], zr.at[pl.ds(1, nz - 1)])
    wr_t[y] = w_v[pl.ds(pl.multiple_of(y * chip_cols, chip_cols), chip_cols), :].T
    prow = iota((tok, 128), 0)
    chunk = jnp.floor((prow.astype(f32) + 0.5) * (1.0 / ro)).astype(jnp.int32)
    zl = lax.bitwise_and(chunk, per_core - 1)
    xx = lax.shift_right_logical(chunk, per_core.bit_length() - 1)
    natural = prow + ro * (zl * NX + xx - chunk)
    plane = iota((tok, 128), 1)
    for j in range(tok // 128):
        perm[:, j * 128:(j + 1) * 128] = (natural == plane + j * 128).astype(f32).astype(bf16)
    for j in range(ny):
        sela[j * SLOT:(j + 1) * SLOT, :] = sell[j, 0:SLOT, :]
    at_sel = sela[...] + wide_bias
    slope[y] = jax.nn.sigmoid(at_sel) / (1.0 + jax.nn.softplus(at_sel))
    to_slope = remotes([(slope.at[y], slope.at[y], pass_dev(d, 0)) for d in y_far], slope.at[pl.ds(0, ny - 1)])
    gath_t[0] = gath[...].reshape(tok, d_model).T
    to_z.wait_recv()
    for d in range(1, nz):
        total = total + zr[d]
    fin[x] = total
    to_fin = remotes([(fin.at[x], fin.at[x], x_dev(d)) for d in x_far], fin.at[pl.ds(0, NX - 1)])
    i = take()
    for d in reversed(y_far):
        to_wr[d].wait_recv()
        there = around(y, -d, ny)
        remote(wr.at[there, :, mine], wr.at[there, :, mine], sibling, i)
    to_wr_sib = together(i, wr.at[pl.ds(0, ny - 1), :, mine])
    to_pos.wait_recv()
    for j in range(ny):
        entries = pos_s[j].astype(f32)
        for d in range(1, ny):
            entries = entries + pos_r[d, j].astype(f32)
        pos_f[j] = entries
    to_fin.wait_recv()

    score = jnp.concatenate([jnp.concatenate([fin[j], fin[j + 1]], axis=1) for j in range(0, NX, 2)], axis=0)
    peak = jnp.max(score, axis=1, keepdims=True)
    terms = jnp.exp(score - peak)
    other = jnp.where(is_pos, 0.0, terms)
    stats = [peak, jnp.sum(other, axis=1, keepdims=True),
             jnp.sum(jnp.where(is_pos, terms, 0.0), axis=1, keepdims=True),
             jnp.sum(jnp.where(is_pos, score, 0.0), axis=1, keepdims=True)]
    eye = iota((ROWS, 128), 0) == iota((ROWS, 128), 1)
    turned = [jnp.sum(jnp.where(eye, s, 0.0), axis=0, keepdims=True) for s in stats]
    st_s[...] = jnp.concatenate(turned + [jnp.zeros((8 - len(turned), 128), f32)], axis=0)
    other = other.astype(bf16)
    for j in range(ny):
        u_s[j] = dot(other, pas[j]).astype(bf16)
    to_u = {d: remote(u_s, u_r.at[d], pass_dev(d, 0)) for d in y_far}
    to_st = remotes([(st_s, st.at[d], pass_dev(d, 0)) for d in y_far], st.at[pl.ds(1, ny - 1)])
    st[0] = st_s[...]
    to_wr_sib.wait_recv()
    for d in y_far:
        there = around(y, -d, ny)
        wr_t[there] = wr[there].T
    to_st.wait_recv()
    peaks = [st[i][0:1] for i in range(ny)]
    highest = functools.reduce(jnp.maximum, peaks)
    scale = [jnp.exp(k - highest) for k in peaks]
    rest = sum(scale[i] * st[i][1:2] for i in range(ny))
    denom = rest + sum(scale[i] * st[i][2:3] for i in range(ny))
    pos_score = sum(st[i][3:4] for i in range(ny))
    log_total = highest + jnp.log(denom)
    lane1 = iota((1, 128), 1)
    counted = (lax.bitwise_and(lane1, SLOT - 1) < per_block) & (lane1 < ny * SLOT)
    loss = jnp.sum(jnp.where(counted, log_total - pos_score, 0.0), axis=1, keepdims=True)
    factor = (loss_scale / n_queries) / denom

    def column(line):
        return jnp.sum(jnp.where(eye, line, 0.0), axis=1, keepdims=True)

    weights, pos_weight = [column(k * factor) for k in scale], column(rest * factor)
    for j in range(ny):
        grads[j] = weights[0] * u_s[j].astype(f32) - pos_weight * pos_f[j]
    to_slope.wait_recv()
    for d in reversed(y_far):
        to_u[d].wait_recv()
        for j in range(ny):
            grads[j] += weights[d] * u_r[d, j].astype(f32)

    for j in range(ny):
        grads[j] = grads[j] * slope[j]
        g_r[j] = grads[j].astype(bf16)
    grad = grads[y]
    at = iota((per_block, qlen, wide), 1)

    def spread(yy, out):
        taken, picks = g_r[yy].astype(f32), sel_r[yy]
        for j in range(ny):
            some = taken[j * SLOT:j * SLOT + per_block].reshape(per_block, 1, wide)
            chosen = at == picks[j * SLOT:j * SLOT + per_block].reshape(per_block, 1, wide)
            out[j * own_rows:(j + 1) * own_rows, :] = jnp.where(chosen, some, 0.0).reshape(own_rows, wide).astype(bf16)

    spread(y, lh)
    to_lh = remote(lh.at[:, theirs], lh_o, sibling)

    out = dot(lh[...], wr_t[y])
    to_sel.wait_recv()
    for d in reversed(y_far):
        there = around(y, -d, ny)
        spread(there, lh_y)
        out = out + dot(lh_y[...], wr_t[there])
    out = dot(perm[...], out.astype(bf16)).astype(bf16)
    for k in range(NC):
        for j in range(NX):
            s1[k, j] = out[j * part:(j + 1) * part, k * 128:(k + 1) * 128]
    to_s1 = remotes([(s1.at[around(c, dc, NC), around(x, dx, NX)], s1_r.at[dx * NC + dc], x_dev(dx, dc))
                     for dx, dc in x_peers], s1_r.at[pl.ds(1, NX * NC - 1)])

    at_row = iota((ROWS, wide), 0)
    real = (lax.bitwise_and(at_row, SLOT - 1) < per_block) & (at_row < ny * SLOT)
    summed = jnp.sum(jnp.where(real, grad, 0.0), axis=0, keepdims=True)
    first = iota((8, voc), 0) == 0
    for j in range(NC):
        gs[j] = jnp.where(first, summed[:, j * voc:(j + 1) * voc], loss)
    to_gs = remote(gs.at[sib], gs_r, sibling)
    to_other.wait_recv()
    gath_t[1] = gath_o[...].reshape(tok, d_model).T
    gw_v[...] = dot(gath_t[0], lh[:, mine])

    to_s1.wait_recv()
    same, cross = s1[c, x].astype(f32), s1_r[1].astype(f32)
    for d in range(1, NX):
        same = same + s1_r[d * NC].astype(f32)
        cross = cross + s1_r[d * NC + 1].astype(f32)
    high[c] = same
    high[sib] = cross
    for core in range(NC):
        for k in range(per_core):
            to_row = (NC * (k // z_block) + core) * z_block + k % z_block
            zf[to_row, 0:ro, :] = high[core, k * ro:(k + 1) * ro]
    z2[...] = zf[...].astype(bf16)
    to_z2 = remotes([(z2.at[around(z, d, nz)], z2_r.at[d], z_dev(d)) for d in z_far], z2_r.at[pl.ds(1, nz - 1)])
    for copy in started[:-1]:
        copy.wait_send()
    to_lh.wait_recv()
    gw_v[...] += dot(gath_t[1], lh_o[...])
    gw_out = pltpu.make_async_copy(gw_v, gw_o, loc_sems.at[0])
    gw_out.start()
    to_gs.wait_recv()
    gb_o[...] = (gs[c][0:1] + gs_r[0:1]).reshape(voc)
    loss_o[...] = (gs[c][1:2, 0:1] + gs_r[1:2, 0:1]) * (1.0 / n_queries)
    total = zf[z]
    to_z2.wait_recv()
    for d in range(1, nz):
        total = total + z2_r[d].astype(f32)
    gh_o[...] = total[0:ro].astype(bf16)

    to_z2.wait_send()
    gw_out.wait()


def hand_out(*refs):
    sems = refs[8]
    pairs = [(refs[i], refs[4 + i]) for i in (0, 1, 3)]
    rows = refs[2].shape[0] // 4
    pairs += [(refs[2].at[pl.ds(i * rows, rows)], refs[6].at[pl.ds(i * rows, rows)]) for i in range(4)]
    copies = [pltpu.make_async_copy(a, b, sems.at[i]) for i, (a, b) in enumerate(pairs)]
    for copy in reversed(copies):
        copy.start()
    for copy in copies:
        copy.wait()


def local(nz, ny, hidden, weight, bias, token_ids, passages, positive, selected):
    n_queries, qlen = token_ids.shape
    own_rows, d = hidden.shape
    voc = weight.shape[1]
    wide = NC * voc
    tok = ny * own_rows
    ro = (NC * tok) // (nz * NX)
    rp = -(-ro // 16) * 16
    part = (nz // 2) * ro
    tile = ROWS * 2 // NX
    i32 = jnp.int32
    vmem = pl.BlockSpec(memory_space=pltpu.VMEM)
    anywhere = pl.BlockSpec(memory_space=pl.ANY)
    hbm = pl.BlockSpec(memory_space=pltpu.HBM)
    scratch = [
        ((ny, own_rows, d), bf16), ((ny, own_rows, d), bf16), ((NC, d, tok), bf16),
        ((d, wide), bf16), ((ny, NC * 128, wide), bf16), ((ny, wide, NC * 128), bf16),
        ((ny, NC * 128, wide), bf16), ((ny, wide, NC * 128), bf16), ((tok, tok), bf16),
        ((voc,), f32), ((NC, 8, voc), f32), None, ((n_queries, qlen), i32), ((NC, n_queries, voc), i32),
        ((ny, 8, wide), i32), ((ny, 8, wide), i32),
        ((ny, 8, wide), f32), ((ny, 8, wide), f32), ((ROWS, wide), f32), ((ROWS, wide), f32),
        ((ny, ROWS, wide), bf16), ((ny, ROWS, wide), bf16), ((ny, ny, ROWS, wide), bf16),
        ((NX, tile, 128), f32), ((NX, tile, 128), f32), ((tile, 128), f32), ((nz, tile, 128), f32),
        ((NX, tile, 128), f32), ((8, 128), f32), ((ny, 8, 128), f32),
        ((ny, ROWS, wide), bf16), ((ny, ny, ROWS, wide), bf16), ((ny, ROWS, wide), f32),
        ((ny, ROWS, wide), f32), ((ny, ROWS, wide), f32),
        ((ny, ROWS, wide), i32), ((ny, ROWS, wide), bf16),
        ((tok, wide), bf16), ((tok, wide), bf16), ((tok, voc), bf16),
        ((NC, 8, voc), f32), ((8, voc), f32),
        ((NC, NX, part, 128), bf16), ((NX * NC, part, 128), bf16), ((NC, part, 128), f32),
        ((nz, rp, 128), f32), ((nz, rp, 128), bf16), ((nz, rp, 128), bf16), ((d, voc), f32),
    ]
    results = pl.pallas_call(
        functools.partial(kernel, nz, ny, n_queries),
        out_shape=(
            jax.ShapeDtypeStruct((1, 1), f32),
            jax.ShapeDtypeStruct((ro, 128), bf16),
            jax.ShapeDtypeStruct((d, voc), f32),
            jax.ShapeDtypeStruct((voc,), f32),
        ),
        in_specs=[hbm] * 7,
        out_specs=(vmem, vmem, anywhere, vmem),
        scratch_shapes=[pltpu.VMEM(*k) if k else pltpu.SMEM((n_queries,), i32) for k in scratch] + [
            pltpu.SemaphoreType.DMA((MAX_SEMS,)),
            pltpu.SemaphoreType.DMA((MAX_SEMS,)),
            pltpu.SemaphoreType.DMA((6 + ny,)),
            pltpu.SemaphoreType.REGULAR((4,)),
        ],
        compiler_params=pltpu.CompilerParams(
            collective_id=0, has_side_effects=True, vmem_limit_bytes=48 * 1024 * 1024
        ),
    )(*(pltpu.with_memory_space_constraint(a, pltpu.HBM)
        for a in (hidden, weight, bias, token_ids, passages, positive, selected)))
    loss, grad_hidden, grad_weight, grad_bias = pl.pallas_call(
        hand_out,
        out_shape=tuple(jax.ShapeDtypeStruct(r.shape, r.dtype) for r in results),
        in_specs=[anywhere] * 4,
        out_specs=(hbm,) * 4,
        scratch_shapes=[pltpu.SemaphoreType.DMA((7,))],
        compiler_params=pltpu.CompilerParams(vmem_limit_bytes=1024 * 1024),
    )(*results)
    return loss.reshape(()), grad_hidden, grad_weight, grad_bias


def solution(mesh):
    in_specs = (
        P("pass", None),
        P(None, ("vocab", "pass")),
        P(("vocab", "pass")),
        P(),
        P("pass", "vocab"),
        P(),
        P(None, ("vocab", "pass")),
    )
    out_specs = (P(), P("vocab", "pass"), P(None, ("vocab", "pass")), P(("vocab", "pass")))
    body = functools.partial(local, mesh.shape["vocab"] // NX, mesh.shape["pass"] // NC)
    return jax.shard_map(body, mesh=mesh, in_specs=in_specs, out_specs=out_specs, check_vma=False)
```

```python
import functools

import jax
import jax.numpy as jnp
from jax import lax
from jax.experimental import pallas as pl
from jax.experimental.pallas import tpu as pltpu
from jax.sharding import PartitionSpec as P

loss_scale = 4096.0
NX = 4
NC = 2
SLOT = 4
ROWS = 16
MAX_SEMS = 37
MESH = pl.DeviceIdType.MESH
f32 = jnp.float32
bf16 = jnp.bfloat16


def dot(a, b):
    return jnp.dot(a, b, preferred_element_type=f32)


def iota(shape, axis):
    return lax.broadcasted_iota(jnp.int32, shape, axis)


def near_last(size):
    return sorted(range(1, size), key=lambda d: -min(d, size - d))


def kernel(nz, ny, n_queries, hidden, weight, bias, tokens, passages, positive_h, selected,
           loss_o, gh_o, gw_o, gb_o,
           gath, gath_o, gath_t, w_v, wr, wr_t, pas, pas_t, perm, bias_v, bias_b, positive, tokens_v, sel_v, selp, lenp,
           maxl, sell, maxa, sela, pool, pos_s, pos_r, sc_s, sc_x, zs, zr, fin, st_s, st, u_s, u_r, slope,
           sel_r, g_r, lh, lh_y, lh_o, gs, gs_r, s1, s1_r, high,
           zf, z2, z2_r, gw_v, send_sems, recv_sems, loc_sems, entry):
    n_pass = ny * NC
    v = lax.axis_index("vocab")
    p = lax.axis_index("pass")
    z, x = lax.div(v, NX), lax.rem(v, NX)
    y, c = lax.div(p, NC), lax.rem(p, NC)
    sib = 1 - c
    own_rows = gath.shape[1]
    d_model = gath.shape[2]
    voc = w_v.shape[1] // NC
    wide = NC * voc
    qlen = tokens_v.shape[1]
    per_block = n_queries // n_pass
    tok = ny * own_rows
    ro = (NC * tok) // (nz * NX)
    per_core = nz // 2
    z_block = nz // n_pass
    part = per_core * ro
    chip_cols = NC * 128
    tile = sc_s.shape[1]

    def around(value, shift, size):
        return lax.rem(value + (shift + size), size)

    def pass_index(dy, dc):
        return around(y, dy, ny) * NC + around(c, dc, NC)

    def pass_dev(dy, dc):
        return (v, pass_index(dy, dc))

    def x_dev(dx, dc=0):
        return (z * NX + around(x, dx, NX), pass_index(0, dc))

    def z_dev(dz):
        return (around(z, dz, nz) * NX + x, p)

    sibling = (v, y * NC + sib)
    x_peers = [(dx, dc) for dx in near_last(NX) + [0] for dc in range(NC) if dx or dc]
    y_far, x_far, z_far = near_last(ny), near_last(NX), near_last(nz)
    started, taken_sems = [], []

    def take():
        taken_sems.append(0)
        return len(taken_sems) - 1

    def describe(src, dst, device, i):
        return pltpu.make_async_remote_copy(
            src_ref=src, dst_ref=dst, send_sem=send_sems.at[i], recv_sem=recv_sems.at[i],
            device_id=device, device_id_type=MESH,
        )

    def remote(src, dst, device, i=None):
        copy = describe(src, dst, device, take() if i is None else i)
        copy.start()
        if i is None:
            started.append(copy)
        return copy

    def together(i, ref):
        whole = describe(ref, ref, sibling, i)
        started.append(whole)
        return whole

    def remotes(copies, ref):
        i = take()
        for src, dst, device in copies:
            remote(src, dst, device, i)
        return together(i, ref)

    mine = pl.ds(pl.multiple_of(c * voc, 128), voc)
    theirs = pl.ds(pl.multiple_of(sib * voc, 128), voc)
    mine_pas = pl.ds(pl.multiple_of(c * 128, 128), 128)
    local = [pltpu.make_async_copy(bias, bias_v, loc_sems.at[0]),
             pltpu.make_async_copy(tokens, tokens_v, loc_sems.at[1]),
             pltpu.make_async_copy(selected, sel_v.at[c], loc_sems.at[2]),
             pltpu.make_async_copy(hidden, gath.at[y], loc_sems.at[3]),
             pltpu.make_async_copy(weight, w_v.at[:, mine], loc_sems.at[4])]
    for j in range(ny):
        local.append(pltpu.make_async_copy(
            passages.at[:, pl.ds(j * wide, wide)], pas.at[j, mine_pas], loc_sems.at[5 + j]))
    local.append(pltpu.make_async_copy(positive_h, positive, loc_sems.at[5 + ny]))
    for copy in local:
        copy.start()

    barrier = pltpu.get_barrier_semaphore()
    passed_on = nz == 16
    z_near = (2, -2, 1, -1) if passed_on else z_far
    peers = ([z_dev(d) for d in z_near] + [pass_dev(d, 0) for d in y_far] + [x_dev(*d) for d in x_peers])
    for device in peers:
        pl.semaphore_signal(barrier, inc=1, device_id=device, device_id_type=MESH)
    pl.semaphore_wait(barrier, len(peers))

    hr = own_rows // 2
    top, bottom = pl.ds(0, hr), pl.ds(hr, hr)
    if ny == 4:
        pieces = [(pl.ds(i, 16), pl.ds(hr + i, 16)) for i in range(0, hr, 16)]
        first = []
        for a, b in pieces:
            first.append((remote(hidden.at[a], gath.at[y, a], pass_dev(1, 0)),
                          remote(hidden.at[b], gath.at[y, b], pass_dev(-1, 0))))
        then_up = remote(hidden.at[bottom], gath.at[y, bottom], pass_dev(1, 0))
        then_down = remote(hidden.at[top], gath.at[y, top], pass_dev(-1, 0))
    else:
        direct = [remote(hidden, gath.at[y], pass_dev(d, 0)) for d in y_far]
    if passed_on:
        pl.semaphore_signal(entry.at[0], inc=1, device_id=z_dev(2), device_id_type=MESH)
        pl.semaphore_signal(entry.at[1], inc=1, device_id=z_dev(-2), device_id_type=MESH)
    to_w = remote(weight, w_v.at[:, mine], sibling)
    for copy in local[:3]:
        copy.wait()
    bias_b[c] = jnp.broadcast_to(bias_v[...].reshape(1, voc), (8, voc))
    to_small = [remote(selected, sel_v.at[c], sibling), remote(bias_b.at[c], bias_b.at[c], sibling)]
    to_pas = remotes([(passages.at[:, pl.ds(j * wide, wide)], pas.at[j, mine_pas], sibling) for j in range(ny)],
                     pas.at[pl.ds(0, ny // 2)])

    if ny == 4:
        up, down, far = around(y, -1, ny), around(y, 1, ny), around(y, 2, ny)
        i = take()
        for (a, b), (to_up, to_down) in zip(pieces, first):
            to_up.wait_recv()
            remote(gath.at[up, a], gath.at[up, a], pass_dev(1, 0), i)
            to_down.wait_recv()
            remote(gath.at[down, b], gath.at[down, b], pass_dev(-1, 0), i)
        relayed = together(i, gath.at[far])
    if passed_on:
        pl.semaphore_wait(entry.at[0], 1)
        pl.semaphore_wait(entry.at[1], 1)
        pl.semaphore_signal(entry.at[2], inc=1, device_id=z_dev(4), device_id_type=MESH)
        pl.semaphore_signal(entry.at[3], inc=1, device_id=z_dev(-4), device_id_type=MESH)
    for ref in (maxl, sell, maxa, sela, selp, lenp, zf):
        ref[...] = jnp.zeros_like(ref)

    lengths = jnp.sum((tokens_v[...] != 1).astype(f32), axis=1, keepdims=True).astype(jnp.int32)
    lengths = jnp.broadcast_to(lengths, (n_queries, wide))
    for copy in to_small:
        copy.wait_recv()
    picks = jnp.concatenate([sel_v[0], sel_v[1]], axis=1)
    for j in range(ny):
        a = 2 * j * per_block
        b = a + per_block
        selp[j, 0:per_block, :] = jnp.where(c == 0, picks[a:b], picks[b:b + per_block])
        lenp[j, 0:per_block, :] = jnp.where(c == 0, lengths[a:b], lengths[b:b + per_block])

    def block(yy):
        logits = dot(gath[yy], w_v[...]).reshape(per_block, qlen, wide)
        at = iota((per_block, qlen, wide), 1)
        valid = at < lenp[yy][0:per_block].reshape(per_block, 1, wide)
        chosen = at == selp[yy][0:per_block].reshape(per_block, 1, wide)
        maxl[yy, 0:per_block, :] = jnp.max(jnp.where(valid, logits, -jnp.inf), axis=1)
        sell[yy, 0:per_block, :] = jnp.sum(jnp.where(chosen, logits, 0.0), axis=1)

    local[3].wait()
    local[4].wait()
    if ny == 4:
        to_w.wait_recv()
        block(y)
        then_up.wait_recv()
        block(up)
        then_down.wait_recv()
        block(down)
    else:
        to_w.wait_recv()
        block(y)
    if ny == 4:
        relayed.wait_recv()
        block(far)
    else:
        for d, copy in zip(y_far, direct):
            copy.wait_recv()
            block(around(y, -d, ny))

    wide_bias = jnp.concatenate([bias_b[0], bias_b[1]], axis=1)[0:1]
    for j in range(ny):
        maxa[j * SLOT:(j + 1) * SLOT, :] = maxl[j, 0:SLOT, :]
    pool[y] = jnp.log1p(jax.nn.softplus(maxa[...] + wide_bias)).astype(bf16)
    to_pool = {d: remote(pool.at[y], pool.at[y], pass_dev(d, 0)) for d in y_far}
    for copy in local[5:]:
        copy.wait()
    to_pas.wait_recv()
    for j in range(ny):
        pas_t[j] = pas[j].T
    row, lane = iota((ROWS, 256), 0), iota((ROWS, 256), 1)
    place = lax.bitwise_and(row, SLOT - 1)
    query = (lax.shift_right_logical(row, 2) * NC + c) * per_block + place
    query = jnp.where((place < per_block) & (row < ny * SLOT), query, -1)
    pos_col = jnp.zeros((ROWS, 256), jnp.int32)
    for q in range(n_queries):
        pos_col = jnp.where(query == q, positive[q], pos_col)
    is_pos = (lane + y * 256) == pos_col
    onehot = is_pos.astype(f32).astype(bf16)

    score = dot(pool[y], pas_t[y])
    for d in reversed(y_far):
        to_pool[d].wait_recv()
        there = around(y, -d, ny)
        score = score + dot(pool[there], pas_t[there])

    for j in range(NX):
        a, b = (j // 2) * tile, (j % 2) * 128
        sc_s[j] = score[a:a + tile, b:b + 128]
    to_x = remotes([(sc_s.at[around(x, d, NX)], sc_x.at[d], x_dev(d)) for d in x_far], sc_x.at[pl.ds(1, NX - 1)])
    for j in range(ny):
        pos_s[j] = dot(onehot, pas[j]).astype(bf16)
    to_pos = remotes([(pos_s.at[around(y, d, ny)], pos_r.at[d], pass_dev(d, 0)) for d in y_far],
                     pos_r.at[pl.ds(1, ny - 1)])
    to_wr = {}
    for d in y_far:
        rows = pl.ds(pl.multiple_of(around(y, d, ny) * chip_cols, chip_cols), chip_cols)
        to_wr[d] = remote(w_v.at[rows, mine], wr.at[y, :, mine], pass_dev(d, 0))
    for j in range(ny):
        sel_r[y, j * SLOT:(j + 1) * SLOT, :] = selp[j, 0:SLOT, :]
    to_sel = remotes([(sel_r.at[y], sel_r.at[y], pass_dev(d, 0)) for d in y_far], sel_r.at[pl.ds(0, ny - 1)])
    to_other = remote(gath, gath_o, sibling)
    total = sc_s[x]
    to_x.wait_recv()
    for d in range(1, NX):
        total = total + sc_x[d]
    zs[...] = total
    if passed_on:
        pl.semaphore_wait(entry.at[2], 1)
        pl.semaphore_wait(entry.at[3], 1)
    to_z = remotes([(zs, zr.at[d], z_dev(d)) for d in z_far], zr.at[pl.ds(1, nz - 1)])
    wr_t[y] = w_v[pl.ds(pl.multiple_of(y * chip_cols, chip_cols), chip_cols), :].T
    prow = iota((tok, 128), 0)
    chunk = jnp.floor((prow.astype(f32) + 0.5) * (1.0 / ro)).astype(jnp.int32)
    zl = lax.bitwise_and(chunk, per_core - 1)
    xx = lax.shift_right_logical(chunk, per_core.bit_length() - 1)
    natural = prow + ro * (zl * NX + xx - chunk)
    plane = iota((tok, 128), 1)
    for j in range(tok // 128):
        perm[:, j * 128:(j + 1) * 128] = (natural == plane + j * 128).astype(f32).astype(bf16)
    for j in range(ny):
        sela[j * SLOT:(j + 1) * SLOT, :] = sell[j, 0:SLOT, :]
    at_sel = sela[...] + wide_bias
    slope[...] = jax.nn.sigmoid(at_sel) / (1.0 + jax.nn.softplus(at_sel))
    gath_t[0] = gath[...].reshape(tok, d_model).T
    to_z.wait_recv()
    for d in range(1, nz):
        total = total + zr[d]
    fin[x] = total
    to_fin = remotes([(fin.at[x], fin.at[x], x_dev(d)) for d in x_far], fin.at[pl.ds(0, NX - 1)])
    i = take()
    for d in reversed(y_far):
        to_wr[d].wait_recv()
        there = around(y, -d, ny)
        remote(wr.at[there, :, mine], wr.at[there, :, mine], sibling, i)
    to_wr_sib = together(i, wr.at[pl.ds(0, ny - 1), :, mine])
    to_pos.wait_recv()
    pos_entries = pos_s[y].astype(f32)
    for d in range(1, ny):
        pos_entries = pos_entries + pos_r[d].astype(f32)
    to_fin.wait_recv()

    score = jnp.concatenate([jnp.concatenate([fin[j], fin[j + 1]], axis=1) for j in range(0, NX, 2)], axis=0)
    peak = jnp.max(score, axis=1, keepdims=True)
    terms = jnp.exp(score - peak)
    other = jnp.where(is_pos, 0.0, terms)
    stats = [peak, jnp.sum(other, axis=1, keepdims=True),
             jnp.sum(jnp.where(is_pos, terms, 0.0), axis=1, keepdims=True),
             jnp.sum(jnp.where(is_pos, score, 0.0), axis=1, keepdims=True)]
    eye = iota((ROWS, 128), 0) == iota((ROWS, 128), 1)
    turned = [jnp.sum(jnp.where(eye, s, 0.0), axis=0, keepdims=True) for s in stats]
    st_s[...] = jnp.concatenate(turned + [jnp.zeros((8 - len(turned), 128), f32)], axis=0)
    other = other.astype(bf16)
    to_u = {}
    for d in y_far:
        there = around(y, d, ny)
        u_s[there] = dot(other, pas[there]).astype(bf16)
        to_u[d] = remote(u_s.at[there], u_r.at[d], pass_dev(d, 0))
    to_st = remotes([(st_s, st.at[d], pass_dev(d, 0)) for d in y_far], st.at[pl.ds(1, ny - 1)])
    st[0] = st_s[...]
    mine_u = dot(other, pas[y])
    to_wr_sib.wait_recv()
    for d in y_far:
        there = around(y, -d, ny)
        wr_t[there] = wr[there].T
    to_st.wait_recv()
    peaks = [st[i][0:1] for i in range(ny)]
    highest = functools.reduce(jnp.maximum, peaks)
    scale = [jnp.exp(k - highest) for k in peaks]
    rest = sum(scale[i] * st[i][1:2] for i in range(ny))
    denom = rest + sum(scale[i] * st[i][2:3] for i in range(ny))
    pos_score = sum(st[i][3:4] for i in range(ny))
    log_total = highest + jnp.log(denom)
    lane1 = iota((1, 128), 1)
    counted = (lax.bitwise_and(lane1, SLOT - 1) < per_block) & (lane1 < ny * SLOT)
    loss = jnp.sum(jnp.where(counted, log_total - pos_score, 0.0), axis=1, keepdims=True)
    factor = (loss_scale / n_queries) / denom

    def column(line):
        return jnp.sum(jnp.where(eye, line, 0.0), axis=1, keepdims=True)

    term = column(scale[0] * factor) * mine_u - column(rest * factor) * pos_entries
    for d in reversed(y_far):
        to_u[d].wait_recv()
        term = term + column(scale[d] * factor) * u_r[d].astype(f32)

    grad = term * slope[...]
    g_r[y] = grad.astype(bf16)
    to_g = {d: remote(g_r.at[y], g_r.at[y], pass_dev(d, 0)) for d in y_far}
    at = iota((per_block, qlen, wide), 1)

    def spread(yy, out):
        taken, picks = g_r[yy].astype(f32), sel_r[yy]
        for j in range(ny):
            some = taken[j * SLOT:j * SLOT + per_block].reshape(per_block, 1, wide)
            chosen = at == picks[j * SLOT:j * SLOT + per_block].reshape(per_block, 1, wide)
            out[j * own_rows:(j + 1) * own_rows, :] = jnp.where(chosen, some, 0.0).reshape(own_rows, wide).astype(bf16)

    spread(y, lh)
    to_lh = remote(lh.at[:, theirs], lh_o, sibling)

    out = dot(lh[...], wr_t[y])
    to_sel.wait_recv()
    for d in reversed(y_far):
        to_g[d].wait_recv()
        there = around(y, -d, ny)
        spread(there, lh_y)
        out = out + dot(lh_y[...], wr_t[there])
    out = dot(perm[...], out.astype(bf16)).astype(bf16)
    for k in range(NC):
        for j in range(NX):
            s1[k, j] = out[j * part:(j + 1) * part, k * 128:(k + 1) * 128]
    to_s1 = remotes([(s1.at[around(c, dc, NC), around(x, dx, NX)], s1_r.at[dx * NC + dc], x_dev(dx, dc))
                     for dx, dc in x_peers], s1_r.at[pl.ds(1, NX * NC - 1)])

    at_row = iota((ROWS, wide), 0)
    real = (lax.bitwise_and(at_row, SLOT - 1) < per_block) & (at_row < ny * SLOT)
    summed = jnp.sum(jnp.where(real, grad, 0.0), axis=0, keepdims=True)
    first = iota((8, voc), 0) == 0
    for j in range(NC):
        gs[j] = jnp.where(first, summed[:, j * voc:(j + 1) * voc], loss)
    to_gs = remote(gs.at[sib], gs_r, sibling)
    to_other.wait_recv()
    gath_t[1] = gath_o[...].reshape(tok, d_model).T
    gw_v[...] = dot(gath_t[0], lh[:, mine])

    to_s1.wait_recv()
    same, cross = s1[c, x].astype(f32), s1_r[1].astype(f32)
    for d in range(1, NX):
        same = same + s1_r[d * NC].astype(f32)
        cross = cross + s1_r[d * NC + 1].astype(f32)
    high[c] = same
    high[sib] = cross
    for core in range(NC):
        for k in range(per_core):
            to_row = (NC * (k // z_block) + core) * z_block + k % z_block
            zf[to_row, 0:ro, :] = high[core, k * ro:(k + 1) * ro]
    z2[...] = zf[...].astype(bf16)
    to_z2 = remotes([(z2.at[around(z, d, nz)], z2_r.at[d], z_dev(d)) for d in z_far], z2_r.at[pl.ds(1, nz - 1)])
    for copy in started[:-1]:
        copy.wait_send()
    to_lh.wait_recv()
    gw_v[...] += dot(gath_t[1], lh_o[...])
    gw_out = pltpu.make_async_copy(gw_v, gw_o, loc_sems.at[0])
    gw_out.start()
    to_gs.wait_recv()
    gb_o[...] = (gs[c][0:1] + gs_r[0:1]).reshape(voc)
    loss_o[...] = (gs[c][1:2, 0:1] + gs_r[1:2, 0:1]) * (1.0 / n_queries)
    total = zf[z]
    to_z2.wait_recv()
    for d in range(1, nz):
        total = total + z2_r[d].astype(f32)
    gh_o[...] = total[0:ro].astype(bf16)

    to_z2.wait_send()
    gw_out.wait()


def hand_out(*refs):
    sems = refs[8]
    pairs = [(refs[i], refs[4 + i]) for i in (0, 1, 3)]
    rows = refs[2].shape[0] // 4
    pairs += [(refs[2].at[pl.ds(i * rows, rows)], refs[6].at[pl.ds(i * rows, rows)]) for i in range(4)]
    copies = [pltpu.make_async_copy(a, b, sems.at[i]) for i, (a, b) in enumerate(pairs)]
    for copy in reversed(copies):
        copy.start()
    for copy in copies:
        copy.wait()


def local(nz, ny, hidden, weight, bias, token_ids, passages, positive, selected):
    n_queries, qlen = token_ids.shape
    own_rows, d = hidden.shape
    voc = weight.shape[1]
    wide = NC * voc
    tok = ny * own_rows
    ro = (NC * tok) // (nz * NX)
    rp = -(-ro // 16) * 16
    part = (nz // 2) * ro
    tile = ROWS * 2 // NX
    i32 = jnp.int32
    vmem = pl.BlockSpec(memory_space=pltpu.VMEM)
    anywhere = pl.BlockSpec(memory_space=pl.ANY)
    hbm = pl.BlockSpec(memory_space=pltpu.HBM)
    scratch = [
        ((ny, own_rows, d), bf16), ((ny, own_rows, d), bf16), ((NC, d, tok), bf16),
        ((d, wide), bf16), ((ny, NC * 128, wide), bf16), ((ny, wide, NC * 128), bf16),
        ((ny, NC * 128, wide), bf16), ((ny, wide, NC * 128), bf16), ((tok, tok), bf16),
        ((voc,), f32), ((NC, 8, voc), f32), None, ((n_queries, qlen), i32), ((NC, n_queries, voc), i32),
        ((ny, 8, wide), i32), ((ny, 8, wide), i32),
        ((ny, 8, wide), f32), ((ny, 8, wide), f32), ((ROWS, wide), f32), ((ROWS, wide), f32),
        ((ny, ROWS, wide), bf16), ((ny, ROWS, wide), bf16), ((ny, ROWS, wide), bf16),
        ((NX, tile, 128), f32), ((NX, tile, 128), f32), ((tile, 128), f32), ((nz, tile, 128), f32),
        ((NX, tile, 128), f32), ((8, 128), f32), ((ny, 8, 128), f32),
        ((ny, ROWS, wide), bf16), ((ny, ROWS, wide), bf16), ((ROWS, wide), f32),
        ((ny, ROWS, wide), i32), ((ny, ROWS, wide), bf16),
        ((tok, wide), bf16), ((tok, wide), bf16), ((tok, voc), bf16),
        ((NC, 8, voc), f32), ((8, voc), f32),
        ((NC, NX, part, 128), bf16), ((NX * NC, part, 128), bf16), ((NC, part, 128), f32),
        ((nz, rp, 128), f32), ((nz, rp, 128), bf16), ((nz, rp, 128), bf16), ((d, voc), f32),
    ]
    results = pl.pallas_call(
        functools.partial(kernel, nz, ny, n_queries),
        out_shape=(
            jax.ShapeDtypeStruct((1, 1), f32),
            jax.ShapeDtypeStruct((ro, 128), bf16),
            jax.ShapeDtypeStruct((d, voc), f32),
            jax.ShapeDtypeStruct((voc,), f32),
        ),
        in_specs=[hbm] * 7,
        out_specs=(vmem, vmem, anywhere, vmem),
        scratch_shapes=[pltpu.VMEM(*k) if k else pltpu.SMEM((n_queries,), i32) for k in scratch] + [
            pltpu.SemaphoreType.DMA((MAX_SEMS,)),
            pltpu.SemaphoreType.DMA((MAX_SEMS,)),
            pltpu.SemaphoreType.DMA((6 + ny,)),
            pltpu.SemaphoreType.REGULAR((4,)),
        ],
        compiler_params=pltpu.CompilerParams(
            collective_id=0, has_side_effects=True, vmem_limit_bytes=48 * 1024 * 1024
        ),
    )(*(pltpu.with_memory_space_constraint(a, pltpu.HBM)
        for a in (hidden, weight, bias, token_ids, passages, positive, selected)))
    loss, grad_hidden, grad_weight, grad_bias = pl.pallas_call(
        hand_out,
        out_shape=tuple(jax.ShapeDtypeStruct(r.shape, r.dtype) for r in results),
        in_specs=[anywhere] * 4,
        out_specs=(hbm,) * 4,
        scratch_shapes=[pltpu.SemaphoreType.DMA((7,))],
        compiler_params=pltpu.CompilerParams(vmem_limit_bytes=1024 * 1024),
    )(*results)
    return loss.reshape(()), grad_hidden, grad_weight, grad_bias


def solution(mesh):
    in_specs = (
        P("pass", None),
        P(None, ("vocab", "pass")),
        P(("vocab", "pass")),
        P(),
        P("pass", "vocab"),
        P(),
        P(None, ("vocab", "pass")),
    )
    out_specs = (P(), P("vocab", "pass"), P(None, ("vocab", "pass")), P(("vocab", "pass")))
    body = functools.partial(local, mesh.shape["vocab"] // NX, mesh.shape["pass"] // NC)
    return jax.shard_map(body, mesh=mesh, in_specs=in_specs, out_specs=out_specs, check_vma=False)
```
